512 devices in a mesh: depth: 32 (over y, z_lo), height: 16 (over z_hi, x, core).
Axes of the slice: x: 4, y: 8, z: 8 (z_hi: 2, z_lo: 4; z = z_hi * 4 + z_lo), core: 2. Of those that a mesh axis runs over, the one named last changes fastest.
Arguments:
- volume: float32 [32, 256, 2048], P('height', 'depth'), may hold values from -6 to 6
- measured: float32 [16, 32, 2048], P(None, 'height', 'depth'), may hold values from -12 to 12
- taps: float32 [4, 16, 256], P(None, None, 'depth'), may hold values from 0.01 to 0.1
- band_offset: int32 [16, 32], replicated, may hold values from -64 to 64
- angle_index: int32 [16], replicated, may hold values from 0 to 719
Outputs:
- denoised: float32 [32, 256, 2048], P('height', 'depth')
The draws below stay inside these ranges and needn't reach their ends.
Inputs may be any that keep to these rules, and one draw needn't show every extreme that they name: `band_offset`: band offsets of every angle and brick lie within plus or minus 64.
All inputs are finite; a program needn't handle non-finite values.
Results may differ from the reference program's by a relative error of at most 0.0003.
Values sent between devices are 32-bit elements; how exact they have to be, the bound alone decides.
A program may use at most 64 MiB of HBM per device.

```python
import math
import jax
import jax.numpy as jnp
from jax import lax

NX = 2048
CD = 8
ANGLES = 16
TAPS = 4
OFFMAX = 64
N_VIEWS = 720
SWEEPS = 2
ND = 256
NH = 32
BRICKS = 32
N_DEPTH = 32


def touch_ends(result, stream_key, least, largest):
    index_at = [jax.random.randint(jax.random.fold_in(stream_key, axis), (), 0, length) for axis, length in enumerate(result.shape)]
    widest = result.shape.index(max(result.shape))
    beside = index_at[:widest] + [(index_at[widest] + 1) % result.shape[widest]] + index_at[widest + 1:]
    return result.at[tuple(index_at)].set(least).at[tuple(beside)].set(largest)


def levels(stream_key, shape, shards, smallest, top_value):
    def one(axis_at, shards_of):
        heights = jax.random.uniform(jax.random.fold_in(jax.random.fold_in(stream_key, 6), axis_at), (shards_of,), jnp.float32, smallest / len(shards), top_value / len(shards))
        return jnp.repeat(jnp.exp(heights), shape[axis_at] // shards_of).reshape((-1,) + (1,) * (len(shape) - axis_at - 1))

    gain = one(*shards[0])
    for cut in shards[1:]:
        gain = gain * one(*cut)
    return gain


def noise(stream_key, shape, scale, most, pieces=(), kind=jnp.bfloat16):
    drawn = scale * jax.random.normal(stream_key, shape, jnp.float32)
    if pieces:
        drawn = drawn * levels(stream_key, shape, pieces, -0.22, 0.18)
    return jnp.clip(drawn, -most, most).astype(kind)


def setup_inputs(seed: int = 0) -> dict:
    arg_keys = jax.random.split(jax.random.key(seed), 6)
    return {
        "volume": noise(arg_keys[0], (NH, ND, NX), 1.0, 6.0, ((0, 16), (1, 32)), jnp.float32),
        "measured": noise(arg_keys[1], (ANGLES, NH, NX), 2.0, 12.0, ((1, 16), (2, 32)), jnp.float32),
        "taps": jnp.clip(jnp.exp(math.log(0.1) - 2.3025851 * jax.random.uniform(arg_keys[2], (TAPS, ANGLES, ND), jnp.float32) ** levels(arg_keys[2], (TAPS, ANGLES, ND), ((2, 32),), -0.2, 0.2)), 0.01, 0.1),
        "band_offset": touch_ends(jax.random.randint(arg_keys[3], (ANGLES, BRICKS), -OFFMAX, OFFMAX + 1), jax.random.fold_in(arg_keys[3], 1), -OFFMAX, OFFMAX).astype(jnp.int32),
        "angle_index": touch_ends(jax.random.randint(arg_keys[4], (ANGLES,), 0, N_VIEWS), jax.random.fold_in(arg_keys[4], 1), 0, N_VIEWS - 1).astype(jnp.int32),
    }


relax_step = 0.5
tv_step = 0.08
tv_eps = 0.1

def cone_weights(taps, angle_index, first_slice, total_slices):
    slices = taps.shape[2]
    angle_value = 2.0 * math.pi / N_VIEWS * angle_index.astype(jnp.float32)
    depth_place = (first_slice + jnp.arange(slices, dtype=jnp.int32)).astype(jnp.float32) + 0.5
    rise = 0.5 + 0.45 * jnp.sin(angle_value)[:, None] * jnp.cos(math.pi / total_slices * depth_place)[None, :]
    return jnp.stack([taps * (1.0 - rise)[None], taps * rise[None]], axis=2)

def binary_shift(values, amount, toward):
    length = values.shape[-1]
    for bit_number in range((2 * OFFMAX).bit_length()):
        stride = 1 << bit_number
        zero_block = jnp.zeros(values.shape[:-1] + (stride,), values.dtype)
        if toward > 0:
            shifted = jnp.concatenate([zero_block, values[..., :length - stride]], axis=-1)
        else:
            shifted = jnp.concatenate([values[..., stride:], zero_block], axis=-1)
        chosen = amount // stride % 2 == 1
        values = jnp.where(chosen, shifted, values)
    return values

def project(block, factor, offsets):
    columns = block.shape[2]
    reach = 2 * OFFMAX
    term = jnp.einsum('kasy,hyx->kashx', factor, block, precision=lax.Precision.HIGHEST)
    padded = jnp.pad(term, ((0, 0), (0, 0), (0, 0), (0, 0), (OFFMAX + TAPS, OFFMAX)))
    window = columns + reach
    summed = padded[0, ..., TAPS:TAPS + window]
    for tap_number in range(1, TAPS):
        summed = summed + padded[tap_number, ..., TAPS - tap_number:TAPS - tap_number + window]
    amount = (offsets + OFFMAX).astype(jnp.int32)[:, None, None, None]
    shifted = binary_shift(summed, amount, 1)[..., reach:reach + columns]
    lower = jnp.pad(shifted[:, 0], ((0, 0), (0, 1), (0, 0)))
    upper = jnp.pad(shifted[:, 1], ((0, 0), (1, 0), (0, 0)))
    return lower + upper

def backproject(extended, factor, offsets):
    columns = extended.shape[2]
    layers = extended.shape[1] - 1
    padded = jnp.pad(extended, ((0, 0), (0, 0), (OFFMAX, OFFMAX + TAPS)))
    amount = (offsets + OFFMAX).astype(jnp.int32)[:, None, None]
    shifted = binary_shift(padded, amount, -1)
    moved = jnp.stack([shifted[..., tap_number:tap_number + columns] for tap_number in range(TAPS)], axis=0)
    stacked = jnp.stack([moved[:, :, :layers], moved[:, :, 1:]], axis=2)
    return jnp.einsum('kasy,kashx->hyx', factor, stacked, precision=lax.Precision.HIGHEST)

def forward(values, dimension, allowed):
    length = values.shape[dimension]
    following = jnp.concatenate([lax.slice_in_dim(values, 1, length, axis=dimension), lax.slice_in_dim(values, length - 1, length, axis=dimension)], axis=dimension)
    return jnp.where(allowed, following - values, 0.0)

def backward(normal, dimension):
    length = normal.shape[dimension]
    before = jnp.concatenate([jnp.zeros_like(lax.slice_in_dim(normal, 0, 1, axis=dimension)), lax.slice_in_dim(normal, 0, length - 1, axis=dimension)], axis=dimension)
    return normal - before

def allowed_mask(positions, total):
    return (positions >= 0) & (positions + 1 < total)

def tv_sweep(values, height_place, depth_place, width_place, height_total, depth_total, width_total):
    along_h = forward(values, 0, allowed_mask(height_place, height_total)[:, None, None])
    along_d = forward(values, 1, allowed_mask(depth_place, depth_total)[None, :, None])
    along_w = forward(values, 2, allowed_mask(width_place, width_total)[None, None, :])
    inverse = 1.0 / jnp.sqrt(tv_eps * tv_eps + along_h * along_h + along_d * along_d + along_w * along_w)
    diverge = backward(along_h * inverse, 0) + backward(along_d * inverse, 1) + backward(along_w * inverse, 2)
    return values + tv_step * diverge

def reference(volume, measured, taps, band_offset, angle_index):
    factor = cone_weights(taps, angle_index, 0, ND)
    bricks = jnp.arange(N_DEPTH, dtype=jnp.int32)

    def brick_image(image, brick):
        start = (brick * CD).astype(jnp.int32)
        block = lax.dynamic_slice_in_dim(volume, start, CD, 1)
        weights_part = lax.dynamic_slice_in_dim(factor, start, CD, 3)
        offsets = lax.dynamic_slice_in_dim(band_offset, brick, 1, 1)[:, 0]
        return (image + project(block, weights_part, offsets), None)
    image, _ = lax.scan(brick_image, jnp.zeros((ANGLES, NH + 1, NX), jnp.float32), bricks)
    residual = measured - image[:, :NH]
    extended = jnp.concatenate([residual, jnp.zeros((ANGLES, 1, NX), jnp.float32)], axis=1)

    def brick_update(carry, brick):
        start = (brick * CD).astype(jnp.int32)
        weights_part = lax.dynamic_slice_in_dim(factor, start, CD, 3)
        offsets = lax.dynamic_slice_in_dim(band_offset, brick, 1, 1)[:, 0]
        return (carry, backproject(extended, weights_part, offsets))
    _, blocks = lax.scan(brick_update, jnp.zeros((), jnp.float32), bricks)
    update = jnp.transpose(blocks, (1, 0, 2, 3)).reshape(NH, ND, NX)
    values = volume + relax_step * update
    height_place = jnp.arange(NH, dtype=jnp.int32)
    depth_place = jnp.arange(ND, dtype=jnp.int32)
    width_place = jnp.arange(NX, dtype=jnp.int32)
    for sweep_index in range(SWEEPS):
        values = tv_sweep(values, height_place, depth_place, width_place, NH, ND, NX)
    return values
```

```python
import functools
import math

import jax
import jax.numpy as jnp
from jax import lax
from jax.experimental import pallas as pl
from jax.experimental.pallas import tpu as pltpu
from jax.sharding import PartitionSpec as P

TAPS = 4
OFFMAX = 64
N_VIEWS = 720
LANES = 128

relax_step = 0.5
tv_step = 0.08
tv_eps = 0.1

MESH = pl.DeviceIdType.MESH


def split_bf16(value):
    high = value.astype(jnp.bfloat16)
    low = (value - high.astype(jnp.float32)).astype(jnp.bfloat16)
    return high, low


def roll_left(value, amount):
    return pltpu.roll(value, value.shape[1] - amount, 1)


def shift_rows(value, amount):
    move = amount + OFFMAX
    top = move // OFFMAX
    moved_left = roll_left(value, OFFMAX)
    moved_right = pltpu.roll(value, OFFMAX, 1)
    value = jnp.where(top == 0, moved_right, jnp.where(top == 1, value, moved_left))
    for bit in range(6):
        stride = 1 << bit
        value = jnp.where((move // stride) % 2 == 1, roll_left(value, stride), value)
    return value


def total_variation(fields, after, before, height_of, depth_of, heights, depths):
    slices, columns = fields[0].shape
    row = lax.broadcasted_iota(jnp.int32, (slices, columns), 0)
    lane = lax.broadcasted_iota(jnp.int32, (slices, columns), 1)
    inner = lane < columns - 1
    last_layer = height_of == heights - 1
    open_row = (row < slices - 1) | (depth_of < depths - 1)
    along_h, along_d, along_w = [], [], []
    for i in range(3):
        here = fields[i]
        up = fields[i + 1] - here
        if i == 2:
            up = jnp.where(last_layer, 0.0, up)
        deep = jnp.where(row == slices - 1, after[i], pltpu.roll(here, slices - 1, 0)) - here
        deep = jnp.where(open_row, deep, 0.0)
        wide = jnp.where(inner, roll_left(here, 1) - here, 0.0)
        scale = lax.rsqrt(tv_eps * tv_eps + up * up + deep * deep + wide * wide)
        if i == 0:
            scale = jnp.where(height_of > 0, scale, 0.0)
        along_h.append(up * scale)
        along_d.append(deep * scale)
        along_w.append(wide * scale)
    here = jnp.where(row == 0, before[0], before[1])
    above = jnp.where(row == 0, before[1], before[2])
    ahead = jnp.where(row == 0, fields[1][0:1], fields[2][0:1])
    up = above - here
    up = jnp.where(last_layer & (row == 1), 0.0, up)
    deep = ahead - here
    wide = jnp.where(inner, roll_left(here, 1) - here, 0.0)
    scale = lax.rsqrt(tv_eps * tv_eps + up * up + deep * deep + wide * wide)
    deep_before = jnp.where(depth_of > 0, deep * scale, 0.0)
    results = []
    for i in (1, 2):
        d_before = jnp.where(row == 0, deep_before[i - 1 : i], pltpu.roll(along_d[i], 1, 0))
        w_before = pltpu.roll(along_w[i], 1, 1)
        diverge = (
            (along_h[i] - along_h[i - 1]) + (along_d[i] - d_before) + (along_w[i] - w_before)
        )
        results.append(fields[i] + tv_step * diverge)
    return results


def kernel(
    heights, depths,
    vol_ref, f1_ref, f2_ref, band_ref, off_ref,
    out_ref,
    halo_ref, part_ref, recv_ref, res_ref,
    main_ref, main_low, main_high,
    lo_ref, hi_ref, got_m, got_pm, got_p, got_mp, got_pp,
    main2_ref, main2_low, main2_high,
    lo2_ref, hi2_ref, got2_m, got2_pm, got2_p, got2_mp,
    halo_sem, scatter_sem, gather_sem, edge_sem, edge2_sem,
):
    height_of = lax.axis_index("height")
    depth_of = lax.axis_index("depth")
    above = lax.rem(height_of + 1, heights)
    below = lax.rem(height_of + heights - 1, heights)
    ahead = lax.rem(depth_of + 1, depths)
    behind = lax.rem(depth_of + depths - 1, depths)
    _, slices, columns = vol_ref.shape
    tiles = columns // LANES
    angles = off_ref.shape[0] // 2

    barrier = pltpu.get_barrier_semaphore()

    def greet(step, carry):
        pl.semaphore_signal(
            barrier, inc=1,
            device_id=(lax.rem(depth_of + step, depths), height_of), device_id_type=MESH,
        )
        return carry

    around = (
        (depth_of, above), (depth_of, below),
        (ahead, above), (ahead, below), (behind, above), (behind, below),
    )
    for target in around:
        pl.semaphore_signal(barrier, inc=1, device_id=target, device_id_type=MESH)
    lax.fori_loop(1, depths, greet, 0)
    pl.semaphore_wait(barrier, depths - 1 + len(around))

    halo_copy = pltpu.make_async_remote_copy(
        src_ref=vol_ref.at[1], dst_ref=halo_ref,
        send_sem=halo_sem.at[0], recv_sem=halo_sem.at[1],
        device_id=(depth_of, above), device_id_type=MESH,
    )
    halo_copy.start()

    zeros = jnp.zeros((slices, LANES), jnp.float32)

    def spread(layers):
        wide = [jnp.concatenate([layer, zeros], axis=1) for layer in layers]
        rows = []
        for layer in wide:
            for tap in range(TAPS):
                rows.append(layer if tap == 0 else pltpu.roll(layer, tap, 1))
        high, low = split_bf16(jnp.concatenate(rows, axis=0))
        return jnp.concatenate([high, low], axis=0)

    own = 2 * TAPS * slices
    first = TAPS * slices
    count = 2 * angles
    image = jnp.dot(
        f1_ref[:, 2 * first :], spread([vol_ref[0], vol_ref[1]]),
        preferred_element_type=jnp.float32,
    )
    halo_copy.wait()
    halo = jnp.where(height_of > 0, halo_ref[...], 0.0)
    image = image + jnp.dot(
        f1_ref[:, : 2 * first], spread([halo]), preferred_element_type=jnp.float32
    )
    image = image[:count] + image[count:]
    image = shift_rows(image, -off_ref[...])
    for r in range(2):
        for tile in range(tiles):
            part_ref[r * tiles + tile] = -image[
                r * angles : (r + 1) * angles, tile * LANES : (tile + 1) * LANES
            ]
    for r in range(2):
        place = r * tiles + depth_of // 2
        part_ref[place] = part_ref[place] + band_ref[r]

    def scatter(step, carry):
        peer = lax.rem(depth_of + step, depths)
        pltpu.make_async_remote_copy(
            src_ref=part_ref.at[peer], dst_ref=recv_ref.at[depth_of],
            send_sem=scatter_sem.at[0], recv_sem=scatter_sem.at[1],
            device_id=(peer, height_of), device_id_type=MESH,
        ).start()
        return carry

    lax.fori_loop(1, depths, scatter, 0)
    recv_ref[depth_of] = part_ref[depth_of]

    def all_of(ref, sem):
        some = ref.at[pl.ds(0, depths - 1)]
        pltpu.make_async_copy(some, some, sem).wait()

    all_of(recv_ref, scatter_sem.at[1])
    sums = [recv_ref[i] for i in range(depths)]
    while len(sums) > 1:
        sums = [sums[i] + sums[i + 1] for i in range(0, len(sums), 2)]
    res_ref[depth_of] = sums[0]

    def gather(step, carry):
        peer = lax.rem(depth_of + step, depths)
        pltpu.make_async_remote_copy(
            src_ref=res_ref.at[depth_of], dst_ref=res_ref.at[depth_of],
            send_sem=gather_sem.at[0], recv_sem=gather_sem.at[1],
            device_id=(peer, height_of), device_id_type=MESH,
        ).start()
        return carry

    lax.fori_loop(1, depths, gather, 0)
    all_of(res_ref, gather_sem.at[1])

    zero_tile = jnp.zeros((angles, LANES), jnp.float32)
    residual = jnp.concatenate(
        [
            jnp.concatenate([res_ref[r * tiles + tile] for tile in range(tiles)] + [zero_tile], axis=1)
            for r in range(2)
        ],
        axis=0,
    )
    residual = shift_rows(residual, off_ref[...])
    high, low = split_bf16(residual)
    update = jnp.dot(
        f2_ref[...], jnp.concatenate([high, low, high, low], axis=0),
        preferred_element_type=jnp.float32,
    )
    updates = []
    for layer in range(3):
        total = None
        for tap in range(TAPS):
            start = layer * first + tap * slices
            term = update[start : start + slices]
            if tap:
                term = roll_left(term, tap)
            total = term if total is None else total + term
        updates.append(total[:, :columns])
    part_c = relax_step * updates[0]
    part_a = vol_ref[0] + relax_step * updates[1]
    part_b = vol_ref[1] + relax_step * updates[2]
    main_ref[0] = part_b
    main_ref[1] = part_a
    main_ref[2] = part_c
    lo_ref[0] = part_a[0:1]
    lo_ref[1] = part_b[0:1]
    lo_ref[2] = part_c[0:1]
    last = slices - 1
    hi_ref[0] = part_b[last:]
    hi_ref[1] = part_a[last:]
    hi_ref[2] = part_c[last:]

    def send_all(moves, sems):
        copies = []
        for i, (src, dst, target) in enumerate(moves):
            copy = pltpu.make_async_remote_copy(
                src_ref=src, dst_ref=dst, send_sem=sems.at[2 * i], recv_sem=sems.at[2 * i + 1],
                device_id=target, device_id_type=MESH,
            )
            copy.start()
            copies.append(copy)
        return copies

    copies = send_all(
        (
            (main_ref.at[pl.ds(1, 2)], main_high, (depth_of, below)),
            (main_ref.at[0], main_low, (depth_of, above)),
            (hi_ref.at[pl.ds(0, 2)], got_m, (ahead, height_of)),
            (hi_ref.at[pl.ds(1, 2)], got_pm, (ahead, below)),
            (lo_ref, got_p, (behind, height_of)),
            (lo_ref.at[1], got_mp, (behind, above)),
            (lo_ref.at[2], got_pp, (behind, below)),
        ),
        edge_sem,
    )
    for copy in copies:
        copy.wait()

    def topped(value):
        return jnp.where(height_of < heights - 1, value, 0.0)

    fields = [
        main_low[...] + part_c,
        part_a,
        part_b + topped(main_high[1]),
        main_high[0],
    ]
    after = [got_mp[...] + got_p[2], got_p[0], got_p[1] + topped(got_pp[...])]
    before = [got_m[1], got_m[0] + topped(got_pm[1]), got_pm[0]]
    places = (height_of, depth_of, heights, depths)
    part_a, part_b = total_variation(fields, after, before, *places)

    main2_ref[0] = part_a
    main2_ref[1] = part_b
    lo2_ref[0] = part_a[0:1]
    lo2_ref[1] = part_b[0:1]
    hi2_ref[0] = part_a[last:]
    hi2_ref[1] = part_b[last:]
    copies = send_all(
        (
            (main2_ref.at[0], main2_high, (depth_of, below)),
            (main2_ref.at[1], main2_low, (depth_of, above)),
            (hi2_ref, got2_m, (ahead, height_of)),
            (hi2_ref.at[0], got2_pm, (ahead, below)),
            (lo2_ref, got2_p, (behind, height_of)),
            (lo2_ref.at[1], got2_mp, (behind, above)),
        ),
        edge2_sem,
    )
    for copy in copies:
        copy.wait()
    fields = [main2_low[...], part_a, part_b, main2_high[...]]
    after = [got2_mp[...], got2_p[0], got2_p[1]]
    before = [got2_m[0], got2_m[1], got2_pm[...]]
    part_a, part_b = total_variation(fields, after, before, *places)
    out_ref[0] = part_a
    out_ref[1] = part_b
    all_of(part_ref, scatter_sem.at[0])
    all_of(res_ref, gather_sem.at[0])


def factor_matrix(taps, angle_index, first_slice, total_slices):
    tap_count, angles, slices = taps.shape
    angle_value = 2.0 * math.pi / N_VIEWS * angle_index.astype(jnp.float32)
    depth_place = (first_slice + jnp.arange(slices, dtype=jnp.int32)).astype(jnp.float32) + 0.5
    rise = (
        0.5
        + 0.45
        * jnp.sin(angle_value)[:, None]
        * jnp.cos(math.pi / total_slices * depth_place)[None, :]
    )
    lower = (taps * (1.0 - rise)[None]).transpose(1, 0, 2).reshape(angles, tap_count * slices)
    upper = (taps * rise[None]).transpose(1, 0, 2).reshape(angles, tap_count * slices)
    none = jnp.zeros_like(lower)
    return jnp.concatenate(
        [
            jnp.concatenate([upper, lower, none], axis=1),
            jnp.concatenate([none, upper, lower], axis=1),
        ],
        axis=0,
    )


def per_device(volume, measured, taps, band_offset, angle_index):
    heights = lax.axis_size("height")
    depths = lax.axis_size("depth")
    layers, slices, columns = volume.shape
    angles = measured.shape[0]
    depth_of = lax.axis_index("depth")
    factor = factor_matrix(taps, angle_index, depth_of * slices, slices * depths)
    high, low = split_bf16(factor)
    first = TAPS * slices

    def doubled(part):
        return [part[:, :first], part[:, :first], part[:, first:], part[:, first:]]

    f1 = jnp.concatenate(
        [jnp.concatenate(doubled(high), axis=1), jnp.concatenate(doubled(low), axis=1)], axis=0
    )
    f2 = jnp.concatenate([high, high, low, low], axis=0).T
    band = jnp.swapaxes(measured, 0, 1)
    none = jnp.zeros_like(band)
    odd = depth_of % 2 == 1
    band = jnp.where(
        odd, jnp.concatenate([none, band], axis=2), jnp.concatenate([band, none], axis=2)
    )
    offsets = lax.dynamic_slice_in_dim(band_offset, depth_of, 1, 1)
    offsets = jnp.concatenate([offsets, offsets], axis=0)
    f32 = jnp.float32
    chunks = (depths, angles, LANES)
    main = (slices, columns)
    edge = (1, columns)
    vmem = pltpu.VMEM
    scratch = [
        vmem(main, f32), vmem(chunks, f32), vmem(chunks, f32), vmem(chunks, f32),
        vmem((3, *main), f32), vmem(main, f32), vmem((2, *main), f32),
        vmem((3, *edge), f32), vmem((3, *edge), f32),
        vmem((2, *edge), f32), vmem((2, *edge), f32), vmem((3, *edge), f32),
        vmem(edge, f32), vmem(edge, f32),
        vmem((2, *main), f32), vmem(main, f32), vmem(main, f32),
        vmem((2, *edge), f32), vmem((2, *edge), f32),
        vmem((2, *edge), f32), vmem(edge, f32), vmem((2, *edge), f32), vmem(edge, f32),
        pltpu.SemaphoreType.DMA((2,)),
        pltpu.SemaphoreType.DMA((2,)),
        pltpu.SemaphoreType.DMA((2,)),
        pltpu.SemaphoreType.DMA((14,)),
        pltpu.SemaphoreType.DMA((12,)),
    ]
    return pl.pallas_call(
        functools.partial(kernel, heights, depths),
        out_shape=jax.ShapeDtypeStruct(volume.shape, f32),
        in_specs=[pl.BlockSpec(memory_space=pltpu.VMEM)] * 5,
        out_specs=pl.BlockSpec(memory_space=pltpu.VMEM),
        scratch_shapes=scratch,
        compiler_params=pltpu.CompilerParams(
            collective_id=0, has_side_effects=True, vmem_limit_bytes=32 * 1024 * 1024
        ),
    )(volume, f1, f2, band, offsets)


def solution(mesh):
    in_specs = (
        P("height", "depth", None),
        P(None, "height", "depth"),
        P(None, None, "depth"),
        P(),
        P(),
    )
    out_specs = P("height", "depth", None)
    return jax.shard_map(
        per_device, mesh=mesh, in_specs=in_specs, out_specs=out_specs, check_vma=False
    )
```

```python
import functools
import math

import jax
import jax.numpy as jnp
from jax import lax
from jax.experimental import pallas as pl
from jax.experimental.pallas import tpu as pltpu
from jax.sharding import PartitionSpec as P

TAPS = 4
OFFMAX = 64
N_VIEWS = 720
LANES = 128
SUBLANES = 8
NEAR = 4

relax_step = 0.5
tv_step = 0.08
tv_eps = 0.1

MESH = pl.DeviceIdType.MESH


def split_bf16(value):
    high = value.astype(jnp.bfloat16)
    low = (value - high.astype(jnp.float32)).astype(jnp.bfloat16)
    return high, low


def roll_left(value, amount):
    return pltpu.roll(value, value.shape[1] - amount, 1)


def shift_rows(value, amount):
    move = amount + OFFMAX
    top = move // OFFMAX
    moved_left = roll_left(value, OFFMAX)
    moved_right = pltpu.roll(value, OFFMAX, 1)
    value = jnp.where(top == 0, moved_right, jnp.where(top == 1, value, moved_left))
    for bit in range(6):
        stride = 1 << bit
        value = jnp.where((move // stride) % 2 == 1, roll_left(value, stride), value)
    return value


def total_variation(fields, after, before, height_of, depth_of, heights, depths):
    slices, columns = fields[0].shape
    row = lax.broadcasted_iota(jnp.int32, (slices, columns), 0)
    lane = lax.broadcasted_iota(jnp.int32, (slices, columns), 1)
    inner = lane < columns - 1
    last_layer = height_of == heights - 1
    open_row = (row < slices - 1) | (depth_of < depths - 1)
    along_h, along_d, along_w = [], [], []
    for i in range(3):
        here = fields[i]
        up = fields[i + 1] - here
        if i == 2:
            up = jnp.where(last_layer, 0.0, up)
        deep = jnp.where(row == slices - 1, after[i], pltpu.roll(here, slices - 1, 0)) - here
        deep = jnp.where(open_row, deep, 0.0)
        wide = jnp.where(inner, roll_left(here, 1) - here, 0.0)
        scale = lax.rsqrt(tv_eps * tv_eps + up * up + deep * deep + wide * wide)
        across = up * scale
        if i == 0:
            across = jnp.where(height_of > 0, across, 0.0)
        along_h.append(across)
        along_d.append(deep * scale)
        along_w.append(wide * scale)
    here = jnp.where(row == 0, before[0], before[1])
    above = jnp.where(row == 0, before[1], before[2])
    ahead = jnp.where(row == 0, fields[1][0:1], fields[2][0:1])
    up = above - here
    up = jnp.where(last_layer & (row == 1), 0.0, up)
    deep = ahead - here
    wide = jnp.where(inner, roll_left(here, 1) - here, 0.0)
    scale = lax.rsqrt(tv_eps * tv_eps + up * up + deep * deep + wide * wide)
    deep_before = jnp.where(depth_of > 0, deep * scale, 0.0)
    results = []
    for i in (1, 2):
        d_before = jnp.where(row == 0, deep_before[i - 1 : i], pltpu.roll(along_d[i], 1, 0))
        w_before = pltpu.roll(along_w[i], 1, 1)
        diverge = (
            (along_h[i] - along_h[i - 1]) + (along_d[i] - d_before) + (along_w[i] - w_before)
        )
        results.append(fields[i] + tv_step * diverge)
    return results


def kernel(
    heights, depths,
    vol_hbm, meas_hbm, taps_hbm, off_hbm, angle_hbm,
    out_ref,
    vol_ref, meas_ref, taps_ref, off_ref, angle_ref,
    halo_ref, part_0, part_1, got_1a, got_1b, got_0a, got_0b, sum_1, sum_0, res_0, res_1,
    main_ref, main_low, main_high,
    lo_ref, hi_ref, got_m, got_pm, got_p, got_mp, got_pp,
    main2_ref, main2_low, main2_high,
    lo2_ref, hi2_ref, got2_m, got2_pm, got2_p, got2_mp,
    load_sem, halo_sem, ring_sem, edge_sem, edge2_sem,
):
    height_of = lax.axis_index("height")
    depth_of = lax.axis_index("depth")
    above, below = height_of + 1, height_of - 1
    has_above, has_below = height_of < heights - 1, height_of > 0
    ahead = lax.rem(depth_of + 1, depths)
    behind = lax.rem(depth_of + depths - 1, depths)
    far_of, near_of = depth_of // NEAR, depth_of % NEAR
    far_count = depths // NEAR
    _, slices, columns = vol_ref.shape
    tiles = columns // LANES
    angles = off_ref.shape[0]
    taps = taps_ref.shape[0]

    loads = [
        pltpu.make_async_copy(src, dst, load_sem.at[i])
        for i, (src, dst) in enumerate(
            (
                (vol_hbm, vol_ref), (angle_hbm, angle_ref), (taps_hbm, taps_ref),
                (off_hbm, off_ref), (meas_hbm, meas_ref),
            )
        )
    ]
    for load in loads:
        load.start()

    barrier = pltpu.get_barrier_semaphore()

    def greet(depth, height):
        pl.semaphore_signal(barrier, inc=1, device_id=(depth, height), device_id_type=MESH)

    def fars():
        order = sorted(range(1, far_count), key=lambda i: -min(i, far_count - i))
        return [lax.rem(far_of + i, far_count) for i in order]

    def nears():
        return [lax.rem(near_of + i, NEAR) for i in range(1, NEAR)]

    @pl.when(has_above)
    def _():
        for depth in (depth_of, ahead, behind):
            greet(depth, above)

    @pl.when(has_below)
    def _():
        for depth in (depth_of, ahead, behind):
            greet(depth, below)

    for depth in (ahead, behind):
        greet(depth, height_of)
    for far in fars():
        greet(far * NEAR + near_of, height_of)
    for near in nears():
        greet(far_of * NEAR + near, height_of)
    partners = far_count + NEAR + 3 * has_above.astype(jnp.int32) + 3 * has_below.astype(jnp.int32)
    pl.semaphore_wait(barrier, partners)

    halo_copy = pltpu.make_async_remote_copy(
        src_ref=vol_hbm.at[1], dst_ref=halo_ref,
        send_sem=halo_sem.at[0], recv_sem=halo_sem.at[1],
        device_id=(depth_of, above), device_id_type=MESH,
    )

    @pl.when(has_above)
    def _():
        halo_copy.start()

    for load in loads[1:]:
        load.wait()

    row = lax.broadcasted_iota(jnp.int32, (angles, LANES), 0)
    lane = lax.broadcasted_iota(jnp.int32, (angles, LANES), 1)
    view = jnp.zeros((angles, LANES), jnp.float32)
    for i in range(angles):
        view = jnp.where(row == i, angle_ref[i].astype(jnp.float32), view)
    angle_value = 2.0 * math.pi / N_VIEWS * view
    depth_place = (depth_of * slices + lane % slices).astype(jnp.float32) + 0.5
    rise = 0.5 + 0.45 * jnp.sin(angle_value) * jnp.cos(math.pi / (slices * depths) * depth_place)
    weight = jnp.concatenate([taps_ref[tap] for tap in range(taps)], axis=0)
    weight = jnp.concatenate(
        [weight, jnp.zeros((taps * slices, LANES - angles), jnp.float32)], axis=1
    )
    weight = jnp.concatenate(
        [weight, jnp.zeros((LANES - taps * slices, LANES), jnp.float32)], axis=0
    ).T[:angles]
    lower, upper = weight * (1.0 - rise), weight * rise
    first = taps * slices
    lower_1 = pltpu.roll(lower, first, 1)
    upper_1 = pltpu.roll(upper, first, 1)
    own = jnp.concatenate([lower, upper + lower_1], axis=0)
    own = jnp.concatenate(split_bf16(own + pltpu.roll(own, 2 * first, 1)), axis=0)
    from_halo = jnp.concatenate(split_bf16((upper + upper_1)[:, : 2 * first]), axis=0)
    back = jnp.concatenate([upper + lower_1, upper_1 + pltpu.roll(lower, 2 * first, 1)], axis=0)
    back = jnp.concatenate([back] * 4, axis=0).T
    back_high = back.astype(jnp.bfloat16).astype(jnp.float32)
    wide_lane = lax.broadcasted_iota(jnp.int32, back.shape, 1)
    back = jnp.where(wide_lane < LANES // 2, back_high, back - back_high).astype(jnp.bfloat16)
    back = back[: 3 * first]
    off_lane = lax.broadcasted_iota(jnp.int32, off_ref.shape, 1)
    offset = jnp.where(off_lane == depth_of, off_ref[...].astype(jnp.float32), 0.0)
    offset = jnp.sum(offset, axis=1, keepdims=True).astype(jnp.int32)
    band_pad = jnp.zeros((angles, LANES - meas_ref.shape[2]), jnp.float32)
    bands = []
    for r in range(2):
        band = jnp.concatenate([meas_ref[:, r, :], band_pad], axis=1)
        bands.append(jnp.where(depth_of % 2 == 1, pltpu.roll(band, LANES // 2, 1), band))

    zeros = jnp.zeros((slices, LANES), jnp.float32)

    def spread(layers):
        wide = [jnp.concatenate([layer, zeros], axis=1) for layer in layers]
        rows = []
        for layer in wide:
            for tap in range(taps):
                rows.append(layer if tap == 0 else pltpu.roll(layer, tap, 1))
        high, low = split_bf16(jnp.concatenate(rows, axis=0))
        return jnp.concatenate([high, low], axis=0)

    def dot(a, b):
        return jnp.dot(a, b, preferred_element_type=jnp.float32)

    def publish(image, band, ref):
        image = shift_rows(image, -offset)
        halves = angles // SUBLANES
        for tile in range(tiles):
            for half in range(halves):
                ref[tile * halves + half] = -image[
                    half * SUBLANES : (half + 1) * SUBLANES, tile * LANES : (tile + 1) * LANES
                ]
        for half in range(halves):
            place = depth_of // 2 * halves + half
            ref[place] = ref[place] + band[half * SUBLANES : (half + 1) * SUBLANES]

    def send(src, dst, number, depth):
        pltpu.make_async_remote_copy(
            src_ref=src, dst_ref=dst,
            send_sem=ring_sem.at[2 * number], recv_sem=ring_sem.at[2 * number + 1],
            device_id=(depth, height_of), device_id_type=MESH,
        ).start()

    def wait_for(ref, number, received):
        pltpu.make_async_copy(ref, ref, ring_sem.at[2 * number + int(received)]).wait()

    def total(parts):
        while len(parts) > 1:
            parts = [a + b for a, b in zip(parts[::2], parts[1::2])]
        return parts[0]

    loads[0].wait()
    both = dot(own, spread([vol_ref[0], vol_ref[1]]))
    both = both[: 2 * angles] + both[2 * angles :]
    publish(both[angles:], bands[1], part_1)
    for far in fars():
        send(part_1.at[pl.ds(far * NEAR, NEAR)], got_1a.at[far_of], 0, far * NEAR + near_of)
    got_1a[far_of] = part_1[pl.ds(far_of * NEAR, NEAR)]

    @pl.when(has_below)
    def _():
        halo_copy.wait_recv()

    @pl.when(jnp.logical_not(has_below))
    def _():
        halo_ref[...] = jnp.zeros_like(halo_ref)

    spilled = dot(from_halo, spread([halo_ref[...]]))
    publish(both[:angles] + (spilled[:angles] + spilled[angles:]), bands[0], part_0)
    for near in nears():
        send(part_0.at[pl.ds(near * far_count, far_count)], got_0a.at[near_of], 1, far_of * NEAR + near)
    got_0a[near_of] = part_0[pl.ds(near_of * far_count, far_count)]

    wait_for(got_1a.at[pl.ds(0, far_count - 1)], 0, True)
    sum_1[...] = total([got_1a[i] for i in range(far_count)])
    for near in nears():
        send(sum_1.at[near], got_1b.at[near_of], 2, far_of * NEAR + near)
    got_1b[near_of] = sum_1[near_of]

    wait_for(got_0a.at[pl.ds(0, NEAR - 1)], 1, True)
    sum_0[...] = total([got_0a[i] for i in range(NEAR)])
    for far in fars():
        send(sum_0.at[far], got_0b.at[far_of], 3, far * NEAR + near_of)
    got_0b[far_of] = sum_0[far_of]

    wait_for(got_1b.at[pl.ds(0, NEAR - 1)], 2, True)
    mine_1, mine_0 = depth_of, near_of * far_count + far_of
    res_1[mine_1] = total([got_1b[i] for i in range(NEAR)])
    for near in nears():
        send(res_1.at[mine_1], res_1.at[mine_1], 4, far_of * NEAR + near)
    wait_for(got_0b.at[pl.ds(0, far_count - 1)], 3, True)
    res_0[mine_0] = total([got_0b[i] for i in range(far_count)])
    for far in fars():
        send(res_0.at[mine_0], res_0.at[mine_0], 5, far * NEAR + near_of)

    wait_for(res_1.at[pl.ds(0, NEAR - 1)], 4, True)
    block_1 = res_1.at[pl.ds(far_of * NEAR, NEAR)]
    for far in fars():
        send(block_1, block_1, 6, far * NEAR + near_of)
    wait_for(res_0.at[pl.ds(0, far_count - 1)], 5, True)
    block_0 = res_0.at[pl.ds(near_of * far_count, far_count)]
    for near in nears():
        send(block_0, block_0, 7, far_of * NEAR + near)
    wait_for(res_1.at[pl.ds(0, depths - NEAR)], 6, True)
    wait_for(res_0.at[pl.ds(0, depths - far_count)], 7, True)

    def settle():
        wait_for(part_1.at[pl.ds(0, depths - NEAR)], 0, False)
        wait_for(part_0.at[pl.ds(0, depths - far_count)], 1, False)
        wait_for(sum_1.at[pl.ds(0, NEAR - 1)], 2, False)
        wait_for(sum_0.at[pl.ds(0, far_count - 1)], 3, False)
        wait_for(res_1.at[pl.ds(0, NEAR - 1)], 4, False)
        wait_for(res_0.at[pl.ds(0, far_count - 1)], 5, False)
        wait_for(res_1.at[pl.ds(0, depths - NEAR)], 6, False)
        wait_for(res_0.at[pl.ds(0, depths - far_count)], 7, False)

        @pl.when(has_above)
        def _():
            halo_copy.wait_send()

    zero_tile = jnp.zeros((angles, LANES), jnp.float32)

    def image_of(ref):
        columns_of = [
            jnp.concatenate([ref[2 * tile], ref[2 * tile + 1]], axis=0) for tile in range(tiles)
        ]
        high, low = split_bf16(
            shift_rows(jnp.concatenate(columns_of + [zero_tile], axis=1), offset)
        )
        return high, low

    high_1, low_1 = image_of(res_1)
    high_0, low_0 = image_of(res_0)
    update = dot(
        back, jnp.concatenate([high_0, high_1, low_0, low_1] * 2, axis=0)
    )
    updates = []
    for layer in range(3):
        whole = None
        for tap in range(taps):
            start = layer * first + tap * slices
            term = update[start : start + slices]
            if tap:
                term = roll_left(term, tap)
            whole = term if whole is None else whole + term
        updates.append(whole[:, :columns])
    part_c = relax_step * updates[0]
    part_a = vol_ref[0] + relax_step * updates[1]
    part_b = vol_ref[1] + relax_step * updates[2]
    main_ref[0] = part_b
    main_ref[1] = part_a
    main_ref[2] = part_c
    lo_ref[0] = part_a[0:1]
    lo_ref[1] = part_b[0:1]
    lo_ref[2] = part_c[0:1]
    last = slices - 1
    hi_ref[0] = part_b[last:]
    hi_ref[1] = part_a[last:]
    hi_ref[2] = part_c[last:]

    def exchange(moves, sems):
        copies = []

        def when(condition, action):
            if condition is None:
                action()
            else:
                pl.when(condition)(action)

        for i, (src, dst, target, sent, got) in enumerate(moves):
            copy = pltpu.make_async_remote_copy(
                src_ref=src, dst_ref=dst, send_sem=sems.at[2 * i], recv_sem=sems.at[2 * i + 1],
                device_id=target, device_id_type=MESH,
            )
            when(sent, copy.start)
            copies.append((copy, sent, got, dst))
        for copy, sent, got, dst in copies:
            when(sent, copy.wait_send)
            when(got, copy.wait_recv)
            if got is not None:

                @pl.when(jnp.logical_not(got))
                def _():
                    dst[...] = jnp.zeros(dst.shape, jnp.float32)

    exchange(
        (
            (main_ref.at[pl.ds(1, 2)], main_high, (depth_of, below), has_below, has_above),
            (main_ref.at[0], main_low, (depth_of, above), has_above, has_below),
            (hi_ref.at[pl.ds(1, 2)], got_pm, (ahead, below), has_below, has_above),
            (lo_ref.at[2], got_pp, (behind, below), has_below, has_above),
            (lo_ref.at[1], got_mp, (behind, above), has_above, has_below),
            (hi_ref.at[pl.ds(0, 2)], got_m, (ahead, height_of), None, None),
            (lo_ref, got_p, (behind, height_of), None, None),
        ),
        edge_sem,
    )
    fields = [main_low[...] + part_c, part_a, part_b + main_high[1], main_high[0]]
    after = [got_mp[...] + got_p[2], got_p[0], got_p[1] + got_pp[...]]
    before = [got_m[1], got_m[0] + got_pm[1], got_pm[0]]
    places = (height_of, depth_of, heights, depths)
    part_a, part_b = total_variation(fields, after, before, *places)

    main2_ref[0] = part_a
    main2_ref[1] = part_b
    lo2_ref[0] = part_a[0:1]
    lo2_ref[1] = part_b[0:1]
    hi2_ref[0] = part_a[last:]
    hi2_ref[1] = part_b[last:]
    exchange(
        (
            (main2_ref.at[0], main2_high, (depth_of, below), has_below, has_above),
            (main2_ref.at[1], main2_low, (depth_of, above), has_above, has_below),
            (hi2_ref.at[0], got2_pm, (ahead, below), has_below, has_above),
            (lo2_ref.at[1], got2_mp, (behind, above), has_above, has_below),
            (hi2_ref, got2_m, (ahead, height_of), None, None),
            (lo2_ref, got2_p, (behind, height_of), None, None),
        ),
        edge2_sem,
    )
    fields = [main2_low[...], part_a, part_b, main2_high[...]]
    after = [got2_mp[...], got2_p[0], got2_p[1]]
    before = [got2_m[0], got2_m[1], got2_pm[...]]
    part_a, part_b = total_variation(fields, after, before, *places)
    out_ref[0] = part_a
    out_ref[1] = part_b
    settle()


def per_device(volume, measured, taps, band_offset, angle_index):
    heights = lax.axis_size("height")
    depths = lax.axis_size("depth")
    f32 = jnp.float32
    layers, slices, columns = volume.shape
    far = depths // NEAR
    taps = jnp.swapaxes(taps, 1, 2)
    tile = (SUBLANES, LANES)
    main = (slices, columns)
    edge = (1, columns)
    vmem = pltpu.VMEM
    scratch = [
        vmem(volume.shape, f32), vmem(measured.shape, f32), vmem(taps.shape, f32),
        vmem(band_offset.shape, jnp.int32), pltpu.SMEM(angle_index.shape, jnp.int32),
        vmem(main, f32), vmem((depths, *tile), f32), vmem((depths, *tile), f32),
        vmem((far, NEAR, *tile), f32), vmem((NEAR, *tile), f32),
        vmem((NEAR, far, *tile), f32), vmem((far, *tile), f32),
        vmem((NEAR, *tile), f32), vmem((far, *tile), f32),
        vmem((depths, *tile), f32), vmem((depths, *tile), f32),
        vmem((3, *main), f32), vmem(main, f32), vmem((2, *main), f32),
        vmem((3, *edge), f32), vmem((3, *edge), f32),
        vmem((2, *edge), f32), vmem((2, *edge), f32), vmem((3, *edge), f32),
        vmem(edge, f32), vmem(edge, f32),
        vmem((2, *main), f32), vmem(main, f32), vmem(main, f32),
        vmem((2, *edge), f32), vmem((2, *edge), f32),
        vmem((2, *edge), f32), vmem(edge, f32), vmem((2, *edge), f32), vmem(edge, f32),
        pltpu.SemaphoreType.DMA((5,)),
        pltpu.SemaphoreType.DMA((2,)),
        pltpu.SemaphoreType.DMA((16,)),
        pltpu.SemaphoreType.DMA((14,)),
        pltpu.SemaphoreType.DMA((12,)),
    ]
    return pl.pallas_call(
        functools.partial(kernel, heights, depths),
        out_shape=jax.ShapeDtypeStruct(volume.shape, f32),
        in_specs=[pl.BlockSpec(memory_space=pl.ANY)] * 5,
        out_specs=pl.BlockSpec(memory_space=pltpu.VMEM),
        scratch_shapes=scratch,
        compiler_params=pltpu.CompilerParams(
            collective_id=0, has_side_effects=True, vmem_limit_bytes=60 * 1024 * 1024
        ),
    )(volume, measured, taps, band_offset, angle_index)


def solution(mesh):
    in_specs = (
        P("height", "depth", None),
        P(None, "height", "depth"),
        P(None, None, "depth"),
        P(),
        P(),
    )
    out_specs = P("height", "depth", None)
    return jax.shard_map(
        per_device, mesh=mesh, in_specs=in_specs, out_specs=out_specs, check_vma=False
    )
```

```python
import functools
import math

import jax
import jax.numpy as jnp
from jax import lax
from jax.experimental import pallas as pl
from jax.experimental.pallas import tpu as pltpu
from jax.sharding import PartitionSpec as P

TAPS = 4
OFFMAX = 64
N_VIEWS = 720
LANES = 128
SUBLANES = 8
NEAR = 4

relax_step = 0.5
tv_step = 0.08
tv_eps = 0.1

MESH = pl.DeviceIdType.MESH


def split_bf16(value):
    high = value.astype(jnp.bfloat16)
    low = (value - high.astype(jnp.float32)).astype(jnp.bfloat16)
    return high, low


def roll_left(value, amount):
    return pltpu.roll(value, value.shape[1] - amount, 1)


def shift_rows(value, amount):
    move = amount + OFFMAX
    top = move // OFFMAX
    moved_left = roll_left(value, OFFMAX)
    moved_right = pltpu.roll(value, OFFMAX, 1)
    value = jnp.where(top == 0, moved_right, jnp.where(top == 1, value, moved_left))
    for bit in range(6):
        stride = 1 << bit
        value = jnp.where((move // stride) % 2 == 1, roll_left(value, stride), value)
    return value


def total_variation(fields, first_layer, height_total, depth_place, depth_total):
    rows, columns = fields[0].shape
    lane = lax.broadcasted_iota(jnp.int32, (rows, columns), 1)
    inner = lane < columns - 1
    open_row = (depth_place >= 0) & (depth_place + 1 < depth_total)
    results = []
    under = None
    for i in range(len(fields) - 1):
        here = fields[i]
        layer = first_layer + i
        up = fields[i + 1] - here
        up = jnp.where((layer >= 0) & (layer + 1 < height_total), up, 0.0)
        deep = jnp.where(open_row, pltpu.roll(here, rows - 1, 0) - here, 0.0)
        wide = jnp.where(inner, roll_left(here, 1) - here, 0.0)
        scale = lax.rsqrt(tv_eps * tv_eps + up * up + deep * deep + wide * wide)
        up = up * scale
        if i:
            deep = deep * scale
            wide = wide * scale
            diverge = (up - under) + (deep - pltpu.roll(deep, 1, 0)) + (wide - pltpu.roll(wide, 1, 1))
            results.append(here + tv_step * diverge)
        under = up
    return results


def kernel(
    heights, depths,
    vol_hbm, meas_hbm, taps_hbm, off_hbm, angle_hbm,
    out_ref,
    vol_ref, meas_ref, taps_ref, off_ref, angle_ref,
    halo_ref, meas_up, side_ref, taps_ahead, taps_behind,
    part_1, got_1a, sum_1, got_1b, res_1,
    part_0, got_0a, sum_0, got_0b, res_0,
    part_2, got_2a, sum_2, got_2b, res_2,
    up_ref, low_ref, down_ref, high_ref,
    up2_ref, low2_ref, up2_edge, low2_edge,
    load_sem, halo_sem, side_sem, ring_sem, edge_sem,
):
    height_of = lax.axis_index("height")
    depth_of = lax.axis_index("depth")
    above, below = height_of + 1, height_of - 1
    has_above, has_below = height_of < heights - 1, height_of > 0
    ahead = lax.rem(depth_of + 1, depths)
    behind = lax.rem(depth_of + depths - 1, depths)
    far_of, near_of = depth_of // NEAR, depth_of % NEAR
    far_count = depths // NEAR
    _, slices, columns = vol_ref.shape
    tiles = columns // LANES
    angles = off_ref.shape[0]
    taps = taps_ref.shape[0]

    barrier = pltpu.get_barrier_semaphore()

    def greet(depth, height):
        pl.semaphore_signal(barrier, inc=1, device_id=(depth, height), device_id_type=MESH)

    def fars():
        order = sorted(range(1, far_count), key=lambda i: -min(i, far_count - i))
        return [lax.rem(far_of + i, far_count) for i in order]

    def nears():
        return [lax.rem(near_of + i, NEAR) for i in range(1, NEAR)]

    @pl.when(has_below)
    def _():
        greet(depth_of, below)

    @pl.when(has_above)
    def _():
        greet(depth_of, above)

    for far in fars():
        greet(far * NEAR + near_of, height_of)
    for near in nears():
        greet(far_of * NEAR + near, height_of)
    for depth in (ahead, behind):
        greet(depth, height_of)

    loads = [
        pltpu.make_async_copy(src, dst, load_sem.at[i])
        for i, (src, dst) in enumerate(
            (
                (vol_hbm, vol_ref), (angle_hbm, angle_ref), (taps_hbm, taps_ref),
                (off_hbm, off_ref), (meas_hbm, meas_ref),
            )
        )
    ]
    for load in loads:
        load.start()
    partners = far_count + NEAR + has_above.astype(jnp.int32) + has_below.astype(jnp.int32)
    pl.semaphore_wait(barrier, partners)

    def remote(src, dst, sems, number, depth, height):
        return pltpu.make_async_remote_copy(
            src_ref=src, dst_ref=dst,
            send_sem=sems.at[2 * number], recv_sem=sems.at[2 * number + 1],
            device_id=(depth, height), device_id_type=MESH,
        )

    halos = [
        remote(vol_hbm.at[0], halo_ref, halo_sem, 0, depth_of, below),
        remote(meas_hbm, meas_up, halo_sem, 1, depth_of, below),
    ]

    @pl.when(has_below)
    def _():
        for copy in halos:
            copy.start()

    for load in loads[1:]:
        load.wait()

    row = lax.broadcasted_iota(jnp.int32, (angles, LANES), 0)
    lane = lax.broadcasted_iota(jnp.int32, (angles, LANES), 1)
    view = jnp.zeros((angles, LANES), jnp.float32)
    for i in range(angles):
        view = jnp.where(row == i, angle_ref[i].astype(jnp.float32), view)
    swing = 0.45 * jnp.sin(2.0 * math.pi / N_VIEWS * view)
    first = taps * slices

    def weights(ref, depth):
        weight = jnp.concatenate([ref[tap] for tap in range(taps)], axis=0)
        weight = jnp.concatenate([weight, jnp.zeros((first, LANES - angles), jnp.float32)], axis=1)
        weight = jnp.concatenate([weight, jnp.zeros((LANES - first, LANES), jnp.float32)], axis=0)
        weight = weight.T[:angles]
        depth_place = (depth * slices + lane % slices).astype(jnp.float32) + 0.5
        rise = 0.5 + swing * jnp.cos(math.pi / (slices * depths) * depth_place)
        return weight * (1.0 - rise), weight * rise

    def offset_of(depth):
        off_lane = lax.broadcasted_iota(jnp.int32, off_ref.shape, 1)
        offset = jnp.where(off_lane == depth, off_ref[...].astype(jnp.float32), 0.0)
        return jnp.sum(offset, axis=1, keepdims=True).astype(jnp.int32)

    def factor(lower, upper):
        return jnp.concatenate(
            [
                upper + pltpu.roll(lower, first, 1),
                pltpu.roll(upper, first, 1) + pltpu.roll(lower, 2 * first, 1),
            ],
            axis=0,
        )

    def transposed(parts):
        whole = jnp.concatenate(parts * 4, axis=0)
        turned = whole.T
        high = turned.astype(jnp.bfloat16).astype(jnp.float32)
        place = lax.broadcasted_iota(jnp.int32, turned.shape, 1)
        return jnp.where(place < turned.shape[1] // 2, high, turned - high).astype(jnp.bfloat16)[: 3 * first]

    lower, upper = weights(taps_ref, depth_of)
    offset = offset_of(depth_of)
    own = jnp.concatenate(
        [upper + pltpu.roll(lower, first, 1), pltpu.roll(upper, first, 1), lower], axis=0
    )
    own = jnp.concatenate(split_bf16(own + pltpu.roll(own, 2 * first, 1)), axis=0)
    from_halo = (lower + pltpu.roll(lower, first, 1))[:, : 2 * first]
    from_halo = jnp.concatenate(split_bf16(from_halo), axis=0)
    band_pad = jnp.zeros((angles, LANES - meas_ref.shape[2]), jnp.float32)

    def band_of(ref, r):
        band = jnp.concatenate([ref[:, r, :], band_pad], axis=1)
        return jnp.where(depth_of % 2 == 1, pltpu.roll(band, LANES // 2, 1), band)

    zeros = jnp.zeros((slices, LANES), jnp.float32)

    def spread(layers):
        wide = [jnp.concatenate([layer, zeros], axis=1) for layer in layers]
        rows = []
        for layer in wide:
            for tap in range(taps):
                rows.append(layer if tap == 0 else pltpu.roll(layer, tap, 1))
        high, low = split_bf16(jnp.concatenate(rows, axis=0))
        return jnp.concatenate([high, low], axis=0)

    def dot(a, b):
        return jnp.dot(a, b, preferred_element_type=jnp.float32)

    halves = angles // SUBLANES

    def publish(image, band, ref):
        image = shift_rows(image, -offset)
        for tile in range(tiles):
            for half in range(halves):
                ref[tile * halves + half] = -image[
                    half * SUBLANES : (half + 1) * SUBLANES, tile * LANES : (tile + 1) * LANES
                ]
        for half in range(halves):
            place = depth_of // 2 * halves + half
            ref[place] = ref[place] + band[half * SUBLANES : (half + 1) * SUBLANES]

    def to_far(src, dst, number):
        for far in fars():
            remote(src(far), dst, ring_sem, number, far * NEAR + near_of, height_of).start()

    def to_near(src, dst, number):
        for near in nears():
            remote(src(near), dst, ring_sem, number, far_of * NEAR + near, height_of).start()

    def wait_for(ref, count, number, received):
        some = ref.at[pl.ds(0, count)]
        pltpu.make_async_copy(some, some, ring_sem.at[2 * number + int(received)]).wait()

    def total(parts):
        while len(parts) > 1:
            parts = [a + b for a, b in zip(parts[::2], parts[1::2])]
        return parts[0]

    class FarFirst:
        def __init__(self, number, part, got_a, summed, got_b, res):
            self.number, self.part, self.got_a = number, part, got_a
            self.summed, self.got_b, self.res = summed, got_b, res

        def one(self):
            to_far(lambda far: self.part.at[pl.ds(far * NEAR, NEAR)], self.got_a.at[far_of], self.number)
            self.got_a[far_of] = self.part[pl.ds(far_of * NEAR, NEAR)]

        def two(self):
            wait_for(self.got_a, far_count - 1, self.number, True)
            self.summed[...] = total([self.got_a[i] for i in range(far_count)])
            to_near(lambda near: self.summed.at[near], self.got_b.at[near_of], self.number + 1)
            self.got_b[near_of] = self.summed[near_of]

        def three(self):
            wait_for(self.got_b, NEAR - 1, self.number + 1, True)
            self.res[depth_of] = total([self.got_b[i] for i in range(NEAR)])
            mine = self.res.at[depth_of]
            to_near(lambda near: mine, mine, self.number + 2)

        def four(self):
            wait_for(self.res, NEAR - 1, self.number + 2, True)
            block = self.res.at[pl.ds(far_of * NEAR, NEAR)]
            to_far(lambda far: block, block, self.number + 3)

        def five(self):
            wait_for(self.res, depths - NEAR, self.number + 3, True)

        def settle(self):
            wait_for(self.part, depths - NEAR, self.number, False)
            wait_for(self.summed, NEAR - 1, self.number + 1, False)
            wait_for(self.res, NEAR - 1, self.number + 2, False)
            wait_for(self.res, depths - NEAR, self.number + 3, False)

    class NearFirst(FarFirst):
        def one(self):
            size = far_count
            to_near(lambda near: self.part.at[pl.ds(near * size, size)], self.got_a.at[near_of], self.number)
            self.got_a[near_of] = self.part[pl.ds(near_of * size, size)]

        def two(self):
            wait_for(self.got_a, NEAR - 1, self.number, True)
            self.summed[...] = total([self.got_a[i] for i in range(NEAR)])
            to_far(lambda far: self.summed.at[far], self.got_b.at[far_of], self.number + 1)
            self.got_b[far_of] = self.summed[far_of]

        def three(self):
            wait_for(self.got_b, far_count - 1, self.number + 1, True)
            place = near_of * far_count + far_of
            self.res[place] = total([self.got_b[i] for i in range(far_count)])
            mine = self.res.at[place]
            to_far(lambda far: mine, mine, self.number + 2)

        def four(self):
            wait_for(self.res, far_count - 1, self.number + 2, True)
            block = self.res.at[pl.ds(near_of * far_count, far_count)]
            to_near(lambda near: block, block, self.number + 3)

        def five(self):
            wait_for(self.res, depths - far_count, self.number + 3, True)

        def settle(self):
            wait_for(self.part, depths - far_count, self.number, False)
            wait_for(self.summed, far_count - 1, self.number + 1, False)
            wait_for(self.res, far_count - 1, self.number + 2, False)
            wait_for(self.res, depths - far_count, self.number + 3, False)

    row_1 = FarFirst(0, part_1, got_1a, sum_1, got_1b, res_1)
    row_2 = NearFirst(4, part_0, got_0a, sum_0, got_0b, res_0)
    row_0 = FarFirst(8, part_2, got_2a, sum_2, got_2b, res_2)
    lowest = jnp.logical_not(has_below)

    loads[0].wait()
    count = 3 * angles
    both = dot(own, spread([vol_ref[0], vol_ref[1]]))
    both = both[:count] + both[count:]
    publish(both[:angles], band_of(meas_ref, 1), part_1)
    row_1.one()

    @pl.when(lowest)
    def _():
        publish(both[2 * angles :], band_of(meas_ref, 0), part_2)
        row_0.one()

    @pl.when(has_above)
    def _():
        for copy in halos:
            copy.wait_recv()
        spilled = dot(from_halo, spread([halo_ref[...]]))
        image = both[angles : 2 * angles] + (spilled[:angles] + spilled[angles:])
        publish(image, band_of(meas_up, 0), part_0)

    @pl.when(jnp.logical_not(has_above))
    def _():
        part_0[...] = jnp.zeros_like(part_0)

    row_2.one()

    last = slices - 2
    sides = [
        remote(taps_hbm, taps_behind, side_sem, 0, ahead, height_of),
        remote(taps_hbm, taps_ahead, side_sem, 1, behind, height_of),
        remote(
            vol_ref.at[:, pl.ds(last, 2)], side_ref.at[:, pl.ds(last, 2)], side_sem, 2, ahead, height_of
        ),
        remote(vol_ref.at[:, pl.ds(0, 2)], side_ref.at[:, pl.ds(0, 2)], side_sem, 3, behind, height_of),
    ]
    for copy in sides:
        copy.start()

    row_1.two()
    pl.when(lowest)(row_0.two)
    row_2.two()
    row_1.three()
    pl.when(lowest)(row_0.three)
    row_2.three()
    for copy in sides:
        copy.wait_recv()
    back = transposed([factor(lower, upper)])
    beyond = []
    for ref, depth, kept in (
        (taps_ahead, ahead, lane % slices < 2),
        (taps_behind, behind, lane % slices >= last),
    ):
        pair = weights(ref, depth)
        beyond.append(factor(*[jnp.where(kept, part, 0.0) for part in pair]))
    beyond = transposed(beyond)
    offset_ahead, offset_behind = offset_of(ahead), offset_of(behind)
    row_1.four()
    pl.when(lowest)(row_0.four)
    row_2.four()
    row_1.five()

    zero_tile = jnp.zeros((angles, LANES), jnp.float32)

    def image_of(ref):
        columns_of = [
            jnp.concatenate([ref[2 * tile], ref[2 * tile + 1]], axis=0) for tile in range(tiles)
        ]
        return jnp.concatenate(columns_of + [zero_tile], axis=1)

    def gathered(update, layer):
        whole = None
        for tap in range(taps):
            start = layer * first + tap * slices
            term = update[start : start + slices]
            if tap:
                term = roll_left(term, tap)
            whole = term if whole is None else whole + term
        return relax_step * whole[:, :columns]

    def backproject(images, layers):
        high, low = zip(*[split_bf16(shift_rows(image, offset)) for image in images])
        update = dot(back, jnp.concatenate([*high, *low] * 2, axis=0))
        shifted = [shift_rows(image, move) for move in (offset_ahead, offset_behind) for image in images]
        high, low = zip(*[split_bf16(image) for image in shifted])
        outer = dot(beyond, jnp.concatenate([*high, *low] * 2, axis=0))
        return [gathered(update, i) for i in layers], [gathered(outer, i) for i in layers]

    side_row = lax.broadcasted_iota(jnp.int32, (slices, columns), 0)
    outside = (side_row < 2) | (side_row >= last)

    def packed(one, two):
        two = jnp.where(side_row < 4, pltpu.roll(two, 2, 0), pltpu.roll(two, slices - 2, 0))
        return jnp.where(outside, one, two)

    def unpacked(value):
        two = jnp.where(side_row < 4, pltpu.roll(value, slices - 2, 0), pltpu.roll(value, 2, 0))
        return value, two

    row_2.five()
    main, side = backproject([image_of(res_1), image_of(res_0)], range(3))
    volume_side = jnp.where(outside, side_ref[...], 0.0)
    layer_0, layer_1 = vol_ref[0] + main[0], vol_ref[1] + main[1]
    side_0, side_1 = volume_side[0] + side[0], volume_side[1] + side[1]
    up_ref[0] = main[2]
    up_ref[1] = layer_1
    up_ref[2] = packed(side[2], side_1)
    down_ref[0] = layer_0
    down_ref[1] = layer_1
    down_ref[2] = packed(side_0, side_1)
    up_copy = remote(up_ref, low_ref, edge_sem, 0, depth_of, above)
    down_copy = remote(down_ref, high_ref, edge_sem, 1, depth_of, below)

    @pl.when(has_above)
    def _():
        up_copy.start()

    @pl.when(has_below)
    def _():
        down_copy.start()

    @pl.when(lowest)
    def _():
        row_0.five()
        image = image_of(res_2)
        low_main, low_side = backproject([jnp.zeros_like(image), image], (2,))
        low_ref[0] = low_main[0]
        low_ref[1] = jnp.zeros((slices, columns), jnp.float32)
        low_ref[2] = packed(low_side[0], jnp.zeros((slices, columns), jnp.float32))

    @pl.when(has_below)
    def _():
        up_copy.wait_recv()

    @pl.when(has_above)
    def _():
        down_copy.wait_recv()

    @pl.when(jnp.logical_not(has_above))
    def _():
        high_ref[...] = jnp.zeros_like(high_ref)

    def joined(inner, outer):
        return jnp.concatenate([inner, outer], axis=0)

    from_low, under = unpacked(low_ref[2])
    over, over_2 = unpacked(high_ref[2])
    fields = [
        joined(low_ref[1], under),
        joined(layer_0 + low_ref[0], side_0 + from_low),
        joined(layer_1, side_1),
        joined(high_ref[0] + main[2], over + side[2]),
        joined(high_ref[1], over_2),
    ]
    place = lax.broadcasted_iota(jnp.int32, fields[0].shape, 0)
    place = depth_of * slices + jnp.where(place < slices + 4, place, place - 2 * slices)
    layers_total, depth_total = 2 * heights, slices * depths
    fields = total_variation(fields, 2 * height_of - 1, layers_total, place, depth_total)

    up2_ref[...] = fields[1][:slices]
    up2_edge[...] = fields[1][slices : slices + 1]
    up_copies = [
        remote(up2_ref, low2_ref, edge_sem, 2, depth_of, above),
        remote(up2_edge, low2_edge, edge_sem, 3, depth_of, above),
    ]

    @pl.when(has_above)
    def _():
        for copy in up_copies:
            copy.start()

    @pl.when(has_below)
    def _():
        for copy in up_copies:
            copy.wait_recv()

    @pl.when(lowest)
    def _():
        low2_ref[...] = jnp.zeros_like(low2_ref)
        low2_edge[...] = jnp.zeros_like(low2_edge)

    edge = jnp.broadcast_to(low2_edge[...], (slices, columns))
    fields = [joined(low2_ref[...], edge), *fields]
    fields = total_variation(fields, 2 * height_of - 1, layers_total, place, depth_total)
    out_ref[0] = fields[0][:slices]
    out_ref[1] = fields[1][:slices]

    row_1.settle()
    row_2.settle()
    pl.when(lowest)(row_0.settle)
    for copy in sides:
        copy.wait_send()

    @pl.when(has_below)
    def _():
        for copy in halos:
            copy.wait_send()
        down_copy.wait_send()

    @pl.when(has_above)
    def _():
        up_copy.wait_send()
        for copy in up_copies:
            copy.wait_send()


def per_device(volume, measured, taps, band_offset, angle_index):
    heights = lax.axis_size("height")
    depths = lax.axis_size("depth")
    f32 = jnp.float32
    layers, slices, columns = volume.shape
    far = depths // NEAR
    taps = jnp.swapaxes(taps, 1, 2)
    tile = (SUBLANES, LANES)
    main = (slices, columns)
    edge = (1, columns)
    vmem = pltpu.VMEM
    far_first = [
        vmem((depths, *tile), f32), vmem((far, NEAR, *tile), f32), vmem((NEAR, *tile), f32),
        vmem((NEAR, *tile), f32), vmem((depths, *tile), f32),
    ]
    near_first = [
        vmem((depths, *tile), f32), vmem((NEAR, far, *tile), f32), vmem((far, *tile), f32),
        vmem((far, *tile), f32), vmem((depths, *tile), f32),
    ]
    scratch = [
        vmem(volume.shape, f32), vmem(measured.shape, f32), vmem(taps.shape, f32),
        vmem(band_offset.shape, jnp.int32), pltpu.SMEM(angle_index.shape, jnp.int32),
        vmem(main, f32), vmem(measured.shape, f32), vmem(volume.shape, f32),
        vmem(taps.shape, f32), vmem(taps.shape, f32),
        *far_first, *near_first, *far_first,
        vmem((3, *main), f32), vmem((3, *main), f32), vmem((3, *main), f32), vmem((3, *main), f32),
        vmem(main, f32), vmem(main, f32), vmem(edge, f32), vmem(edge, f32),
        pltpu.SemaphoreType.DMA((5,)),
        pltpu.SemaphoreType.DMA((4,)),
        pltpu.SemaphoreType.DMA((8,)),
        pltpu.SemaphoreType.DMA((24,)),
        pltpu.SemaphoreType.DMA((8,)),
    ]
    return pl.pallas_call(
        functools.partial(kernel, heights, depths),
        out_shape=jax.ShapeDtypeStruct(volume.shape, f32),
        in_specs=[pl.BlockSpec(memory_space=pl.ANY)] * 5,
        out_specs=pl.BlockSpec(memory_space=pltpu.VMEM),
        scratch_shapes=scratch,
        compiler_params=pltpu.CompilerParams(
            collective_id=0, has_side_effects=True, vmem_limit_bytes=60 * 1024 * 1024
        ),
    )(volume, measured, taps, band_offset, angle_index)


def solution(mesh):
    in_specs = (
        P("height", "depth", None),
        P(None, "height", "depth"),
        P(None, None, "depth"),
        P(),
        P(),
    )
    out_specs = P("height", "depth", None)
    return jax.shard_map(
        per_device, mesh=mesh, in_specs=in_specs, out_specs=out_specs, check_vma=False
    )
```

```python
import functools
import math

import jax
import jax.numpy as jnp
from jax import lax
from jax.experimental import pallas as pl
from jax.experimental.pallas import tpu as pltpu
from jax.sharding import PartitionSpec as P

TAPS = 4
OFFMAX = 64
N_VIEWS = 720
LANES = 128
SUBLANES = 8
NEAR = 4

relax_step = 0.5
tv_step = 0.08
tv_eps = 0.1

MESH = pl.DeviceIdType.MESH


def split_bf16(value):
    high = value.astype(jnp.bfloat16)
    low = (value - high.astype(jnp.float32)).astype(jnp.bfloat16)
    return high, low


def roll_left(value, amount):
    return pltpu.roll(value, value.shape[1] - amount, 1)


def shift_rows(value, amount):
    move = amount + OFFMAX
    top = move // OFFMAX
    moved_left = roll_left(value, OFFMAX)
    moved_right = pltpu.roll(value, OFFMAX, 1)
    value = jnp.where(top == 0, moved_right, jnp.where(top == 1, value, moved_left))
    for bit in range(6):
        stride = 1 << bit
        value = jnp.where((move // stride) % 2 == 1, roll_left(value, stride), value)
    return value


def total_variation(fields, first_layer, height_total, depth_place, depth_total):
    rows, columns = fields[0].shape
    lane = lax.broadcasted_iota(jnp.int32, (rows, columns), 1)
    inner = lane < columns - 1
    open_row = (depth_place >= 0) & (depth_place + 1 < depth_total)
    results = []
    under = None
    for i in range(len(fields) - 1):
        here = fields[i]
        layer = first_layer + i
        up = fields[i + 1] - here
        up = jnp.where((layer >= 0) & (layer + 1 < height_total), up, 0.0)
        deep = jnp.where(open_row, pltpu.roll(here, rows - 1, 0) - here, 0.0)
        wide = jnp.where(inner, roll_left(here, 1) - here, 0.0)
        scale = lax.rsqrt(tv_eps * tv_eps + up * up + deep * deep + wide * wide)
        up = up * scale
        if i:
            deep = deep * scale
            wide = wide * scale
            diverge = (up - under) + (deep - pltpu.roll(deep, 1, 0)) + (wide - pltpu.roll(wide, 1, 1))
            results.append(here + tv_step * diverge)
        under = up
    return results


def kernel(
    heights, depths,
    vol_hbm, meas_hbm, taps_hbm, off_hbm, angle_hbm,
    out_ref,
    vol_ref, meas_ref, taps_ref, off_ref, angle_ref,
    halo_ref, band_ref, band_up, side_ref, taps_ahead, taps_behind,
    part_1, got_1a, sum_1, got_1b, res_1,
    part_2, got_2a, sum_2, got_2b, res_2,
    part_0, got_0a, sum_0, got_0b, res_0,
    up_ref, low_ref, down_ref, high_ref,
    up2_ref, low2_ref,
    load_sem, halo_sem, side_sem, ring_sem, edge_sem,
):
    height_of = lax.axis_index("height")
    depth_of = lax.axis_index("depth")
    above, below = height_of + 1, height_of - 1
    has_above, has_below = height_of < heights - 1, height_of > 0
    ahead = lax.rem(depth_of + 1, depths)
    behind = lax.rem(depth_of + depths - 1, depths)
    far_of, near_of = depth_of // NEAR, depth_of % NEAR
    far_count = depths // NEAR
    _, slices, columns = vol_ref.shape
    tiles = columns // LANES
    angles = off_ref.shape[0]
    taps = taps_ref.shape[0]

    barrier = pltpu.get_barrier_semaphore()

    def greet(depth, height):
        pl.semaphore_signal(barrier, inc=1, device_id=(depth, height), device_id_type=MESH)

    def fars():
        order = sorted(range(1, far_count), key=lambda i: -min(i, far_count - i))
        return [lax.rem(far_of + i, far_count) for i in order]

    def nears():
        return [lax.rem(near_of + i, NEAR) for i in range(1, NEAR)]

    @pl.when(has_below)
    def _():
        greet(depth_of, below)

    @pl.when(has_above)
    def _():
        greet(depth_of, above)

    for far in fars():
        greet(far * NEAR + near_of, height_of)
    for near in nears():
        greet(far_of * NEAR + near, height_of)
    for depth in (ahead, behind):
        greet(depth, height_of)

    loads = [
        pltpu.make_async_copy(src, dst, load_sem.at[i])
        for i, (src, dst) in enumerate(
            (
                (vol_hbm, vol_ref), (angle_hbm, angle_ref), (taps_hbm, taps_ref),
                (off_hbm, off_ref), (meas_hbm, meas_ref),
            )
        )
    ]
    for load in loads:
        load.start()
    partners = far_count + NEAR + has_above.astype(jnp.int32) + has_below.astype(jnp.int32)
    pl.semaphore_wait(barrier, partners)

    def remote(src, dst, sems, number, depth, height):
        return pltpu.make_async_remote_copy(
            src_ref=src, dst_ref=dst,
            send_sem=sems.at[2 * number], recv_sem=sems.at[2 * number + 1],
            device_id=(depth, height), device_id_type=MESH,
        )

    halos = [
        remote(vol_hbm.at[0], halo_ref, halo_sem, 0, depth_of, below),
        remote(band_ref, band_up, halo_sem, 1, depth_of, below),
    ]
    pl.when(has_below)(halos[0].start)
    for load in loads[1:]:
        load.wait()
    band_pad = jnp.zeros((angles, LANES - meas_ref.shape[2]), jnp.float32)

    def band_of(r):
        band = jnp.concatenate([meas_ref[:, r, :], band_pad], axis=1)
        return jnp.where(depth_of % 2 == 1, pltpu.roll(band, LANES // 2, 1), band)

    band_ref[...] = band_of(0)
    pl.when(has_below)(halos[1].start)

    row = lax.broadcasted_iota(jnp.int32, (angles, LANES), 0)
    lane = lax.broadcasted_iota(jnp.int32, (angles, LANES), 1)
    view = jnp.zeros((angles, LANES), jnp.float32)
    for i in range(angles):
        view = jnp.where(row == i, angle_ref[i].astype(jnp.float32), view)
    swing = 0.45 * jnp.sin(2.0 * math.pi / N_VIEWS * view)
    first = taps * slices

    def weights(ref, depth):
        weight = jnp.concatenate([ref[tap] for tap in range(taps)], axis=0)
        weight = jnp.concatenate([weight, jnp.zeros((first, LANES - angles), jnp.float32)], axis=1)
        weight = jnp.concatenate([weight, jnp.zeros((LANES - first, LANES), jnp.float32)], axis=0)
        weight = weight.T[:angles]
        depth_place = (depth * slices + lane % slices).astype(jnp.float32) + 0.5
        rise = 0.5 + swing * jnp.cos(math.pi / (slices * depths) * depth_place)
        return weight * (1.0 - rise), weight * rise

    def offset_of(depth):
        off_lane = lax.broadcasted_iota(jnp.int32, off_ref.shape, 1)
        offset = jnp.where(off_lane == depth, off_ref[...].astype(jnp.float32), 0.0)
        return jnp.sum(offset, axis=1, keepdims=True).astype(jnp.int32)

    def factor(lower, upper):
        return jnp.concatenate(
            [
                upper + pltpu.roll(lower, first, 1),
                pltpu.roll(upper, first, 1) + pltpu.roll(lower, 2 * first, 1),
            ],
            axis=0,
        )

    def transposed(parts):
        whole = jnp.concatenate(parts * 4, axis=0)
        turned = whole.T
        high = turned.astype(jnp.bfloat16).astype(jnp.float32)
        place = lax.broadcasted_iota(jnp.int32, turned.shape, 1)
        return jnp.where(place < turned.shape[1] // 2, high, turned - high).astype(jnp.bfloat16)[: 3 * first]

    lower, upper = weights(taps_ref, depth_of)
    offset = offset_of(depth_of)
    own = jnp.concatenate(
        [upper + pltpu.roll(lower, first, 1), pltpu.roll(upper, first, 1), lower], axis=0
    )
    own = jnp.concatenate(split_bf16(own + pltpu.roll(own, 2 * first, 1)), axis=0)
    from_halo = (lower + pltpu.roll(lower, first, 1))[:, : 2 * first]
    from_halo = jnp.concatenate(split_bf16(from_halo), axis=0)
    zeros = jnp.zeros((slices, LANES), jnp.float32)

    def spread(layers):
        wide = [jnp.concatenate([layer, zeros], axis=1) for layer in layers]
        rows = []
        for layer in wide:
            for tap in range(taps):
                rows.append(layer if tap == 0 else pltpu.roll(layer, tap, 1))
        high, low = split_bf16(jnp.concatenate(rows, axis=0))
        return jnp.concatenate([high, low], axis=0)

    def dot(a, b):
        return jnp.dot(a, b, preferred_element_type=jnp.float32)

    halves = angles // SUBLANES

    def publish(image, band, ref):
        image = shift_rows(image, -offset)
        for tile in range(tiles):
            for half in range(halves):
                ref[tile * halves + half] = -image[
                    half * SUBLANES : (half + 1) * SUBLANES, tile * LANES : (tile + 1) * LANES
                ]
        for half in range(halves):
            place = depth_of // 2 * halves + half
            ref[place] = ref[place] + band[half * SUBLANES : (half + 1) * SUBLANES]

    def to_far(src, dst, number):
        for far in fars():
            remote(src(far), dst, ring_sem, number, far * NEAR + near_of, height_of).start()

    def to_near(src, dst, number):
        for near in nears():
            remote(src(near), dst, ring_sem, number, far_of * NEAR + near, height_of).start()

    def wait_for(ref, count, number, received):
        some = ref.at[pl.ds(0, count)]
        pltpu.make_async_copy(some, some, ring_sem.at[2 * number + int(received)]).wait()

    def total(parts):
        while len(parts) > 1:
            parts = [a + b for a, b in zip(parts[::2], parts[1::2])]
        return parts[0]

    class NearFirst:
        def __init__(self, number, part, got_a, summed, got_b, res):
            self.number, self.part, self.got_a = number, part, got_a
            self.summed, self.got_b, self.res = summed, got_b, res

        def one(self):
            size = far_count
            to_near(lambda near: self.part.at[pl.ds(near * size, size)], self.got_a.at[near_of], self.number)
            self.got_a[near_of] = self.part[pl.ds(near_of * size, size)]

        def two(self):
            wait_for(self.got_a, NEAR - 1, self.number, True)
            self.summed[...] = total([self.got_a[i] for i in range(NEAR)])
            to_far(lambda far: self.summed.at[far], self.got_b.at[far_of], self.number + 1)
            self.got_b[far_of] = self.summed[far_of]

        def three(self):
            wait_for(self.got_b, far_count - 1, self.number + 1, True)
            place = near_of * far_count + far_of
            self.res[place] = total([self.got_b[i] for i in range(far_count)])
            mine = self.res.at[place]
            to_far(lambda far: mine, mine, self.number + 2)

        def four(self):
            wait_for(self.res, far_count - 1, self.number + 2, True)
            block = self.res.at[pl.ds(near_of * far_count, far_count)]
            to_near(lambda near: block, block, self.number + 3)

        def five(self):
            wait_for(self.res, depths - far_count, self.number + 3, True)

        def settle(self):
            wait_for(self.part, depths - far_count, self.number, False)
            wait_for(self.summed, far_count - 1, self.number + 1, False)
            wait_for(self.res, far_count - 1, self.number + 2, False)
            wait_for(self.res, depths - far_count, self.number + 3, False)

    class FarFirst:
        def __init__(self, number, part, got_a, summed, got_b, res):
            self.number, self.part, self.got_a = number, part, got_a
            self.summed, self.got_b, self.res = summed, got_b, res

        def one(self):
            to_far(lambda far: self.part.at[pl.ds(far * NEAR, NEAR)], self.got_a.at[far_of], self.number)
            self.got_a[far_of] = self.part[pl.ds(far_of * NEAR, NEAR)]

        def two(self):
            wait_for(self.got_a, far_count - 1, self.number, True)
            self.summed[...] = total([self.got_a[i] for i in range(far_count)])
            to_near(lambda near: self.summed, self.got_b.at[near_of], self.number + 1)
            self.got_b[near_of] = self.summed[...]

        def three(self):
            wait_for(self.got_b, NEAR - 1, self.number + 1, True)
            place = pl.ds(far_of * NEAR, NEAR)
            self.res[place] = total([self.got_b[i] for i in range(NEAR)])
            block = self.res.at[place]
            to_far(lambda far: block, block, self.number + 2)

        def five(self):
            wait_for(self.res, depths - NEAR, self.number + 2, True)

        def settle(self):
            wait_for(self.part, depths - NEAR, self.number, False)
            wait_for(self.got_b, NEAR - 1, self.number + 1, False)
            wait_for(self.res, depths - NEAR, self.number + 2, False)

    row_1 = NearFirst(0, part_1, got_1a, sum_1, got_1b, res_1)
    row_2 = FarFirst(4, part_2, got_2a, sum_2, got_2b, res_2)
    row_0 = FarFirst(7, part_0, got_0a, sum_0, got_0b, res_0)
    late = height_of == heights // 2 - 1
    lowest = jnp.logical_not(has_below)

    loads[0].wait()
    count = 3 * angles
    both = dot(own, spread([vol_ref[0], vol_ref[1]]))
    both = both[:count] + both[count:]
    publish(both[:angles], band_of(1), part_1)
    row_1.one()

    @pl.when(lowest)
    def _():
        publish(both[2 * angles :], band_ref[...], part_0)
        row_0.one()

    pl.when(late)(row_1.two)

    @pl.when(has_above)
    def _():
        for copy in halos:
            copy.wait_recv()
        spilled = dot(from_halo, spread([halo_ref[...]]))
        image = both[angles : 2 * angles] + (spilled[:angles] + spilled[angles:])
        publish(image, band_up[...], part_2)

    @pl.when(jnp.logical_not(has_above))
    def _():
        part_2[...] = jnp.zeros_like(part_2)

    row_2.one()

    last = slices - 2
    sides = [
        remote(taps_hbm, taps_behind, side_sem, 0, ahead, height_of),
        remote(taps_hbm, taps_ahead, side_sem, 1, behind, height_of),
        remote(
            vol_ref.at[:, pl.ds(last, 2)], side_ref.at[:, pl.ds(last, 2)], side_sem, 2, ahead, height_of
        ),
        remote(vol_ref.at[:, pl.ds(0, 2)], side_ref.at[:, pl.ds(0, 2)], side_sem, 3, behind, height_of),
    ]
    for copy in sides:
        copy.start()

    pl.when(jnp.logical_not(late))(row_1.two)
    pl.when(lowest)(row_0.two)
    row_2.two()
    for copy in sides:
        copy.wait_recv()
    back = transposed([factor(lower, upper)])
    beyond = []
    for ref, depth, kept in (
        (taps_ahead, ahead, lane % slices < 2),
        (taps_behind, behind, lane % slices >= last),
    ):
        pair = weights(ref, depth)
        beyond.append(factor(*[jnp.where(kept, part, 0.0) for part in pair]))
    beyond = transposed(beyond)
    offset_ahead, offset_behind = offset_of(ahead), offset_of(behind)
    row_1.three()
    pl.when(lowest)(row_0.three)
    row_2.three()
    row_1.four()
    row_1.five()

    zero_tile = jnp.zeros((angles, LANES), jnp.float32)

    def image_of(ref):
        columns_of = [
            jnp.concatenate([ref[2 * tile], ref[2 * tile + 1]], axis=0) for tile in range(tiles)
        ]
        return jnp.concatenate(columns_of + [zero_tile], axis=1)

    def gathered(update, layer):
        whole = None
        for tap in range(taps):
            start = layer * first + tap * slices
            term = update[start : start + slices]
            if tap:
                term = roll_left(term, tap)
            whole = term if whole is None else whole + term
        return relax_step * whole[:, :columns]

    def prepared(image):
        moves = (offset, offset_ahead, offset_behind)
        return [split_bf16(shift_rows(image, move)) for move in moves]

    def backproject(one, two, layers):
        def stacked(moves):
            pairs = [image[move] for move in moves for image in (one, two)]
            return jnp.concatenate([part for side in zip(*pairs) for part in side] * 2, axis=0)

        update = dot(back, stacked((0,)))
        outer = dot(beyond, stacked((1, 2)))
        return [gathered(update, i) for i in layers], [gathered(outer, i) for i in layers]

    side_row = lax.broadcasted_iota(jnp.int32, (slices, columns), 0)
    outside = (side_row < 2) | (side_row >= last)

    def packed(one, two):
        two = jnp.where(side_row < 4, pltpu.roll(two, 2, 0), pltpu.roll(two, slices - 2, 0))
        return jnp.where(outside, one, two)

    def unpacked(value):
        two = jnp.where(side_row < 4, pltpu.roll(value, slices - 2, 0), pltpu.roll(value, 2, 0))
        return value, two

    image_1 = prepared(image_of(res_1))
    row_2.five()
    main, side = backproject(image_1, prepared(image_of(res_2)), range(3))
    volume_side = jnp.where(outside, side_ref[...], 0.0)
    layer_0, layer_1 = vol_ref[0] + main[0], vol_ref[1] + main[1]
    side_0, side_1 = volume_side[0] + side[0], volume_side[1] + side[1]
    up_ref[0] = main[2]
    up_ref[1] = layer_1
    up_ref[2] = packed(side[2], side_1)
    down_ref[0] = layer_0
    down_ref[1] = layer_1
    down_ref[2] = packed(side_0, side_1)
    up_copy = remote(up_ref, low_ref, edge_sem, 0, depth_of, above)
    down_copy = remote(down_ref, high_ref, edge_sem, 1, depth_of, below)

    @pl.when(has_above)
    def _():
        up_copy.start()

    @pl.when(has_below)
    def _():
        down_copy.start()

    @pl.when(lowest)
    def _():
        row_0.five()
        image = prepared(image_of(res_0))
        nothing = [[jnp.zeros_like(part) for part in pair] for pair in image]
        low_main, low_side = backproject(nothing, image, (2,))
        low_ref[0] = low_main[0]
        low_ref[1] = jnp.zeros((slices, columns), jnp.float32)
        low_ref[2] = packed(low_side[0], jnp.zeros((slices, columns), jnp.float32))

    pl.when(has_below)(up_copy.wait_recv)
    from_low, under = unpacked(low_ref[2])
    layer_0 = layer_0 + low_ref[0]
    side_0 = side_0 + from_low
    up2_ref[0] = layer_0
    up2_ref[1] = side_0
    up_copies = [
        remote(up2_ref.at[0], low2_ref.at[0], edge_sem, 2, depth_of, above),
        remote(
            up2_ref.at[1, pl.ds(0, 2)], low2_ref.at[1, pl.ds(0, 2)], edge_sem, 3, depth_of, above
        ),
    ]

    @pl.when(has_above)
    def _():
        for copy in up_copies:
            copy.start()
        down_copy.wait_recv()

    @pl.when(jnp.logical_not(has_above))
    def _():
        high_ref[...] = jnp.zeros_like(high_ref)

    @pl.when(has_below)
    def _():
        for copy in up_copies:
            copy.wait_recv()

    @pl.when(lowest)
    def _():
        low2_ref[...] = jnp.zeros_like(low2_ref)

    def joined(inner, outer):
        return jnp.concatenate([inner, outer], axis=0)

    over, over_2 = unpacked(high_ref[2])
    fields = [
        joined(low2_ref[0], jnp.where(side_row < 2, low2_ref[1], 0.0)),
        joined(low_ref[1], under),
        joined(layer_0, side_0),
        joined(layer_1, side_1),
        joined(high_ref[0] + main[2], over + side[2]),
        joined(high_ref[1], over_2),
    ]
    place = lax.broadcasted_iota(jnp.int32, fields[0].shape, 0)
    place = depth_of * slices + jnp.where(place < slices + 4, place, place - 2 * slices)
    layers_total, depth_total = 2 * heights, slices * depths
    fields = total_variation(fields, 2 * height_of - 2, layers_total, place, depth_total)
    fields = total_variation(fields, 2 * height_of - 1, layers_total, place, depth_total)
    out_ref[0] = fields[0][:slices]
    out_ref[1] = fields[1][:slices]

    row_1.settle()
    row_2.settle()
    pl.when(lowest)(row_0.settle)
    for copy in sides:
        copy.wait_send()

    @pl.when(has_below)
    def _():
        for copy in halos:
            copy.wait_send()
        down_copy.wait_send()

    @pl.when(has_above)
    def _():
        up_copy.wait_send()
        for copy in up_copies:
            copy.wait_send()


def per_device(volume, measured, taps, band_offset, angle_index):
    heights = lax.axis_size("height")
    depths = lax.axis_size("depth")
    f32 = jnp.float32
    layers, slices, columns = volume.shape
    far = depths // NEAR
    taps = jnp.swapaxes(taps, 1, 2)
    tile = (SUBLANES, LANES)
    main = (slices, columns)
    vmem = pltpu.VMEM
    far_first = [
        vmem((depths, *tile), f32), vmem((far, NEAR, *tile), f32), vmem((NEAR, *tile), f32),
        vmem((NEAR, NEAR, *tile), f32), vmem((depths, *tile), f32),
    ]
    near_first = [
        vmem((depths, *tile), f32), vmem((NEAR, far, *tile), f32), vmem((far, *tile), f32),
        vmem((far, *tile), f32), vmem((depths, *tile), f32),
    ]
    scratch = [
        vmem(volume.shape, f32), vmem(measured.shape, f32), vmem(taps.shape, f32),
        vmem(band_offset.shape, jnp.int32), pltpu.SMEM(angle_index.shape, jnp.int32),
        vmem(main, f32), *[vmem((measured.shape[0], LANES), f32)] * 2, vmem(volume.shape, f32),
        vmem(taps.shape, f32), vmem(taps.shape, f32),
        *near_first, *far_first, *far_first,
        vmem((3, *main), f32), vmem((3, *main), f32), vmem((3, *main), f32), vmem((3, *main), f32),
        vmem((2, *main), f32), vmem((2, *main), f32),
        pltpu.SemaphoreType.DMA((5,)),
        pltpu.SemaphoreType.DMA((4,)),
        pltpu.SemaphoreType.DMA((8,)),
        pltpu.SemaphoreType.DMA((24,)),
        pltpu.SemaphoreType.DMA((8,)),
    ]
    return pl.pallas_call(
        functools.partial(kernel, heights, depths),
        out_shape=jax.ShapeDtypeStruct(volume.shape, f32),
        in_specs=[pl.BlockSpec(memory_space=pl.ANY)] * 5,
        out_specs=pl.BlockSpec(memory_space=pltpu.VMEM),
        scratch_shapes=scratch,
        compiler_params=pltpu.CompilerParams(
            collective_id=0, has_side_effects=True, vmem_limit_bytes=60 * 1024 * 1024
        ),
    )(volume, measured, taps, band_offset, angle_index)


def solution(mesh):
    in_specs = (
        P("height", "depth", None),
        P(None, "height", "depth"),
        P(None, None, "depth"),
        P(),
        P(),
    )
    out_specs = P("height", "depth", None)
    return jax.shard_map(
        per_device, mesh=mesh, in_specs=in_specs, out_specs=out_specs, check_vma=False
    )
```

```python
import functools
import math

import jax
import jax.numpy as jnp
from jax import lax
from jax.experimental import pallas as pl
from jax.experimental.pallas import tpu as pltpu
from jax.sharding import PartitionSpec as P

TAPS = 4
OFFMAX = 64
N_VIEWS = 720
LANES = 128
SUBLANES = 8
NEAR = 4

relax_step = 0.5
tv_step = 0.08
tv_eps = 0.1

MESH = pl.DeviceIdType.MESH


def split_bf16(value):
    high = value.astype(jnp.bfloat16)
    low = (value - high.astype(jnp.float32)).astype(jnp.bfloat16)
    return high, low


def roll_left(value, amount):
    return pltpu.roll(value, value.shape[1] - amount, 1)


def shift_rows(value, amount):
    move = amount + OFFMAX
    top = move // OFFMAX
    moved_left = roll_left(value, OFFMAX)
    moved_right = pltpu.roll(value, OFFMAX, 1)
    value = jnp.where(top == 0, moved_right, jnp.where(top == 1, value, moved_left))
    for bit in range(6):
        stride = 1 << bit
        value = jnp.where((move // stride) % 2 == 1, roll_left(value, stride), value)
    return value


def total_variation(fields, first_layer, height_total, depth_place, depth_total):
    rows, columns = fields[0].shape
    lane = lax.broadcasted_iota(jnp.int32, (rows, columns), 1)
    inner = lane < columns - 1
    open_row = (depth_place >= 0) & (depth_place + 1 < depth_total)
    results = []
    under = None
    for i in range(len(fields) - 1):
        here = fields[i]
        layer = first_layer + i
        up = fields[i + 1] - here
        up = jnp.where((layer >= 0) & (layer + 1 < height_total), up, 0.0)
        deep = jnp.where(open_row, pltpu.roll(here, rows - 1, 0) - here, 0.0)
        wide = jnp.where(inner, roll_left(here, 1) - here, 0.0)
        scale = lax.rsqrt(tv_eps * tv_eps + up * up + deep * deep + wide * wide)
        up = up * scale
        if i:
            deep = deep * scale
            wide = wide * scale
            diverge = (up - under) + (deep - pltpu.roll(deep, 1, 0)) + (wide - pltpu.roll(wide, 1, 1))
            results.append(here + tv_step * diverge)
        under = up
    return results


def kernel(
    heights, depths,
    vol_hbm, meas_hbm, taps_hbm, off_hbm, angle_hbm,
    out_ref,
    vol_ref, meas_ref, taps_ref, off_ref, angle_ref,
    halo_ref, band_ref, band_up, side_ref, taps_ahead, taps_behind,
    part_1, got_1, res_1,
    part_2, got_2a, sum_2, got_2b, res_2,
    part_0, got_0a, sum_0, got_0b, res_0,
    up_ref, low_ref, down_ref, high_ref,
    up2_ref, low2_ref,
    load_sem, halo_sem, side_sem, ring_sem, edge_sem,
):
    height_of = lax.axis_index("height")
    depth_of = lax.axis_index("depth")
    above, below = height_of + 1, height_of - 1
    has_above, has_below = height_of < heights - 1, height_of > 0
    ahead = lax.rem(depth_of + 1, depths)
    behind = lax.rem(depth_of + depths - 1, depths)
    far_of, near_of = depth_of // NEAR, depth_of % NEAR
    far_count = depths // NEAR
    _, slices, columns = vol_ref.shape
    tiles = columns // LANES
    angles = off_ref.shape[0]
    taps = taps_ref.shape[0]

    barrier = pltpu.get_barrier_semaphore()

    def greet(depth, height):
        pl.semaphore_signal(barrier, inc=1, device_id=(depth, height), device_id_type=MESH)

    def fars():
        order = sorted(range(1, far_count), key=lambda i: -min(i, far_count - i))
        return [lax.rem(far_of + i, far_count) for i in order]

    def nears():
        return [lax.rem(near_of + i, NEAR) for i in range(1, NEAR)]

    def everyone():
        order = [(i, j) for i in range(far_count) for j in range(NEAR) if i or j]
        order.sort(key=lambda ij: -min(ij[0], far_count - ij[0]) - min(ij[1], NEAR - ij[1]))
        return [
            lax.rem(far_of + i, far_count) * NEAR + lax.rem(near_of + j, NEAR) for i, j in order
        ]

    @pl.when(has_below)
    def _():
        greet(depth_of, below)

    @pl.when(has_above)
    def _():
        greet(depth_of, above)

    for depth in everyone():
        greet(depth, height_of)

    loads = [
        pltpu.make_async_copy(src, dst, load_sem.at[i])
        for i, (src, dst) in enumerate(
            (
                (vol_hbm, vol_ref), (angle_hbm, angle_ref), (taps_hbm, taps_ref),
                (off_hbm, off_ref), (meas_hbm, meas_ref),
            )
        )
    ]
    for load in loads:
        load.start()
    def remote(src, dst, sems, number, depth, height):
        return pltpu.make_async_remote_copy(
            src_ref=src, dst_ref=dst,
            send_sem=sems.at[2 * number], recv_sem=sems.at[2 * number + 1],
            device_id=(depth, height), device_id_type=MESH,
        )

    for load in loads:
        load.wait()
    band_pad = jnp.zeros((angles, LANES - meas_ref.shape[2]), jnp.float32)

    def band_of(r):
        band = jnp.concatenate([meas_ref[:, r, :], band_pad], axis=1)
        return jnp.where(depth_of % 2 == 1, pltpu.roll(band, LANES // 2, 1), band)

    band_ref[...] = band_of(0)

    row = lax.broadcasted_iota(jnp.int32, (angles, LANES), 0)
    lane = lax.broadcasted_iota(jnp.int32, (angles, LANES), 1)
    view = jnp.zeros((angles, LANES), jnp.float32)
    for i in range(angles):
        view = jnp.where(row == i, angle_ref[i].astype(jnp.float32), view)
    swing = 0.45 * jnp.sin(2.0 * math.pi / N_VIEWS * view)
    first = taps * slices

    def weights(ref, depth):
        weight = jnp.concatenate([ref[tap] for tap in range(taps)], axis=0)
        weight = jnp.concatenate([weight, jnp.zeros((first, LANES - angles), jnp.float32)], axis=1)
        weight = jnp.concatenate([weight, jnp.zeros((LANES - first, LANES), jnp.float32)], axis=0)
        weight = weight.T[:angles]
        depth_place = (depth * slices + lane % slices).astype(jnp.float32) + 0.5
        rise = 0.5 + swing * jnp.cos(math.pi / (slices * depths) * depth_place)
        return weight * (1.0 - rise), weight * rise

    def offset_of(depth):
        off_lane = lax.broadcasted_iota(jnp.int32, off_ref.shape, 1)
        offset = jnp.where(off_lane == depth, off_ref[...].astype(jnp.float32), 0.0)
        return jnp.sum(offset, axis=1, keepdims=True).astype(jnp.int32)

    def factor(lower, upper):
        return jnp.concatenate(
            [
                upper + pltpu.roll(lower, first, 1),
                pltpu.roll(upper, first, 1) + pltpu.roll(lower, 2 * first, 1),
            ],
            axis=0,
        )

    def transposed(parts):
        whole = jnp.concatenate(parts * 4, axis=0)
        turned = whole.T
        high = turned.astype(jnp.bfloat16).astype(jnp.float32)
        place = lax.broadcasted_iota(jnp.int32, turned.shape, 1)
        return jnp.where(place < turned.shape[1] // 2, high, turned - high).astype(jnp.bfloat16)[: 3 * first]

    lower, upper = weights(taps_ref, depth_of)
    offset = offset_of(depth_of)
    own = jnp.concatenate(
        [upper + pltpu.roll(lower, first, 1), pltpu.roll(upper, first, 1), lower], axis=0
    )
    own = jnp.concatenate(split_bf16(own + pltpu.roll(own, 2 * first, 1)), axis=0)
    from_halo = (lower + pltpu.roll(lower, first, 1))[:, : 2 * first]
    from_halo = jnp.concatenate(split_bf16(from_halo), axis=0)
    zeros = jnp.zeros((slices, LANES), jnp.float32)

    def spread(layers):
        wide = [jnp.concatenate([layer, zeros], axis=1) for layer in layers]
        rows = []
        for layer in wide:
            for tap in range(taps):
                rows.append(layer if tap == 0 else pltpu.roll(layer, tap, 1))
        high, low = split_bf16(jnp.concatenate(rows, axis=0))
        return jnp.concatenate([high, low], axis=0)

    def dot(a, b):
        return jnp.dot(a, b, preferred_element_type=jnp.float32)

    halves = angles // SUBLANES

    def publish(image, ref):
        image = shift_rows(image, -offset)
        for tile in range(tiles):
            for half in range(halves):
                ref[tile * halves + half] = -image[
                    half * SUBLANES : (half + 1) * SUBLANES, tile * LANES : (tile + 1) * LANES
                ]

    def measure(band, ref):
        for half in range(halves):
            place = depth_of // 2 * halves + half
            ref[place] = ref[place] + band[half * SUBLANES : (half + 1) * SUBLANES]

    def to_far(src, dst, number):
        for far in fars():
            remote(src(far), dst, ring_sem, number, far * NEAR + near_of, height_of).start()

    def to_near(src, dst, number):
        for near in nears():
            remote(src(near), dst, ring_sem, number, far_of * NEAR + near, height_of).start()

    def wait_for(ref, count, number, received):
        some = ref.at[pl.ds(0, count)]
        pltpu.make_async_copy(some, some, ring_sem.at[2 * number + int(received)]).wait()

    def total(parts):
        while len(parts) > 1:
            parts = [a + b for a, b in zip(parts[::2], parts[1::2])]
        return parts[0]

    class Direct:
        def __init__(self, number, part, got, res):
            self.number, self.part, self.got, self.res = number, part, got, res

        def one(self):
            for peer in everyone():
                remote(
                    self.part.at[peer], self.got.at[depth_of], ring_sem, self.number, peer, height_of
                ).start()
            self.got[depth_of] = self.part[depth_of]

        def two(self):
            wait_for(self.got, depths - 1, self.number, True)
            self.res[depth_of] = total([self.got[i] for i in range(depths)])
            mine = self.res.at[depth_of]
            for peer in everyone():
                remote(mine, mine, ring_sem, self.number + 1, peer, height_of).start()

        def five(self):
            wait_for(self.res, depths - 1, self.number + 1, True)

        def settle(self):
            wait_for(self.part, depths - 1, self.number, False)
            wait_for(self.res, depths - 1, self.number + 1, False)

    class FarFirst:
        def __init__(self, number, part, got_a, summed, got_b, res):
            self.number, self.part, self.got_a = number, part, got_a
            self.summed, self.got_b, self.res = summed, got_b, res

        def one(self):
            to_far(lambda far: self.part.at[pl.ds(far * NEAR, NEAR)], self.got_a.at[far_of], self.number)
            self.got_a[far_of] = self.part[pl.ds(far_of * NEAR, NEAR)]

        def two(self):
            wait_for(self.got_a, far_count - 1, self.number, True)
            self.summed[...] = total([self.got_a[i] for i in range(far_count)])
            to_near(lambda near: self.summed, self.got_b.at[near_of], self.number + 1)
            self.got_b[near_of] = self.summed[...]

        def three(self):
            wait_for(self.got_b, NEAR - 1, self.number + 1, True)
            place = pl.ds(far_of * NEAR, NEAR)
            self.res[place] = total([self.got_b[i] for i in range(NEAR)])
            block = self.res.at[place]
            to_far(lambda far: block, block, self.number + 2)

        def five(self):
            wait_for(self.res, depths - NEAR, self.number + 2, True)

        def settle(self):
            wait_for(self.part, depths - NEAR, self.number, False)
            wait_for(self.got_b, NEAR - 1, self.number + 1, False)
            wait_for(self.res, depths - NEAR, self.number + 2, False)

    row_1 = Direct(0, part_1, got_1, res_1)
    row_2 = FarFirst(4, part_2, got_2a, sum_2, got_2b, res_2)
    row_0 = FarFirst(7, part_0, got_0a, sum_0, got_0b, res_0)
    late = has_below & (height_of == heights // 2 - 1)
    soon = jnp.logical_not(late)
    lowest = jnp.logical_not(has_below)

    count = 3 * angles
    both = dot(own, spread([vol_ref[0], vol_ref[1]]))
    both = both[:count] + both[count:]
    publish(both[:angles], part_1)
    measure(band_of(1), part_1)

    @pl.when(lowest)
    def _():
        publish(both[2 * angles :], part_0)
        measure(band_ref[...], part_0)

    partners = depths - 1 + has_above.astype(jnp.int32) + has_below.astype(jnp.int32)
    pl.semaphore_wait(barrier, partners)

    halos = [
        remote(vol_hbm.at[0], halo_ref, halo_sem, 0, depth_of, below),
        remote(band_ref, band_up, halo_sem, 1, depth_of, below),
    ]

    @pl.when(has_below)
    def _():
        for copy in halos:
            copy.start()

    row_1.one()
    pl.when(lowest)(row_0.one)
    pl.when(late)(row_1.two)

    @pl.when(has_above)
    def _():
        halos[0].wait_recv()
        spilled = dot(from_halo, spread([halo_ref[...]]))
        image = both[angles : 2 * angles] + (spilled[:angles] + spilled[angles:])
        publish(image, part_2)
        halos[1].wait_recv()
        measure(band_up[...], part_2)

    @pl.when(jnp.logical_not(has_above))
    def _():
        part_2[...] = jnp.zeros_like(part_2)

    row_2.one()

    last = slices - 2
    sides = [
        remote(taps_hbm, taps_behind, side_sem, 0, ahead, height_of),
        remote(taps_hbm, taps_ahead, side_sem, 1, behind, height_of),
        remote(
            vol_ref.at[:, pl.ds(last, 2)], side_ref.at[:, pl.ds(last, 2)], side_sem, 2, ahead, height_of
        ),
        remote(vol_ref.at[:, pl.ds(0, 2)], side_ref.at[:, pl.ds(0, 2)], side_sem, 3, behind, height_of),
    ]
    for copy in sides:
        copy.start()

    pl.when(soon)(row_1.two)
    pl.when(lowest)(row_0.two)
    row_2.two()
    for copy in sides:
        copy.wait_recv()
    back = transposed([factor(lower, upper)])
    beyond = []
    for ref, depth, kept in (
        (taps_ahead, ahead, lane % slices < 2),
        (taps_behind, behind, lane % slices >= last),
    ):
        pair = weights(ref, depth)
        beyond.append(factor(*[jnp.where(kept, part, 0.0) for part in pair]))
    beyond = transposed(beyond)
    offset_ahead, offset_behind = offset_of(ahead), offset_of(behind)
    pl.when(lowest)(row_0.three)
    row_2.three()
    row_1.five()

    zero_tile = jnp.zeros((angles, LANES), jnp.float32)

    def image_of(ref):
        columns_of = [
            jnp.concatenate([ref[2 * tile], ref[2 * tile + 1]], axis=0) for tile in range(tiles)
        ]
        return jnp.concatenate(columns_of + [zero_tile], axis=1)

    def gathered(update, layer):
        whole = None
        for tap in range(taps):
            start = layer * first + tap * slices
            term = update[start : start + slices]
            if tap:
                term = roll_left(term, tap)
            whole = term if whole is None else whole + term
        return relax_step * whole[:, :columns]

    def prepared(image, moves):
        return [split_bf16(shift_rows(image, move)) for move in moves]

    def stacked(pairs):
        return jnp.concatenate([part for side in zip(*pairs) for part in side] * 2, axis=0)

    around = (offset_ahead, offset_behind)

    side_row = lax.broadcasted_iota(jnp.int32, (slices, columns), 0)
    outside = (side_row < 2) | (side_row >= last)

    def packed(one, two):
        two = jnp.where(side_row < 4, pltpu.roll(two, 2, 0), pltpu.roll(two, slices - 2, 0))
        return jnp.where(outside, one, two)

    def unpacked(value):
        two = jnp.where(side_row < 4, pltpu.roll(value, slices - 2, 0), pltpu.roll(value, 2, 0))
        return value, two

    def mixed(one, two):
        return stacked([one[0], two[0], one[1], two[1]])

    def pieces(src, dst, places, number, height):
        return [
            remote(src.at[place], dst.at[place], edge_sem, number + i, depth_of, height)
            for i, place in enumerate(places)
        ]

    whole_1 = image_of(res_1)
    own_1, around_1 = prepared(whole_1, (offset,)), prepared(whole_1, around)
    zero = jnp.zeros_like(whole_1).astype(jnp.bfloat16)
    nothing = [(zero, zero)] * 2
    volume_side = jnp.where(outside, side_ref[...], 0.0)
    update = dot(back[:first], stacked([own_1[0], nothing[0]]))
    layer_0 = vol_ref[0] + gathered(update, 0)
    update = dot(beyond[:first], mixed(around_1, nothing))
    side_0 = volume_side[0] + gathered(update, 0)
    down_ref[0] = layer_0
    down_ref[1] = side_0
    edges = (pl.ds(0, 2), pl.ds(last, 2))
    down_copies = pieces(
        down_ref, high_ref, (0, (1, edges[0]), (1, edges[1]), 2, (3, edges[1])), 2, below
    )
    up_copies = pieces(up_ref, low_ref, (pl.ds(0, 2), 2), 0, above)
    next_copies = pieces(up2_ref, low2_ref, (0, (1, edges[0])), 7, above)

    @pl.when(has_below)
    def _():
        for copy in down_copies[:3]:
            copy.start()

    def completed():
        @pl.when(has_below)
        def _():
            for copy in up_copies:
                copy.wait_recv()

        up2_ref[0] = layer_0 + low_ref[0]
        up2_ref[1] = side_0 + unpacked(low_ref[2])[0]

        @pl.when(has_above)
        def _():
            for copy in next_copies:
                copy.start()

    pl.when(late)(completed)
    row_2.five()
    whole_2 = image_of(res_2)
    update = dot(back[first:], stacked(own_1 + prepared(whole_2, (offset,))))
    layer_1, part_2h2 = vol_ref[1] + gathered(update, 0), gathered(update, 1)
    up_ref[0] = part_2h2
    up_ref[1] = layer_1
    down_ref[2] = layer_1
    pl.when(has_above)(up_copies[0].start)
    pl.when(has_below)(down_copies[3].start)
    update = dot(beyond[first:], mixed(around_1, prepared(whole_2, around)))
    side_1, side_2h2 = volume_side[1] + gathered(update, 0), gathered(update, 1)
    up_ref[2] = packed(side_2h2, side_1)
    down_ref[3] = side_1
    pl.when(has_above)(up_copies[1].start)
    pl.when(has_below)(down_copies[4].start)

    @pl.when(lowest)
    def _():
        row_0.five()
        image = prepared(image_of(res_0), (offset, *around))
        update = dot(back, stacked([nothing[0], image[0]]))
        low_ref[0] = gathered(update, 2)
        low_ref[1] = jnp.zeros((slices, columns), jnp.float32)
        update = dot(beyond, mixed(nothing, image[1:]))
        low_ref[2] = packed(gathered(update, 2), jnp.zeros((slices, columns), jnp.float32))

    pl.when(soon)(completed)

    @pl.when(has_above)
    def _():
        for copy in down_copies:
            copy.wait_recv()

    @pl.when(jnp.logical_not(has_above))
    def _():
        high_ref[...] = jnp.zeros_like(high_ref)

    @pl.when(has_below)
    def _():
        for copy in next_copies:
            copy.wait_recv()

    @pl.when(lowest)
    def _():
        low2_ref[...] = jnp.zeros_like(low2_ref)

    def joined(inner, outer):
        return jnp.concatenate([inner, outer], axis=0)

    fields = [
        joined(low2_ref[0], jnp.where(side_row < 2, low2_ref[1], 0.0)),
        joined(low_ref[1], unpacked(low_ref[2])[1]),
        joined(up2_ref[0], up2_ref[1]),
        joined(layer_1, side_1),
        joined(high_ref[0] + part_2h2, jnp.where(outside, high_ref[1], 0.0) + side_2h2),
        joined(high_ref[2], jnp.where(side_row >= last, high_ref[3], 0.0)),
    ]
    place = lax.broadcasted_iota(jnp.int32, fields[0].shape, 0)
    place = depth_of * slices + jnp.where(place < slices + 4, place, place - 2 * slices)
    layers_total, depth_total = 2 * heights, slices * depths
    fields = total_variation(fields, 2 * height_of - 2, layers_total, place, depth_total)
    fields = total_variation(fields, 2 * height_of - 1, layers_total, place, depth_total)
    out_ref[0] = fields[0][:slices]
    out_ref[1] = fields[1][:slices]

    row_1.settle()
    row_2.settle()
    pl.when(lowest)(row_0.settle)
    for copy in sides:
        copy.wait_send()

    @pl.when(has_below)
    def _():
        for copy in (*halos, *down_copies):
            copy.wait_send()

    @pl.when(has_above)
    def _():
        for copy in (*up_copies, *next_copies):
            copy.wait_send()


def per_device(volume, measured, taps, band_offset, angle_index):
    heights = lax.axis_size("height")
    depths = lax.axis_size("depth")
    f32 = jnp.float32
    layers, slices, columns = volume.shape
    far = depths // NEAR
    taps = jnp.swapaxes(taps, 1, 2)
    tile = (SUBLANES, LANES)
    main = (slices, columns)
    vmem = pltpu.VMEM
    far_first = [
        vmem((depths, *tile), f32), vmem((far, NEAR, *tile), f32), vmem((NEAR, *tile), f32),
        vmem((NEAR, NEAR, *tile), f32), vmem((depths, *tile), f32),
    ]
    scratch = [
        vmem(volume.shape, f32), vmem(measured.shape, f32), vmem(taps.shape, f32),
        vmem(band_offset.shape, jnp.int32), pltpu.SMEM(angle_index.shape, jnp.int32),
        vmem(main, f32), *[vmem((measured.shape[0], LANES), f32)] * 2, vmem(volume.shape, f32),
        vmem(taps.shape, f32), vmem(taps.shape, f32),
        *[vmem((depths, *tile), f32)] * 3, *far_first, *far_first,
        vmem((3, *main), f32), vmem((3, *main), f32), vmem((4, *main), f32), vmem((4, *main), f32),
        vmem((2, *main), f32), vmem((2, *main), f32),
        pltpu.SemaphoreType.DMA((5,)),
        pltpu.SemaphoreType.DMA((4,)),
        pltpu.SemaphoreType.DMA((8,)),
        pltpu.SemaphoreType.DMA((20,)),
        pltpu.SemaphoreType.DMA((18,)),
    ]
    return pl.pallas_call(
        functools.partial(kernel, heights, depths),
        out_shape=jax.ShapeDtypeStruct(volume.shape, f32),
        in_specs=[pl.BlockSpec(memory_space=pl.ANY)] * 5,
        out_specs=pl.BlockSpec(memory_space=pltpu.VMEM),
        scratch_shapes=scratch,
        compiler_params=pltpu.CompilerParams(
            collective_id=0, has_side_effects=True, vmem_limit_bytes=60 * 1024 * 1024
        ),
    )(volume, measured, taps, band_offset, angle_index)


def solution(mesh):
    in_specs = (
        P("height", "depth", None),
        P(None, "height", "depth"),
        P(None, None, "depth"),
        P(),
        P(),
    )
    out_specs = P("height", "depth", None)
    return jax.shard_map(
        per_device, mesh=mesh, in_specs=in_specs, out_specs=out_specs, check_vma=False
    )
```

```python
import functools
import math

import jax
import jax.numpy as jnp
from jax import lax
from jax.experimental import pallas as pl
from jax.experimental.pallas import tpu as pltpu
from jax.sharding import PartitionSpec as P

TAPS = 4
OFFMAX = 64
N_VIEWS = 720
LANES = 128
SUBLANES = 8
NEAR = 4

relax_step = 0.5
tv_step = 0.08
tv_eps = 0.1

MESH = pl.DeviceIdType.MESH


def split_bf16(value):
    high = value.astype(jnp.bfloat16)
    low = (value - high.astype(jnp.float32)).astype(jnp.bfloat16)
    return high, low


def roll_left(value, amount):
    return pltpu.roll(value, value.shape[1] - amount, 1)


def shift_rows(value, amount):
    move = amount + OFFMAX
    top = move // OFFMAX
    moved_left = roll_left(value, OFFMAX)
    moved_right = pltpu.roll(value, OFFMAX, 1)
    value = jnp.where(top == 0, moved_right, jnp.where(top == 1, value, moved_left))
    for bit in range(6):
        stride = 1 << bit
        value = jnp.where((move // stride) % 2 == 1, roll_left(value, stride), value)
    return value


def directions(here, over, layer, height_total, depth_place, depth_total):
    rows, columns = here.shape
    inner = lax.broadcasted_iota(jnp.int32, (rows, columns), 1) < columns - 1
    open_row = (depth_place >= 0) & (depth_place + 1 < depth_total)
    up = jnp.where((layer >= 0) & (layer + 1 < height_total), over - here, 0.0)
    deep = jnp.where(open_row, pltpu.roll(here, rows - 1, 0) - here, 0.0)
    wide = jnp.where(inner, roll_left(here, 1) - here, 0.0)
    scale = lax.rsqrt(tv_eps * tv_eps + up * up + deep * deep + wide * wide)
    return up * scale, deep * scale, wide * scale


def denoised(here, normal, under):
    up, deep, wide = normal
    diverge = (up - under) + (deep - pltpu.roll(deep, 1, 0)) + (wide - pltpu.roll(wide, 1, 1))
    return here + tv_step * diverge


def kernel(
    heights, depths,
    vol_hbm, meas_hbm, taps_hbm, off_hbm, angle_hbm,
    out_ref,
    vol_ref, meas_ref, taps_ref, off_ref, angle_ref,
    halo_ref, band_ref, band_up, side_ref, taps_ahead, taps_behind,
    part_1, got_1, res_1,
    part_2, got_2a, sum_2, got_2b, res_2,
    part_0, got_0a, sum_0, got_0b, res_0,
    up_ref, low_ref, down_ref, high_ref,
    up2_ref, low2_ref,
    load_sem, halo_sem, side_sem, ring_sem, edge_sem,
):
    height_of = lax.axis_index("height")
    depth_of = lax.axis_index("depth")
    above, below = height_of + 1, height_of - 1
    has_above, has_below = height_of < heights - 1, height_of > 0
    ahead = lax.rem(depth_of + 1, depths)
    behind = lax.rem(depth_of + depths - 1, depths)
    far_of, near_of = depth_of // NEAR, depth_of % NEAR
    far_count = depths // NEAR
    _, slices, columns = vol_ref.shape
    tiles = columns // LANES
    angles = off_ref.shape[0]
    taps = taps_ref.shape[0]

    barrier = pltpu.get_barrier_semaphore()

    def greet(depth, height):
        pl.semaphore_signal(barrier, inc=1, device_id=(depth, height), device_id_type=MESH)

    def fars():
        order = sorted(range(1, far_count), key=lambda i: -min(i, far_count - i))
        return [lax.rem(far_of + i, far_count) for i in order]

    def nears():
        return [lax.rem(near_of + i, NEAR) for i in range(1, NEAR)]

    def everyone():
        order = [(i, j) for i in range(far_count) for j in range(NEAR) if i or j]
        order.sort(key=lambda ij: -min(ij[0], far_count - ij[0]) - min(ij[1], NEAR - ij[1]))
        return [
            lax.rem(far_of + i, far_count) * NEAR + lax.rem(near_of + j, NEAR) for i, j in order
        ]

    @pl.when(has_below)
    def _():
        greet(depth_of, below)

    @pl.when(has_above)
    def _():
        greet(depth_of, above)

    for depth in everyone():
        greet(depth, height_of)

    loads = [
        pltpu.make_async_copy(src, dst, load_sem.at[i])
        for i, (src, dst) in enumerate(
            (
                (vol_hbm, vol_ref), (angle_hbm, angle_ref), (taps_hbm, taps_ref),
                (off_hbm, off_ref), (meas_hbm, meas_ref),
            )
        )
    ]
    for load in loads:
        load.start()
    def remote(src, dst, sems, number, depth, height):
        return pltpu.make_async_remote_copy(
            src_ref=src, dst_ref=dst,
            send_sem=sems.at[2 * number], recv_sem=sems.at[2 * number + 1],
            device_id=(depth, height), device_id_type=MESH,
        )

    for load in loads:
        load.wait()
    band_pad = jnp.zeros((angles, LANES - meas_ref.shape[2]), jnp.float32)

    def band_of(r):
        band = jnp.concatenate([meas_ref[:, r, :], band_pad], axis=1)
        return jnp.where(depth_of % 2 == 1, pltpu.roll(band, LANES // 2, 1), band)

    band_ref[...] = band_of(0)

    row = lax.broadcasted_iota(jnp.int32, (angles, LANES), 0)
    lane = lax.broadcasted_iota(jnp.int32, (angles, LANES), 1)
    view = jnp.zeros((angles, LANES), jnp.float32)
    for i in range(angles):
        view = jnp.where(row == i, angle_ref[i].astype(jnp.float32), view)
    swing = 0.45 * jnp.sin(2.0 * math.pi / N_VIEWS * view)
    first = taps * slices

    def weights(ref, depth):
        weight = jnp.concatenate([ref[tap] for tap in range(taps)], axis=0)
        weight = jnp.concatenate([weight, jnp.zeros((first, LANES - angles), jnp.float32)], axis=1)
        weight = jnp.concatenate([weight, jnp.zeros((LANES - first, LANES), jnp.float32)], axis=0)
        weight = weight.T[:angles]
        depth_place = (depth * slices + lane % slices).astype(jnp.float32) + 0.5
        rise = 0.5 + swing * jnp.cos(math.pi / (slices * depths) * depth_place)
        return weight * (1.0 - rise), weight * rise

    def offset_of(depth):
        off_lane = lax.broadcasted_iota(jnp.int32, off_ref.shape, 1)
        offset = jnp.where(off_lane == depth, off_ref[...].astype(jnp.float32), 0.0)
        return jnp.sum(offset, axis=1, keepdims=True).astype(jnp.int32)

    def factor(lower, upper):
        return jnp.concatenate(
            [
                upper + pltpu.roll(lower, first, 1),
                pltpu.roll(upper, first, 1) + pltpu.roll(lower, 2 * first, 1),
            ],
            axis=0,
        )

    def transposed(parts):
        whole = jnp.concatenate(parts * 4, axis=0)
        turned = whole.T
        high = turned.astype(jnp.bfloat16).astype(jnp.float32)
        place = lax.broadcasted_iota(jnp.int32, turned.shape, 1)
        return jnp.where(place < turned.shape[1] // 2, high, turned - high).astype(jnp.bfloat16)[: 3 * first]

    lower, upper = weights(taps_ref, depth_of)
    offset = offset_of(depth_of)
    own = jnp.concatenate(
        [upper + pltpu.roll(lower, first, 1), pltpu.roll(upper, first, 1), lower], axis=0
    )
    own = jnp.concatenate(split_bf16(own + pltpu.roll(own, 2 * first, 1)), axis=0)
    from_halo = (lower + pltpu.roll(lower, first, 1))[:, : 2 * first]
    from_halo = jnp.concatenate(split_bf16(from_halo), axis=0)
    zeros = jnp.zeros((slices, LANES), jnp.float32)

    def spread(layers):
        wide = [jnp.concatenate([layer, zeros], axis=1) for layer in layers]
        rows = []
        for layer in wide:
            for tap in range(taps):
                rows.append(layer if tap == 0 else pltpu.roll(layer, tap, 1))
        high, low = split_bf16(jnp.concatenate(rows, axis=0))
        return jnp.concatenate([high, low], axis=0)

    def dot(a, b):
        return jnp.dot(a, b, preferred_element_type=jnp.float32)

    halves = angles // SUBLANES

    def publish(image, ref):
        image = shift_rows(image, -offset)
        for tile in range(tiles):
            for half in range(halves):
                ref[tile * halves + half] = -image[
                    half * SUBLANES : (half + 1) * SUBLANES, tile * LANES : (tile + 1) * LANES
                ]

    def measure(band, ref):
        for half in range(halves):
            place = depth_of // 2 * halves + half
            ref[place] = ref[place] + band[half * SUBLANES : (half + 1) * SUBLANES]

    def to_far(src, dst, number):
        for far in fars():
            remote(src(far), dst, ring_sem, number, far * NEAR + near_of, height_of).start()

    def to_near(src, dst, number):
        for near in nears():
            remote(src(near), dst, ring_sem, number, far_of * NEAR + near, height_of).start()

    def wait_for(ref, count, number, received):
        some = ref.at[pl.ds(0, count)]
        pltpu.make_async_copy(some, some, ring_sem.at[2 * number + int(received)]).wait()

    def total(parts):
        while len(parts) > 1:
            parts = [a + b for a, b in zip(parts[::2], parts[1::2])]
        return parts[0]

    class Direct:
        def __init__(self, number, part, got, res):
            self.number, self.part, self.got, self.res = number, part, got, res

        def one(self):
            for peer in everyone():
                remote(
                    self.part.at[peer], self.got.at[depth_of], ring_sem, self.number, peer, height_of
                ).start()
            self.got[depth_of] = self.part[depth_of]

        def two(self):
            wait_for(self.got, depths - 1, self.number, True)
            self.res[depth_of] = total([self.got[i] for i in range(depths)])
            mine = self.res.at[depth_of]
            for peer in everyone():
                remote(mine, mine, ring_sem, self.number + 1, peer, height_of).start()

        def five(self):
            wait_for(self.res, depths - 1, self.number + 1, True)

        def settle(self):
            wait_for(self.part, depths - 1, self.number, False)
            wait_for(self.res, depths - 1, self.number + 1, False)

    class FarFirst:
        def __init__(self, number, part, got_a, summed, got_b, res):
            self.number, self.part, self.got_a = number, part, got_a
            self.summed, self.got_b, self.res = summed, got_b, res

        def one(self):
            to_far(lambda far: self.part.at[pl.ds(far * NEAR, NEAR)], self.got_a.at[far_of], self.number)
            self.got_a[far_of] = self.part[pl.ds(far_of * NEAR, NEAR)]

        def two(self):
            wait_for(self.got_a, far_count - 1, self.number, True)
            self.summed[...] = total([self.got_a[i] for i in range(far_count)])
            to_near(lambda near: self.summed, self.got_b.at[near_of], self.number + 1)
            self.got_b[near_of] = self.summed[...]

        def three(self):
            wait_for(self.got_b, NEAR - 1, self.number + 1, True)
            place = pl.ds(far_of * NEAR, NEAR)
            self.res[place] = total([self.got_b[i] for i in range(NEAR)])
            block = self.res.at[place]
            to_far(lambda far: block, block, self.number + 2)

        def five(self):
            wait_for(self.res, depths - NEAR, self.number + 2, True)

        def settle(self):
            wait_for(self.part, depths - NEAR, self.number, False)
            wait_for(self.got_b, NEAR - 1, self.number + 1, False)
            wait_for(self.res, depths - NEAR, self.number + 2, False)

    row_1 = Direct(0, part_1, got_1, res_1)
    row_2 = FarFirst(4, part_2, got_2a, sum_2, got_2b, res_2)
    row_0 = FarFirst(7, part_0, got_0a, sum_0, got_0b, res_0)
    late = has_below & (height_of == heights // 2 - 1)
    soon = jnp.logical_not(late)
    lowest = jnp.logical_not(has_below)

    count = 3 * angles
    both = dot(own, spread([vol_ref[0], vol_ref[1]]))
    both = both[:count] + both[count:]
    publish(both[:angles], part_1)
    measure(band_of(1), part_1)

    @pl.when(lowest)
    def _():
        publish(both[2 * angles :], part_0)
        measure(band_ref[...], part_0)

    partners = depths - 1 + has_above.astype(jnp.int32) + has_below.astype(jnp.int32)
    pl.semaphore_wait(barrier, partners)

    halos = [
        remote(vol_hbm.at[0], halo_ref, halo_sem, 0, depth_of, below),
        remote(band_ref, band_up, halo_sem, 1, depth_of, below),
    ]

    @pl.when(has_below)
    def _():
        for copy in halos:
            copy.start()

    row_1.one()
    pl.when(lowest)(row_0.one)
    pl.when(late)(row_1.two)

    @pl.when(has_above)
    def _():
        halos[0].wait_recv()
        spilled = dot(from_halo, spread([halo_ref[...]]))
        image = both[angles : 2 * angles] + (spilled[:angles] + spilled[angles:])
        publish(image, part_2)
        halos[1].wait_recv()
        measure(band_up[...], part_2)

    @pl.when(jnp.logical_not(has_above))
    def _():
        part_2[...] = jnp.zeros_like(part_2)

    row_2.one()

    last = slices - 2
    sides = [
        remote(taps_hbm, taps_behind, side_sem, 0, ahead, height_of),
        remote(taps_hbm, taps_ahead, side_sem, 1, behind, height_of),
        remote(
            vol_ref.at[:, pl.ds(last, 2)], side_ref.at[:, pl.ds(last, 2)], side_sem, 2, ahead, height_of
        ),
        remote(vol_ref.at[:, pl.ds(0, 2)], side_ref.at[:, pl.ds(0, 2)], side_sem, 3, behind, height_of),
    ]
    for copy in sides:
        copy.start()

    pl.when(soon)(row_1.two)
    pl.when(lowest)(row_0.two)
    row_2.two()
    for copy in sides:
        copy.wait_recv()
    back = transposed([factor(lower, upper)])
    beyond = []
    for ref, depth, kept in (
        (taps_ahead, ahead, lane % slices < 2),
        (taps_behind, behind, lane % slices >= last),
    ):
        pair = weights(ref, depth)
        beyond.append(factor(*[jnp.where(kept, part, 0.0) for part in pair]))
    beyond = transposed(beyond)
    offset_ahead, offset_behind = offset_of(ahead), offset_of(behind)
    pl.when(lowest)(row_0.three)
    row_2.three()
    row_1.five()

    zero_tile = jnp.zeros((angles, LANES), jnp.float32)

    def image_of(ref):
        columns_of = [
            jnp.concatenate([ref[2 * tile], ref[2 * tile + 1]], axis=0) for tile in range(tiles)
        ]
        return jnp.concatenate(columns_of + [zero_tile], axis=1)

    def gathered(update, layer):
        whole = None
        for tap in range(taps):
            start = layer * first + tap * slices
            term = update[start : start + slices]
            if tap:
                term = roll_left(term, tap)
            whole = term if whole is None else whole + term
        return relax_step * whole[:, :columns]

    def prepared(image, moves):
        return [split_bf16(shift_rows(image, move)) for move in moves]

    def stacked(pairs):
        return jnp.concatenate([part for side in zip(*pairs) for part in side] * 2, axis=0)

    around = (offset_ahead, offset_behind)

    side_row = lax.broadcasted_iota(jnp.int32, (slices, columns), 0)
    outside = (side_row < 2) | (side_row >= last)

    def mixed(one, two):
        return stacked([one[0], two[0], one[1], two[1]])

    def pieces(src, dst, places, number, height):
        return [
            remote(src.at[place], dst.at[place], edge_sem, number + i, depth_of, height)
            for i, place in enumerate(places)
        ]

    whole_1 = image_of(res_1)
    own_1, around_1 = prepared(whole_1, (offset,)), prepared(whole_1, around)
    zero = jnp.zeros_like(whole_1).astype(jnp.bfloat16)
    nothing = [(zero, zero)] * 2
    volume_side = jnp.where(outside, side_ref[...], 0.0)
    update = dot(back[:first], stacked([own_1[0], nothing[0]]))
    layer_0 = vol_ref[0] + gathered(update, 0)
    update = dot(beyond[:first], mixed(around_1, nothing))
    side_0 = volume_side[0] + gathered(update, 0)
    down_ref[0] = layer_0
    down_ref[1] = side_0
    edges = (pl.ds(0, 2), pl.ds(last, 2))
    down_copies = pieces(
        down_ref, high_ref, (0, (1, edges[0]), (1, edges[1]), 2, (3, edges[1])), 2, below
    )
    up_copies = pieces(
        up_ref, low_ref, (0, (1, edges[0]), (1, edges[1]), 2, (3, edges[0]), (3, edges[1])), 7, above
    )
    next_copies = pieces(up2_ref, low2_ref, (0, (1, edges[0])), 13, above)

    @pl.when(has_below)
    def _():
        for copy in down_copies[:3]:
            copy.start()

    def completed():
        @pl.when(has_below)
        def _():
            for copy in up_copies[:3]:
                copy.wait_recv()

        up2_ref[0] = layer_0 + low_ref[0]
        up2_ref[1] = side_0 + jnp.where(outside, low_ref[1], 0.0)

        @pl.when(has_above)
        def _():
            for copy in next_copies:
                copy.start()

    pl.when(late)(completed)
    row_2.five()
    whole_2 = image_of(res_2)
    update = dot(back[first:], stacked(own_1 + prepared(whole_2, (offset,))))
    layer_1, part_2h2 = vol_ref[1] + gathered(update, 0), gathered(update, 1)
    up_ref[0] = part_2h2
    up_ref[2] = layer_1
    down_ref[2] = layer_1
    pl.when(has_above)(up_copies[0].start)
    pl.when(has_below)(down_copies[3].start)
    update = dot(beyond[first:], mixed(around_1, prepared(whole_2, around)))
    side_1, side_2h2 = volume_side[1] + gathered(update, 0), gathered(update, 1)
    up_ref[1] = side_2h2
    up_ref[3] = side_1
    down_ref[3] = side_1

    @pl.when(has_above)
    def _():
        for copy in up_copies[1:]:
            copy.start()

    pl.when(has_below)(down_copies[4].start)

    @pl.when(lowest)
    def _():
        row_0.five()
        image = prepared(image_of(res_0), (offset, *around))
        update = dot(back, stacked([nothing[0], image[0]]))
        low_ref[0] = gathered(update, 2)
        update = dot(beyond, mixed(nothing, image[1:]))
        low_ref[1] = gathered(update, 2)
        low_ref[2] = jnp.zeros((slices, columns), jnp.float32)
        low_ref[3] = jnp.zeros((slices, columns), jnp.float32)
        low2_ref[...] = jnp.zeros_like(low2_ref)

    @pl.when(jnp.logical_not(has_above))
    def _():
        high_ref[...] = jnp.zeros_like(high_ref)

    def arrive(condition, copies):
        @pl.when(condition)
        def _():
            for copy in copies:
                copy.wait_recv()

    def layer_of(inner, outer, kept=outside):
        return jnp.concatenate([inner, jnp.where(kept, outer, 0.0)], axis=0)

    place = lax.broadcasted_iota(jnp.int32, (2 * slices, columns), 0)
    place = depth_of * slices + jnp.where(place < slices + 4, place, place - 2 * slices)

    def normal(here, over, layer):
        layer = 2 * height_of + layer
        return directions(here, over, layer, 2 * heights, place, slices * depths)

    arrive(has_above, down_copies[:3])
    at_1 = layer_of(layer_1, side_1)
    at_2 = layer_of(high_ref[0] + part_2h2, high_ref[1] + side_2h2)
    n_1 = normal(at_1, at_2, 1)
    pl.when(soon)(completed)
    at_0 = layer_of(up2_ref[0], up2_ref[1])
    n_0 = normal(at_0, at_1, 0)
    next_1 = denoised(at_1, n_1, n_0[0])
    arrive(has_below, up_copies[3:])
    below_1 = layer_of(low_ref[2], low_ref[3])
    m_1 = normal(below_1, at_0, -1)
    next_0 = denoised(at_0, n_0, m_1[0])
    then_0 = normal(next_0, next_1, 0)
    arrive(has_below, next_copies)
    below_2 = layer_of(low2_ref[0], low2_ref[1], side_row < 2)
    under_1 = denoised(below_1, m_1, normal(below_2, below_1, -2)[0])
    out_ref[0] = denoised(next_0, then_0, normal(under_1, next_0, -1)[0])[:slices]
    arrive(has_above, down_copies[3:])
    at_3 = layer_of(high_ref[2], high_ref[3], side_row >= last)
    next_2 = denoised(at_2, normal(at_2, at_3, 2), n_1[0])
    out_ref[1] = denoised(next_1, normal(next_1, next_2, 1), then_0[0])[:slices]

    row_1.settle()
    row_2.settle()
    pl.when(lowest)(row_0.settle)
    for copy in sides:
        copy.wait_send()

    @pl.when(has_below)
    def _():
        for copy in (*halos, *down_copies):
            copy.wait_send()

    @pl.when(has_above)
    def _():
        for copy in (*up_copies, *next_copies):
            copy.wait_send()


def per_device(volume, measured, taps, band_offset, angle_index):
    heights = lax.axis_size("height")
    depths = lax.axis_size("depth")
    f32 = jnp.float32
    layers, slices, columns = volume.shape
    far = depths // NEAR
    taps = jnp.swapaxes(taps, 1, 2)
    tile = (SUBLANES, LANES)
    main = (slices, columns)
    vmem = pltpu.VMEM
    far_first = [
        vmem((depths, *tile), f32), vmem((far, NEAR, *tile), f32), vmem((NEAR, *tile), f32),
        vmem((NEAR, NEAR, *tile), f32), vmem((depths, *tile), f32),
    ]
    scratch = [
        vmem(volume.shape, f32), vmem(measured.shape, f32), vmem(taps.shape, f32),
        vmem(band_offset.shape, jnp.int32), pltpu.SMEM(angle_index.shape, jnp.int32),
        vmem(main, f32), *[vmem((measured.shape[0], LANES), f32)] * 2, vmem(volume.shape, f32),
        vmem(taps.shape, f32), vmem(taps.shape, f32),
        *[vmem((depths, *tile), f32)] * 3, *far_first, *far_first,
        *[vmem((4, *main), f32)] * 4,
        vmem((2, *main), f32), vmem((2, *main), f32),
        pltpu.SemaphoreType.DMA((5,)),
        pltpu.SemaphoreType.DMA((4,)),
        pltpu.SemaphoreType.DMA((8,)),
        pltpu.SemaphoreType.DMA((20,)),
        pltpu.SemaphoreType.DMA((30,)),
    ]
    return pl.pallas_call(
        functools.partial(kernel, heights, depths),
        out_shape=jax.ShapeDtypeStruct(volume.shape, f32),
        in_specs=[pl.BlockSpec(memory_space=pl.ANY)] * 5,
        out_specs=pl.BlockSpec(memory_space=pltpu.VMEM),
        scratch_shapes=scratch,
        compiler_params=pltpu.CompilerParams(
            collective_id=0, has_side_effects=True, vmem_limit_bytes=60 * 1024 * 1024
        ),
    )(volume, measured, taps, band_offset, angle_index)


def solution(mesh):
    in_specs = (
        P("height", "depth", None),
        P(None, "height", "depth"),
        P(None, None, "depth"),
        P(),
        P(),
    )
    out_specs = P("height", "depth", None)
    return jax.shard_map(
        per_device, mesh=mesh, in_specs=in_specs, out_specs=out_specs, check_vma=False
    )
```

```python
import functools
import math

import jax
import jax.numpy as jnp
from jax import lax
from jax.experimental import pallas as pl
from jax.experimental.pallas import tpu as pltpu
from jax.sharding import PartitionSpec as P

TAPS = 4
OFFMAX = 64
N_VIEWS = 720
LANES = 128
SUBLANES = 8
NEAR = 4

relax_step = 0.5
tv_step = 0.08
tv_eps = 0.1

MESH = pl.DeviceIdType.MESH


def split_bf16(value):
    high = value.astype(jnp.bfloat16)
    low = (value - high.astype(jnp.float32)).astype(jnp.bfloat16)
    return high, low


def roll_left(value, amount):
    return pltpu.roll(value, value.shape[1] - amount, 1)


def shift_rows(value, amount):
    move = amount + OFFMAX
    top = move // OFFMAX
    moved_left = roll_left(value, OFFMAX)
    moved_right = pltpu.roll(value, OFFMAX, 1)
    value = jnp.where(top == 0, moved_right, jnp.where(top == 1, value, moved_left))
    for bit in range(6):
        stride = 1 << bit
        value = jnp.where((move // stride) % 2 == 1, roll_left(value, stride), value)
    return value


def directions(here, over, layer, height_total, depth_place, depth_total):
    rows, columns = here.shape
    inner = lax.broadcasted_iota(jnp.int32, (rows, columns), 1) < columns - 1
    open_row = (depth_place >= 0) & (depth_place + 1 < depth_total)
    up = jnp.where((layer >= 0) & (layer + 1 < height_total), over - here, 0.0)
    deep = jnp.where(open_row, pltpu.roll(here, rows - 1, 0) - here, 0.0)
    wide = jnp.where(inner, roll_left(here, 1) - here, 0.0)
    scale = lax.rsqrt(tv_eps * tv_eps + up * up + deep * deep + wide * wide)
    return up * scale, deep * scale, wide * scale


def denoised(here, normal, under):
    up, deep, wide = normal
    diverge = (up - under) + (deep - pltpu.roll(deep, 1, 0)) + (wide - pltpu.roll(wide, 1, 1))
    return here + tv_step * diverge


def kernel(
    heights, depths,
    vol_hbm, meas_hbm, taps_hbm, off_hbm, angle_hbm,
    out_ref,
    vol_ref, meas_ref, taps_ref, off_ref, angle_ref,
    halo_ref, band_ref, band_up, side_ref, taps_ahead, taps_behind,
    part_1, got_1, res_1,
    part_2, got_2a, sum_2, got_2b, res_2,
    part_0, got_0a, sum_0, got_0b, res_0,
    up_ref, low_ref, down_ref, high_ref,
    up2_ref, low2_ref, result,
    load_sem, halo_sem, side_sem, ring_sem, edge_sem,
):
    height_of = lax.axis_index("height")
    depth_of = lax.axis_index("depth")
    above, below = height_of + 1, height_of - 1
    has_above, has_below = height_of < heights - 1, height_of > 0
    ahead = lax.rem(depth_of + 1, depths)
    behind = lax.rem(depth_of + depths - 1, depths)
    far_of, near_of = depth_of // NEAR, depth_of % NEAR
    far_count = depths // NEAR
    _, slices, columns = vol_ref.shape
    tiles = columns // LANES
    angles = off_ref.shape[0]
    taps = taps_ref.shape[0]

    loads = [
        pltpu.make_async_copy(src, dst, load_sem.at[i])
        for i, (src, dst) in enumerate(
            (
                (vol_hbm, vol_ref), (angle_hbm, angle_ref), (taps_hbm, taps_ref),
                (off_hbm, off_ref), (meas_hbm, meas_ref),
            )
        )
    ]
    for load in loads:
        load.start()
    def remote(src, dst, sems, number, depth, height):
        return pltpu.make_async_remote_copy(
            src_ref=src, dst_ref=dst,
            send_sem=sems.at[2 * number], recv_sem=sems.at[2 * number + 1],
            device_id=(depth, height), device_id_type=MESH,
        )

    barrier = pltpu.get_barrier_semaphore()

    def greet(depth, height):
        pl.semaphore_signal(barrier, inc=1, device_id=(depth, height), device_id_type=MESH)

    def fars():
        order = sorted(range(1, far_count), key=lambda i: -min(i, far_count - i))
        return [lax.rem(far_of + i, far_count) for i in order]

    def nears():
        return [lax.rem(near_of + i, NEAR) for i in range(1, NEAR)]

    def everyone():
        order = [(i, j) for i in range(far_count) for j in range(NEAR) if i or j]
        order.sort(key=lambda ij: -min(ij[0], far_count - ij[0]) - min(ij[1], NEAR - ij[1]))
        return [
            lax.rem(far_of + i, far_count) * NEAR + lax.rem(near_of + j, NEAR) for i, j in order
        ]

    @pl.when(has_below)
    def _():
        greet(depth_of, below)

    @pl.when(has_above)
    def _():
        greet(depth_of, above)

    for depth in everyone():
        greet(depth, height_of)

    for load in loads[1:4]:
        load.wait()
    row = lax.broadcasted_iota(jnp.int32, (angles, LANES), 0)
    lane = lax.broadcasted_iota(jnp.int32, (angles, LANES), 1)
    view = jnp.zeros((angles, LANES), jnp.float32)
    for i in range(angles):
        view = jnp.where(row == i, angle_ref[i].astype(jnp.float32), view)
    swing = 0.45 * jnp.sin(2.0 * math.pi / N_VIEWS * view)
    first = taps * slices

    def weights(ref, depth):
        weight = jnp.concatenate([ref[tap] for tap in range(taps)], axis=0)
        weight = jnp.concatenate([weight, jnp.zeros((first, LANES - angles), jnp.float32)], axis=1)
        weight = jnp.concatenate([weight, jnp.zeros((LANES - first, LANES), jnp.float32)], axis=0)
        weight = weight.T[:angles]
        depth_place = (depth * slices + lane % slices).astype(jnp.float32) + 0.5
        rise = 0.5 + swing * jnp.cos(math.pi / (slices * depths) * depth_place)
        return weight * (1.0 - rise), weight * rise

    def offset_of(depth):
        off_lane = lax.broadcasted_iota(jnp.int32, off_ref.shape, 1)
        offset = jnp.where(off_lane == depth, off_ref[...].astype(jnp.float32), 0.0)
        return jnp.sum(offset, axis=1, keepdims=True).astype(jnp.int32)

    def factor(lower, upper):
        return jnp.concatenate(
            [
                upper + pltpu.roll(lower, first, 1),
                pltpu.roll(upper, first, 1) + pltpu.roll(lower, 2 * first, 1),
            ],
            axis=0,
        )

    def transposed(parts):
        whole = jnp.concatenate(parts * 4, axis=0)
        turned = whole.T
        high = turned.astype(jnp.bfloat16).astype(jnp.float32)
        place = lax.broadcasted_iota(jnp.int32, turned.shape, 1)
        return jnp.where(place < turned.shape[1] // 2, high, turned - high).astype(jnp.bfloat16)[: 3 * first]

    lower, upper = weights(taps_ref, depth_of)
    offset = offset_of(depth_of)
    own = jnp.concatenate(
        [upper + pltpu.roll(lower, first, 1), pltpu.roll(upper, first, 1), lower], axis=0
    )
    own = jnp.concatenate(split_bf16(own + pltpu.roll(own, 2 * first, 1)), axis=0)
    from_halo = (lower + pltpu.roll(lower, first, 1))[:, : 2 * first]
    from_halo = jnp.concatenate(split_bf16(from_halo), axis=0)
    zeros = jnp.zeros((slices, LANES), jnp.float32)

    def spread(layers):
        wide = [jnp.concatenate([layer, zeros], axis=1) for layer in layers]
        rows = []
        for layer in wide:
            for tap in range(taps):
                rows.append(layer if tap == 0 else pltpu.roll(layer, tap, 1))
        high, low = split_bf16(jnp.concatenate(rows, axis=0))
        return jnp.concatenate([high, low], axis=0)

    def dot(a, b):
        return jnp.dot(a, b, preferred_element_type=jnp.float32)

    halves = angles // SUBLANES

    def publish(image, ref):
        image = shift_rows(image, -offset)
        for tile in range(tiles):
            for half in range(halves):
                ref[tile * halves + half] = -image[
                    half * SUBLANES : (half + 1) * SUBLANES, tile * LANES : (tile + 1) * LANES
                ]

    def measure(band, ref):
        for half in range(halves):
            place = depth_of // 2 * halves + half
            ref[place] = ref[place] + band[half * SUBLANES : (half + 1) * SUBLANES]

    def to_far(src, dst, number):
        for far in fars():
            remote(src(far), dst, ring_sem, number, far * NEAR + near_of, height_of).start()

    def to_near(src, dst, number):
        for near in nears():
            remote(src(near), dst, ring_sem, number, far_of * NEAR + near, height_of).start()

    def wait_for(ref, count, number, received):
        some = ref.at[pl.ds(0, count)]
        pltpu.make_async_copy(some, some, ring_sem.at[2 * number + int(received)]).wait()

    def total(parts):
        while len(parts) > 1:
            parts = [a + b for a, b in zip(parts[::2], parts[1::2])]
        return parts[0]

    class Direct:
        def __init__(self, number, part, got, res):
            self.number, self.part, self.got, self.res = number, part, got, res

        def one(self):
            for peer in everyone():
                remote(
                    self.part.at[peer], self.got.at[depth_of], ring_sem, self.number, peer, height_of
                ).start()
            self.got[depth_of] = self.part[depth_of]

        def two(self):
            wait_for(self.got, depths - 1, self.number, True)
            self.res[depth_of] = total([self.got[i] for i in range(depths)])
            mine = self.res.at[depth_of]
            for peer in everyone():
                remote(mine, mine, ring_sem, self.number + 1, peer, height_of).start()

        def five(self):
            wait_for(self.res, depths - 1, self.number + 1, True)

        def settle(self):
            wait_for(self.part, depths - 1, self.number, False)
            wait_for(self.res, depths - 1, self.number + 1, False)

    class FarFirst:
        def __init__(self, number, part, got_a, summed, got_b, res):
            self.number, self.part, self.got_a = number, part, got_a
            self.summed, self.got_b, self.res = summed, got_b, res

        def one(self):
            to_far(lambda far: self.part.at[pl.ds(far * NEAR, NEAR)], self.got_a.at[far_of], self.number)
            self.got_a[far_of] = self.part[pl.ds(far_of * NEAR, NEAR)]

        def two(self):
            wait_for(self.got_a, far_count - 1, self.number, True)
            self.summed[...] = total([self.got_a[i] for i in range(far_count)])
            to_near(lambda near: self.summed, self.got_b.at[near_of], self.number + 1)
            self.got_b[near_of] = self.summed[...]

        def three(self):
            wait_for(self.got_b, NEAR - 1, self.number + 1, True)
            place = pl.ds(far_of * NEAR, NEAR)
            self.res[place] = total([self.got_b[i] for i in range(NEAR)])
            block = self.res.at[place]
            to_far(lambda far: block, block, self.number + 2)

        def five(self):
            wait_for(self.res, depths - NEAR, self.number + 2, True)

        def settle(self):
            wait_for(self.part, depths - NEAR, self.number, False)
            wait_for(self.got_b, NEAR - 1, self.number + 1, False)
            wait_for(self.res, depths - NEAR, self.number + 2, False)

    row_1 = Direct(0, part_1, got_1, res_1)
    row_2 = FarFirst(4, part_2, got_2a, sum_2, got_2b, res_2)
    row_0 = FarFirst(7, part_0, got_0a, sum_0, got_0b, res_0)
    late = has_below & (height_of == heights // 2 - 1)
    soon = jnp.logical_not(late)
    lowest = jnp.logical_not(has_below)

    count = 3 * angles
    loads[0].wait()
    both = dot(own, spread([vol_ref[0], vol_ref[1]]))
    both = both[:count] + both[count:]
    publish(both[:angles], part_1)
    loads[4].wait()
    band_pad = jnp.zeros((angles, LANES - meas_ref.shape[2]), jnp.float32)

    def band_of(r):
        band = jnp.concatenate([meas_ref[:, r, :], band_pad], axis=1)
        return jnp.where(depth_of % 2 == 1, pltpu.roll(band, LANES // 2, 1), band)

    band_ref[...] = band_of(0)
    measure(band_of(1), part_1)

    @pl.when(lowest)
    def _():
        publish(both[2 * angles :], part_0)
        measure(band_ref[...], part_0)

    partners = depths - 1 + has_above.astype(jnp.int32) + has_below.astype(jnp.int32)
    pl.semaphore_wait(barrier, partners)

    halos = [
        remote(vol_hbm.at[0], halo_ref, halo_sem, 0, depth_of, below),
        remote(band_ref, band_up, halo_sem, 1, depth_of, below),
    ]

    @pl.when(has_below)
    def _():
        for copy in halos:
            copy.start()

    row_1.one()
    pl.when(lowest)(row_0.one)
    pl.when(late)(row_1.two)

    @pl.when(has_above)
    def _():
        halos[0].wait_recv()
        spilled = dot(from_halo, spread([halo_ref[...]]))
        image = both[angles : 2 * angles] + (spilled[:angles] + spilled[angles:])
        publish(image, part_2)
        halos[1].wait_recv()
        measure(band_up[...], part_2)

    @pl.when(jnp.logical_not(has_above))
    def _():
        part_2[...] = jnp.zeros_like(part_2)

    row_2.one()

    last = slices - 2
    sides = [
        remote(taps_hbm, taps_behind, side_sem, 0, ahead, height_of),
        remote(taps_hbm, taps_ahead, side_sem, 1, behind, height_of),
        remote(
            vol_ref.at[:, pl.ds(last, 2)], side_ref.at[:, pl.ds(last, 2)], side_sem, 2, ahead, height_of
        ),
        remote(vol_ref.at[:, pl.ds(0, 2)], side_ref.at[:, pl.ds(0, 2)], side_sem, 3, behind, height_of),
    ]
    for copy in sides:
        copy.start()

    pl.when(soon)(row_1.two)
    pl.when(lowest)(row_0.two)
    row_2.two()
    for copy in sides:
        copy.wait_recv()
    back = transposed([factor(lower, upper)])
    beyond = []
    for ref, depth, kept in (
        (taps_ahead, ahead, lane % slices < 2),
        (taps_behind, behind, lane % slices >= last),
    ):
        pair = weights(ref, depth)
        beyond.append(factor(*[jnp.where(kept, part, 0.0) for part in pair]))
    beyond = transposed(beyond)
    offset_ahead, offset_behind = offset_of(ahead), offset_of(behind)
    pl.when(lowest)(row_0.three)
    row_2.three()
    row_1.five()

    zero_tile = jnp.zeros((angles, LANES), jnp.float32)

    def image_of(ref):
        columns_of = [
            jnp.concatenate([ref[2 * tile], ref[2 * tile + 1]], axis=0) for tile in range(tiles)
        ]
        return jnp.concatenate(columns_of + [zero_tile], axis=1)

    def gathered(update, layer):
        whole = None
        for tap in range(taps):
            start = layer * first + tap * slices
            term = update[start : start + slices]
            if tap:
                term = roll_left(term, tap)
            whole = term if whole is None else whole + term
        return relax_step * whole[:, :columns]

    def prepared(image, moves):
        return [split_bf16(shift_rows(image, move)) for move in moves]

    def stacked(pairs):
        return jnp.concatenate([part for side in zip(*pairs) for part in side] * 2, axis=0)

    around = (offset_ahead, offset_behind)

    side_row = lax.broadcasted_iota(jnp.int32, (slices, columns), 0)
    outside = (side_row < 2) | (side_row >= last)

    def mixed(one, two):
        return stacked([one[0], two[0], one[1], two[1]])

    def pieces(src, dst, places, number, height):
        return [
            remote(src.at[place], dst.at[place], edge_sem, number + i, depth_of, height)
            for i, place in enumerate(places)
        ]

    whole_1 = image_of(res_1)
    own_1, around_1 = prepared(whole_1, (offset,)), prepared(whole_1, around)
    zero = jnp.zeros_like(whole_1).astype(jnp.bfloat16)
    nothing = [(zero, zero)] * 2
    volume_side = jnp.where(outside, side_ref[...], 0.0)
    update = dot(back[:first], stacked([own_1[0], nothing[0]]))
    layer_0 = vol_ref[0] + gathered(update, 0)
    update = dot(beyond[:first], mixed(around_1, nothing))
    side_0 = volume_side[0] + gathered(update, 0)
    down_ref[0] = layer_0
    down_ref[1] = side_0
    edges = (pl.ds(0, 2), pl.ds(last, 2))
    down_copies = pieces(
        down_ref, high_ref, (0, (1, edges[0]), (1, edges[1]), 2, (3, edges[1])), 2, below
    )
    up_copies = pieces(
        up_ref, low_ref, (0, (1, edges[0]), (1, edges[1]), 2, (3, edges[0]), (3, edges[1])), 7, above
    )
    next_copies = pieces(up2_ref, low2_ref, (0, (1, edges[0])), 13, above)

    @pl.when(has_below)
    def _():
        for copy in down_copies[:3]:
            copy.start()

    def completed():
        @pl.when(has_below)
        def _():
            for copy in up_copies[:3]:
                copy.wait_recv()

        up2_ref[0] = layer_0 + low_ref[0]
        up2_ref[1] = side_0 + jnp.where(outside, low_ref[1], 0.0)

        @pl.when(has_above)
        def _():
            for copy in next_copies:
                copy.start()

    pl.when(late)(completed)
    row_2.five()
    whole_2 = image_of(res_2)
    update = dot(back[first:], stacked(own_1 + prepared(whole_2, (offset,))))
    layer_1, part_2h2 = vol_ref[1] + gathered(update, 0), gathered(update, 1)
    up_ref[0] = part_2h2
    up_ref[2] = layer_1
    down_ref[2] = layer_1
    pl.when(has_above)(up_copies[0].start)
    pl.when(has_below)(down_copies[3].start)
    update = dot(beyond[first:], mixed(around_1, prepared(whole_2, around)))
    side_1, side_2h2 = volume_side[1] + gathered(update, 0), gathered(update, 1)
    up_ref[1] = side_2h2
    up_ref[3] = side_1
    down_ref[3] = side_1

    @pl.when(has_above)
    def _():
        for copy in up_copies[1:]:
            copy.start()

    pl.when(has_below)(down_copies[4].start)

    @pl.when(lowest)
    def _():
        row_0.five()
        image = prepared(image_of(res_0), (offset, *around))
        update = dot(back, stacked([nothing[0], image[0]]))
        low_ref[0] = gathered(update, 2)
        update = dot(beyond, mixed(nothing, image[1:]))
        low_ref[1] = gathered(update, 2)
        low_ref[2] = jnp.zeros((slices, columns), jnp.float32)
        low_ref[3] = jnp.zeros((slices, columns), jnp.float32)
        low2_ref[...] = jnp.zeros_like(low2_ref)

    @pl.when(jnp.logical_not(has_above))
    def _():
        high_ref[...] = jnp.zeros_like(high_ref)

    def arrive(condition, copies):
        @pl.when(condition)
        def _():
            for copy in copies:
                copy.wait_recv()

    def layer_of(inner, outer, kept=outside):
        return jnp.concatenate([inner, jnp.where(kept, outer, 0.0)], axis=0)

    place = lax.broadcasted_iota(jnp.int32, (2 * slices, columns), 0)
    place = depth_of * slices + jnp.where(place < slices + 4, place, place - 2 * slices)

    def normal(here, over, layer):
        layer = 2 * height_of + layer
        return directions(here, over, layer, 2 * heights, place, slices * depths)

    arrive(has_above, down_copies[:3])
    at_1 = layer_of(layer_1, side_1)
    at_2 = layer_of(high_ref[0] + part_2h2, high_ref[1] + side_2h2)
    n_1 = normal(at_1, at_2, 1)
    pl.when(soon)(completed)
    at_0 = layer_of(up2_ref[0], up2_ref[1])
    n_0 = normal(at_0, at_1, 0)
    next_1 = denoised(at_1, n_1, n_0[0])
    arrive(has_below, up_copies[3:])
    below_1 = layer_of(low_ref[2], low_ref[3])
    m_1 = normal(below_1, at_0, -1)
    next_0 = denoised(at_0, n_0, m_1[0])
    then_0 = normal(next_0, next_1, 0)
    row_1.settle()
    row_2.settle()
    pl.when(lowest)(row_0.settle)
    for copy in sides:
        copy.wait_send()

    @pl.when(has_below)
    def _():
        for copy in (*halos, *down_copies[:3]):
            copy.wait_send()

    arrive(has_below, next_copies)
    below_2 = layer_of(low2_ref[0], low2_ref[1], side_row < 2)
    under_1 = denoised(below_1, m_1, normal(below_2, below_1, -2)[0])
    stores = [pltpu.make_async_copy(result.at[i], out_ref.at[i], load_sem.at[i]) for i in range(2)]
    result[0] = denoised(next_0, then_0, normal(under_1, next_0, -1)[0])[:slices]
    stores[0].start()
    arrive(has_above, down_copies[3:])
    at_3 = layer_of(high_ref[2], high_ref[3], side_row >= last)
    next_2 = denoised(at_2, normal(at_2, at_3, 2), n_1[0])
    result[1] = denoised(next_1, normal(next_1, next_2, 1), then_0[0])[:slices]
    stores[1].start()

    for store in stores:
        store.wait()

    @pl.when(has_below)
    def _():
        down_copies[3].wait_send()
        down_copies[4].wait_send()

    @pl.when(has_above)
    def _():
        for copy in (*up_copies, *next_copies):
            copy.wait_send()


def per_device(volume, measured, taps, band_offset, angle_index):
    heights = lax.axis_size("height")
    depths = lax.axis_size("depth")
    f32 = jnp.float32
    layers, slices, columns = volume.shape
    far = depths // NEAR
    taps = jnp.swapaxes(taps, 1, 2)
    tile = (SUBLANES, LANES)
    main = (slices, columns)
    vmem = pltpu.VMEM
    far_first = [
        vmem((depths, *tile), f32), vmem((far, NEAR, *tile), f32), vmem((NEAR, *tile), f32),
        vmem((NEAR, NEAR, *tile), f32), vmem((depths, *tile), f32),
    ]
    scratch = [
        vmem(volume.shape, f32), vmem(measured.shape, f32), vmem(taps.shape, f32),
        vmem(band_offset.shape, jnp.int32), pltpu.SMEM(angle_index.shape, jnp.int32),
        vmem(main, f32), *[vmem((measured.shape[0], LANES), f32)] * 2, vmem(volume.shape, f32),
        vmem(taps.shape, f32), vmem(taps.shape, f32),
        *[vmem((depths, *tile), f32)] * 3, *far_first, *far_first,
        *[vmem((4, *main), f32)] * 4,
        vmem((2, *main), f32), vmem((2, *main), f32), vmem(volume.shape, f32),
        pltpu.SemaphoreType.DMA((5,)),
        pltpu.SemaphoreType.DMA((4,)),
        pltpu.SemaphoreType.DMA((8,)),
        pltpu.SemaphoreType.DMA((20,)),
        pltpu.SemaphoreType.DMA((30,)),
    ]
    return pl.pallas_call(
        functools.partial(kernel, heights, depths),
        out_shape=jax.ShapeDtypeStruct(volume.shape, f32),
        in_specs=[pl.BlockSpec(memory_space=pl.ANY)] * 5,
        out_specs=pl.BlockSpec(memory_space=pl.ANY),
        scratch_shapes=scratch,
        compiler_params=pltpu.CompilerParams(
            collective_id=0, has_side_effects=True, vmem_limit_bytes=60 * 1024 * 1024
        ),
    )(volume, measured, taps, band_offset, angle_index)


def solution(mesh):
    in_specs = (
        P("height", "depth", None),
        P(None, "height", "depth"),
        P(None, None, "depth"),
        P(),
        P(),
    )
    out_specs = P("height", "depth", None)
    return jax.shard_map(
        per_device, mesh=mesh, in_specs=in_specs, out_specs=out_specs, check_vma=False
    )
```

```python
import functools
import math

import jax
import jax.numpy as jnp
from jax import lax
from jax.experimental import pallas as pl
from jax.experimental.pallas import tpu as pltpu
from jax.sharding import PartitionSpec as P

TAPS = 4
OFFMAX = 64
N_VIEWS = 720
LANES = 128
SUBLANES = 8
NEAR = 4

relax_step = 0.5
tv_step = 0.08
tv_eps = 0.1

MESH = pl.DeviceIdType.MESH


def split_bf16(value):
    high = value.astype(jnp.bfloat16)
    low = (value - high.astype(jnp.float32)).astype(jnp.bfloat16)
    return high, low


def roll_left(value, amount):
    return pltpu.roll(value, value.shape[1] - amount, 1)


def shift_rows(value, amount):
    move = amount + OFFMAX
    top = move // OFFMAX
    moved_left = roll_left(value, OFFMAX)
    moved_right = pltpu.roll(value, OFFMAX, 1)
    value = jnp.where(top == 0, moved_right, jnp.where(top == 1, value, moved_left))
    for bit in range(6):
        stride = 1 << bit
        value = jnp.where((move // stride) % 2 == 1, roll_left(value, stride), value)
    return value


def directions(here, over, layer, height_total, depth_place, depth_total):
    rows, columns = here.shape
    inner = lax.broadcasted_iota(jnp.int32, (rows, columns), 1) < columns - 1
    open_row = (depth_place >= 0) & (depth_place + 1 < depth_total)
    up = jnp.where((layer >= 0) & (layer + 1 < height_total), over - here, 0.0)
    deep = jnp.where(open_row, pltpu.roll(here, rows - 1, 0) - here, 0.0)
    wide = jnp.where(inner, roll_left(here, 1) - here, 0.0)
    scale = lax.rsqrt(tv_eps * tv_eps + up * up + deep * deep + wide * wide)
    return up * scale, deep * scale, wide * scale


def denoised(here, normal, under):
    up, deep, wide = normal
    diverge = (up - under) + (deep - pltpu.roll(deep, 1, 0)) + (wide - pltpu.roll(wide, 1, 1))
    return here + tv_step * diverge


def kernel(
    heights, depths,
    vol_hbm, meas_hbm, taps_hbm, off_hbm, angle_hbm,
    out_ref,
    vol_ref, meas_ref, taps_ref, off_ref, angle_ref,
    halo_ref, band_ref, band_up, side_ref, taps_ahead, taps_behind,
    part_1, got_1, res_1,
    part_2, got_2a, sum_2, got_2b, res_2,
    part_0, got_0a, sum_0, got_0b, res_0,
    up_ref, low_ref, down_ref, high_ref,
    up2_ref, low2_ref, result,
    load_sem, halo_sem, side_sem, ring_sem, edge_sem,
):
    height_of = lax.axis_index("height")
    depth_of = lax.axis_index("depth")
    above, below = height_of + 1, height_of - 1
    has_above, has_below = height_of < heights - 1, height_of > 0
    ahead = lax.rem(depth_of + 1, depths)
    behind = lax.rem(depth_of + depths - 1, depths)
    far_of, near_of = depth_of // NEAR, depth_of % NEAR
    far_count = depths // NEAR
    _, slices, columns = vol_ref.shape
    tiles = columns // LANES
    angles = off_ref.shape[0]
    taps = taps_ref.shape[0]

    loads = [
        pltpu.make_async_copy(src, dst, load_sem.at[i])
        for i, (src, dst) in enumerate(
            (
                (vol_hbm, vol_ref), (angle_hbm, angle_ref), (taps_hbm, taps_ref),
                (off_hbm, off_ref), (meas_hbm, meas_ref),
            )
        )
    ]
    for load in loads:
        load.start()
    def remote(src, dst, sems, number, depth, height):
        return pltpu.make_async_remote_copy(
            src_ref=src, dst_ref=dst,
            send_sem=sems.at[2 * number], recv_sem=sems.at[2 * number + 1],
            device_id=(depth, height), device_id_type=MESH,
        )

    barrier = pltpu.get_barrier_semaphore()

    def greet(depth, height):
        pl.semaphore_signal(barrier, inc=1, device_id=(depth, height), device_id_type=MESH)

    def fars():
        order = sorted(range(1, far_count), key=lambda i: -min(i, far_count - i))
        return [lax.rem(far_of + i, far_count) for i in order]

    def nears():
        return [lax.rem(near_of + i, NEAR) for i in range(1, NEAR)]

    def everyone():
        order = [(i, j) for i in range(far_count) for j in range(NEAR) if i or j]
        order.sort(key=lambda ij: -min(ij[0], far_count - ij[0]) - min(ij[1], NEAR - ij[1]))
        return [
            lax.rem(far_of + i, far_count) * NEAR + lax.rem(near_of + j, NEAR) for i, j in order
        ]

    @pl.when(has_below)
    def _():
        greet(depth_of, below)

    @pl.when(has_above)
    def _():
        greet(depth_of, above)

    for depth in everyone():
        greet(depth, height_of)

    for load in loads[1:4]:
        load.wait()
    row = lax.broadcasted_iota(jnp.int32, (angles, LANES), 0)
    lane = lax.broadcasted_iota(jnp.int32, (angles, LANES), 1)
    view = jnp.zeros((angles, LANES), jnp.float32)
    for i in range(angles):
        view = jnp.where(row == i, angle_ref[i].astype(jnp.float32), view)
    swing = 0.45 * jnp.sin(2.0 * math.pi / N_VIEWS * view)
    first = taps * slices

    def weights(ref, depth):
        weight = jnp.concatenate([ref[tap] for tap in range(taps)], axis=0)
        weight = jnp.concatenate([weight, jnp.zeros((first, LANES - angles), jnp.float32)], axis=1)
        weight = jnp.concatenate([weight, jnp.zeros((LANES - first, LANES), jnp.float32)], axis=0)
        weight = weight.T[:angles]
        depth_place = (depth * slices + lane % slices).astype(jnp.float32) + 0.5
        rise = 0.5 + swing * jnp.cos(math.pi / (slices * depths) * depth_place)
        return weight * (1.0 - rise), weight * rise

    def offset_of(depth):
        off_lane = lax.broadcasted_iota(jnp.int32, off_ref.shape, 1)
        offset = jnp.where(off_lane == depth, off_ref[...].astype(jnp.float32), 0.0)
        return jnp.sum(offset, axis=1, keepdims=True).astype(jnp.int32)

    def factor(lower, upper):
        return jnp.concatenate(
            [
                upper + pltpu.roll(lower, first, 1),
                pltpu.roll(upper, first, 1) + pltpu.roll(lower, 2 * first, 1),
            ],
            axis=0,
        )

    def transposed(parts):
        whole = jnp.concatenate(parts * 4, axis=0)
        turned = whole.T
        high = turned.astype(jnp.bfloat16).astype(jnp.float32)
        place = lax.broadcasted_iota(jnp.int32, turned.shape, 1)
        return jnp.where(place < turned.shape[1] // 2, high, turned - high).astype(jnp.bfloat16)[: 3 * first]

    lower, upper = weights(taps_ref, depth_of)
    offset = offset_of(depth_of)
    own = jnp.concatenate(
        [upper + pltpu.roll(lower, first, 1), pltpu.roll(upper, first, 1), lower], axis=0
    )
    own = jnp.concatenate(split_bf16(own + pltpu.roll(own, 2 * first, 1)), axis=0)
    from_halo = (lower + pltpu.roll(lower, first, 1))[:, : 2 * first]
    from_halo = jnp.concatenate(split_bf16(from_halo), axis=0)
    zeros = jnp.zeros((slices, LANES), jnp.float32)

    def spread(layers):
        wide = [jnp.concatenate([layer, zeros], axis=1) for layer in layers]
        rows = []
        for layer in wide:
            for tap in range(taps):
                rows.append(layer if tap == 0 else pltpu.roll(layer, tap, 1))
        high, low = split_bf16(jnp.concatenate(rows, axis=0))
        return jnp.concatenate([high, low], axis=0)

    def dot(a, b):
        return jnp.dot(a, b, preferred_element_type=jnp.float32)

    halves = angles // SUBLANES

    def publish(image, ref):
        image = shift_rows(image, -offset)
        for tile in range(tiles):
            for half in range(halves):
                ref[tile * halves + half] = -image[
                    half * SUBLANES : (half + 1) * SUBLANES, tile * LANES : (tile + 1) * LANES
                ]

    def measure(band, ref):
        for half in range(halves):
            place = depth_of // 2 * halves + half
            ref[place] = ref[place] + band[half * SUBLANES : (half + 1) * SUBLANES]

    def to_far(src, dst, number):
        for far in fars():
            remote(src(far), dst, ring_sem, number, far * NEAR + near_of, height_of).start()

    def to_near(src, dst, number):
        for near in nears():
            remote(src(near), dst, ring_sem, number, far_of * NEAR + near, height_of).start()

    def wait_for(ref, count, number, received):
        some = ref.at[pl.ds(0, count)]
        pltpu.make_async_copy(some, some, ring_sem.at[2 * number + int(received)]).wait()

    def total(parts):
        while len(parts) > 1:
            parts = [a + b for a, b in zip(parts[::2], parts[1::2])]
        return parts[0]

    class Direct:
        def __init__(self, number, part, got, res):
            self.number, self.part, self.got, self.res = number, part, got, res

        def one(self):
            for peer in everyone():
                remote(
                    self.part.at[peer], self.got.at[depth_of], ring_sem, self.number, peer, height_of
                ).start()
            self.got[depth_of] = self.part[depth_of]

        def two(self):
            wait_for(self.got, depths - 1, self.number, True)
            self.res[depth_of] = total([self.got[i] for i in range(depths)])
            mine = self.res.at[depth_of]
            for peer in everyone():
                remote(mine, mine, ring_sem, self.number + 1, peer, height_of).start()

        def five(self):
            wait_for(self.res, depths - 1, self.number + 1, True)

        def settle(self):
            wait_for(self.part, depths - 1, self.number, False)
            wait_for(self.res, depths - 1, self.number + 1, False)

    class FarFirst:
        def __init__(self, number, part, got_a, summed, got_b, res):
            self.number, self.part, self.got_a = number, part, got_a
            self.summed, self.got_b, self.res = summed, got_b, res

        def one(self):
            to_far(lambda far: self.part.at[pl.ds(far * NEAR, NEAR)], self.got_a.at[far_of], self.number)
            self.got_a[far_of] = self.part[pl.ds(far_of * NEAR, NEAR)]

        def two(self):
            wait_for(self.got_a, far_count - 1, self.number, True)
            self.summed[...] = total([self.got_a[i] for i in range(far_count)])
            to_near(lambda near: self.summed, self.got_b.at[near_of], self.number + 1)
            self.got_b[near_of] = self.summed[...]

        def three(self):
            wait_for(self.got_b, NEAR - 1, self.number + 1, True)
            place = pl.ds(far_of * NEAR, NEAR)
            self.res[place] = total([self.got_b[i] for i in range(NEAR)])
            block = self.res.at[place]
            to_far(lambda far: block, block, self.number + 2)

        def five(self):
            wait_for(self.res, depths - NEAR, self.number + 2, True)

        def settle(self):
            wait_for(self.part, depths - NEAR, self.number, False)
            wait_for(self.got_b, NEAR - 1, self.number + 1, False)
            wait_for(self.res, depths - NEAR, self.number + 2, False)

    row_1 = Direct(0, part_1, got_1, res_1)
    row_2 = FarFirst(4, part_2, got_2a, sum_2, got_2b, res_2)
    row_0 = FarFirst(7, part_0, got_0a, sum_0, got_0b, res_0)
    late = has_below & (height_of == heights // 2 - 1)
    soon = jnp.logical_not(late)
    lowest = jnp.logical_not(has_below)

    count = 3 * angles
    loads[0].wait()
    both = dot(own, spread([vol_ref[0], vol_ref[1]]))
    both = both[:count] + both[count:]
    publish(both[:angles], part_1)
    loads[4].wait()
    band_pad = jnp.zeros((angles, LANES - meas_ref.shape[2]), jnp.float32)

    def band_of(r):
        band = jnp.concatenate([meas_ref[:, r, :], band_pad], axis=1)
        return jnp.where(depth_of % 2 == 1, pltpu.roll(band, LANES // 2, 1), band)

    band_ref[...] = band_of(0)
    measure(band_of(1), part_1)

    @pl.when(lowest)
    def _():
        publish(both[2 * angles :], part_0)
        measure(band_ref[...], part_0)

    partners = depths - 1 + has_above.astype(jnp.int32) + has_below.astype(jnp.int32)
    pl.semaphore_wait(barrier, partners)

    halos = [
        remote(vol_hbm.at[0], halo_ref, halo_sem, 0, depth_of, below),
        remote(band_ref, band_up, halo_sem, 1, depth_of, below),
    ]

    @pl.when(has_below)
    def _():
        for copy in halos:
            copy.start()

    row_1.one()
    pl.when(lowest)(row_0.one)
    pl.when(late)(row_1.two)

    @pl.when(has_above)
    def _():
        halos[0].wait_recv()
        spilled = dot(from_halo, spread([halo_ref[...]]))
        image = both[angles : 2 * angles] + (spilled[:angles] + spilled[angles:])
        publish(image, part_2)
        halos[1].wait_recv()
        measure(band_up[...], part_2)

    @pl.when(jnp.logical_not(has_above))
    def _():
        part_2[...] = jnp.zeros_like(part_2)

    row_2.one()

    last = slices - 2
    sides = [
        remote(taps_hbm, taps_behind, side_sem, 0, ahead, height_of),
        remote(taps_hbm, taps_ahead, side_sem, 1, behind, height_of),
        remote(
            vol_ref.at[:, pl.ds(last, 2)], side_ref.at[:, pl.ds(last, 2)], side_sem, 2, ahead, height_of
        ),
        remote(vol_ref.at[:, pl.ds(0, 2)], side_ref.at[:, pl.ds(0, 2)], side_sem, 3, behind, height_of),
    ]
    for copy in sides:
        copy.start()

    pl.when(soon)(row_1.two)
    pl.when(lowest)(row_0.two)
    row_2.two()
    back = transposed([factor(lower, upper)])
    pl.when(lowest)(row_0.three)
    row_2.three()
    for copy in sides:
        copy.wait_recv()
    beyond = []
    for ref, depth, kept in (
        (taps_ahead, ahead, lane % slices < 2),
        (taps_behind, behind, lane % slices >= last),
    ):
        pair = weights(ref, depth)
        beyond.append(factor(*[jnp.where(kept, part, 0.0) for part in pair]))
    beyond = transposed(beyond)
    offset_ahead, offset_behind = offset_of(ahead), offset_of(behind)
    row_1.five()

    zero_tile = jnp.zeros((angles, LANES), jnp.float32)

    def image_of(ref):
        columns_of = [
            jnp.concatenate([ref[2 * tile], ref[2 * tile + 1]], axis=0) for tile in range(tiles)
        ]
        return jnp.concatenate(columns_of + [zero_tile], axis=1)

    def gathered(update, layer):
        whole = None
        for tap in range(taps):
            start = layer * first + tap * slices
            term = update[start : start + slices]
            if tap:
                term = roll_left(term, tap)
            whole = term if whole is None else whole + term
        return relax_step * whole[:, :columns]

    def prepared(image, moves):
        return [split_bf16(shift_rows(image, move)) for move in moves]

    def stacked(pairs):
        return jnp.concatenate([part for side in zip(*pairs) for part in side] * 2, axis=0)

    around = (offset_ahead, offset_behind)

    side_row = lax.broadcasted_iota(jnp.int32, (slices, columns), 0)
    outside = (side_row < 2) | (side_row >= last)

    def mixed(one, two):
        return stacked([one[0], two[0], one[1], two[1]])

    def pieces(src, dst, places, number, height):
        return [
            remote(src.at[place], dst.at[place], edge_sem, number + i, depth_of, height)
            for i, place in enumerate(places)
        ]

    whole_1 = image_of(res_1)
    own_1, around_1 = prepared(whole_1, (offset,)), prepared(whole_1, around)
    zero = jnp.zeros_like(whole_1).astype(jnp.bfloat16)
    nothing = [(zero, zero)] * 2
    volume_side = jnp.where(outside, side_ref[...], 0.0)
    update = dot(back[:first], stacked([own_1[0], nothing[0]]))
    layer_0 = vol_ref[0] + gathered(update, 0)
    update = dot(beyond[:first], mixed(around_1, nothing))
    side_0 = volume_side[0] + gathered(update, 0)
    down_ref[0] = layer_0
    down_ref[1] = side_0
    edges = (pl.ds(0, 2), pl.ds(last, 2))
    down_copies = pieces(
        down_ref, high_ref, (0, (1, edges[0]), (1, edges[1]), 2, (3, edges[1])), 2, below
    )
    up_copies = pieces(
        up_ref, low_ref, (0, (1, edges[0]), (1, edges[1]), 2, (3, edges[0]), (3, edges[1])), 7, above
    )
    next_copies = pieces(up2_ref, low2_ref, (0, (1, edges[0])), 13, above)

    @pl.when(has_below)
    def _():
        for copy in down_copies[:3]:
            copy.start()

    def completed():
        @pl.when(has_below)
        def _():
            for copy in up_copies[:3]:
                copy.wait_recv()

        up2_ref[0] = layer_0 + low_ref[0]
        up2_ref[1] = side_0 + jnp.where(outside, low_ref[1], 0.0)

        @pl.when(has_above)
        def _():
            for copy in next_copies:
                copy.start()

    pl.when(late)(completed)
    row_2.five()
    whole_2 = image_of(res_2)
    update = dot(back[first:], stacked(own_1 + prepared(whole_2, (offset,))))
    layer_1, part_2h2 = vol_ref[1] + gathered(update, 0), gathered(update, 1)
    up_ref[0] = part_2h2
    up_ref[2] = layer_1
    down_ref[2] = layer_1
    pl.when(has_above)(up_copies[0].start)
    pl.when(has_below)(down_copies[3].start)
    update = dot(beyond[first:], mixed(around_1, prepared(whole_2, around)))
    side_1, side_2h2 = volume_side[1] + gathered(update, 0), gathered(update, 1)
    up_ref[1] = side_2h2
    up_ref[3] = side_1
    down_ref[3] = side_1

    @pl.when(has_above)
    def _():
        for copy in up_copies[1:]:
            copy.start()

    pl.when(has_below)(down_copies[4].start)

    @pl.when(lowest)
    def _():
        row_0.five()
        image = prepared(image_of(res_0), (offset, *around))
        update = dot(back, stacked([nothing[0], image[0]]))
        low_ref[0] = gathered(update, 2)
        update = dot(beyond, mixed(nothing, image[1:]))
        low_ref[1] = gathered(update, 2)
        low_ref[2] = jnp.zeros((slices, columns), jnp.float32)
        low_ref[3] = jnp.zeros((slices, columns), jnp.float32)
        low2_ref[...] = jnp.zeros_like(low2_ref)

    @pl.when(jnp.logical_not(has_above))
    def _():
        high_ref[...] = jnp.zeros_like(high_ref)

    def arrive(condition, copies):
        @pl.when(condition)
        def _():
            for copy in copies:
                copy.wait_recv()

    def layer_of(inner, outer, kept=outside):
        return jnp.concatenate([inner, jnp.where(kept, outer, 0.0)], axis=0)

    place = lax.broadcasted_iota(jnp.int32, (2 * slices, columns), 0)
    place = depth_of * slices + jnp.where(place < slices + 4, place, place - 2 * slices)

    def normal(here, over, layer):
        layer = 2 * height_of + layer
        return directions(here, over, layer, 2 * heights, place, slices * depths)

    arrive(has_above, down_copies[:3])
    at_1 = layer_of(layer_1, side_1)
    at_2 = layer_of(high_ref[0] + part_2h2, high_ref[1] + side_2h2)
    n_1 = normal(at_1, at_2, 1)
    pl.when(soon)(completed)
    at_0 = layer_of(up2_ref[0], up2_ref[1])
    n_0 = normal(at_0, at_1, 0)
    next_1 = denoised(at_1, n_1, n_0[0])
    arrive(has_below, up_copies[3:])
    below_1 = layer_of(low_ref[2], low_ref[3])
    m_1 = normal(below_1, at_0, -1)
    next_0 = denoised(at_0, n_0, m_1[0])
    then_0 = normal(next_0, next_1, 0)
    row_1.settle()
    row_2.settle()
    pl.when(lowest)(row_0.settle)
    for copy in sides:
        copy.wait_send()

    @pl.when(has_below)
    def _():
        for copy in (*halos, *down_copies[:3]):
            copy.wait_send()

    arrive(has_below, next_copies)
    below_2 = layer_of(low2_ref[0], low2_ref[1], side_row < 2)
    under_1 = denoised(below_1, m_1, normal(below_2, below_1, -2)[0])
    stores = [pltpu.make_async_copy(result.at[i], out_ref.at[i], load_sem.at[i]) for i in range(2)]
    result[0] = denoised(next_0, then_0, normal(under_1, next_0, -1)[0])[:slices]
    stores[0].start()
    arrive(has_above, down_copies[3:])
    at_3 = layer_of(high_ref[2], high_ref[3], side_row >= last)
    next_2 = denoised(at_2, normal(at_2, at_3, 2), n_1[0])
    result[1] = denoised(next_1, normal(next_1, next_2, 1), then_0[0])[:slices]
    stores[1].start()

    for store in stores:
        store.wait()

    @pl.when(has_below)
    def _():
        down_copies[3].wait_send()
        down_copies[4].wait_send()

    @pl.when(has_above)
    def _():
        for copy in (*up_copies, *next_copies):
            copy.wait_send()


def per_device(volume, measured, taps, band_offset, angle_index):
    heights = lax.axis_size("height")
    depths = lax.axis_size("depth")
    f32 = jnp.float32
    layers, slices, columns = volume.shape
    far = depths // NEAR
    taps = jnp.swapaxes(taps, 1, 2)
    tile = (SUBLANES, LANES)
    main = (slices, columns)
    vmem = pltpu.VMEM
    far_first = [
        vmem((depths, *tile), f32), vmem((far, NEAR, *tile), f32), vmem((NEAR, *tile), f32),
        vmem((NEAR, NEAR, *tile), f32), vmem((depths, *tile), f32),
    ]
    scratch = [
        vmem(volume.shape, f32), vmem(measured.shape, f32), vmem(taps.shape, f32),
        vmem(band_offset.shape, jnp.int32), pltpu.SMEM(angle_index.shape, jnp.int32),
        vmem(main, f32), *[vmem((measured.shape[0], LANES), f32)] * 2, vmem(volume.shape, f32),
        vmem(taps.shape, f32), vmem(taps.shape, f32),
        *[vmem((depths, *tile), f32)] * 3, *far_first, *far_first,
        *[vmem((4, *main), f32)] * 4,
        vmem((2, *main), f32), vmem((2, *main), f32), vmem(volume.shape, f32),
        pltpu.SemaphoreType.DMA((5,)),
        pltpu.SemaphoreType.DMA((4,)),
        pltpu.SemaphoreType.DMA((8,)),
        pltpu.SemaphoreType.DMA((20,)),
        pltpu.SemaphoreType.DMA((30,)),
    ]
    return pl.pallas_call(
        functools.partial(kernel, heights, depths),
        out_shape=jax.ShapeDtypeStruct(volume.shape, f32),
        in_specs=[pl.BlockSpec(memory_space=pl.ANY)] * 5,
        out_specs=pl.BlockSpec(memory_space=pl.ANY),
        scratch_shapes=scratch,
        compiler_params=pltpu.CompilerParams(
            collective_id=0, has_side_effects=True, vmem_limit_bytes=60 * 1024 * 1024
        ),
    )(volume, measured, taps, band_offset, angle_index)


def solution(mesh):
    in_specs = (
        P("height", "depth", None),
        P(None, "height", "depth"),
        P(None, None, "depth"),
        P(),
        P(),
    )
    out_specs = P("height", "depth", None)
    return jax.shard_map(
        per_device, mesh=mesh, in_specs=in_specs, out_specs=out_specs, check_vma=False
    )
```

```python
import functools
import math

import jax
import jax.numpy as jnp
from jax import lax
from jax.experimental import pallas as pl
from jax.experimental.pallas import tpu as pltpu
from jax.sharding import PartitionSpec as P

TAPS = 4
OFFMAX = 64
N_VIEWS = 720
LANES = 128
SUBLANES = 8
NEAR = 4

relax_step = 0.5
tv_step = 0.08
tv_eps = 0.1

MESH = pl.DeviceIdType.MESH


def split_bf16(value):
    high = value.astype(jnp.bfloat16)
    low = (value - high.astype(jnp.float32)).astype(jnp.bfloat16)
    return high, low


def roll_left(value, amount):
    return pltpu.roll(value, value.shape[1] - amount, 1)


def shift_rows(value, amount):
    move = amount + OFFMAX
    top = move // OFFMAX
    moved_left = roll_left(value, OFFMAX)
    moved_right = pltpu.roll(value, OFFMAX, 1)
    value = jnp.where(top == 0, moved_right, jnp.where(top == 1, value, moved_left))
    for bit in range(6):
        stride = 1 << bit
        value = jnp.where((move // stride) % 2 == 1, roll_left(value, stride), value)
    return value


def directions(here, over, layer, height_total, depth_place, depth_total):
    rows, columns = here.shape
    inner = lax.broadcasted_iota(jnp.int32, (rows, columns), 1) < columns - 1
    open_row = (depth_place >= 0) & (depth_place + 1 < depth_total)
    up = jnp.where((layer >= 0) & (layer + 1 < height_total), over - here, 0.0)
    deep = jnp.where(open_row, pltpu.roll(here, rows - 1, 0) - here, 0.0)
    wide = jnp.where(inner, roll_left(here, 1) - here, 0.0)
    scale = lax.rsqrt(tv_eps * tv_eps + up * up + deep * deep + wide * wide)
    return up * scale, deep * scale, wide * scale


def denoised(here, normal, under):
    up, deep, wide = normal
    diverge = (up - under) + (deep - pltpu.roll(deep, 1, 0)) + (wide - pltpu.roll(wide, 1, 1))
    return here + tv_step * diverge


def kernel(
    heights, depths,
    vol_hbm, meas_hbm, taps_hbm, off_hbm, angle_hbm,
    out_ref,
    vol_ref, meas_ref, taps_ref, off_ref, angle_ref,
    halo_ref, band_ref, band_up, side_ref, taps_ahead, taps_behind,
    part_1, got_1, res_1,
    part_2, got_2a, sum_2, got_2b, res_2,
    part_0, got_0a, sum_0, got_0b, res_0,
    up_ref, low_ref, down_ref, high_ref,
    up2_ref, low2_ref, result,
    load_sem, halo_sem, side_sem, ring_sem, edge_sem,
):
    height_of = lax.axis_index("height")
    depth_of = lax.axis_index("depth")
    above, below = height_of + 1, height_of - 1
    has_above, has_below = height_of < heights - 1, height_of > 0
    ahead = lax.rem(depth_of + 1, depths)
    behind = lax.rem(depth_of + depths - 1, depths)
    far_of, near_of = depth_of // NEAR, depth_of % NEAR
    far_count = depths // NEAR
    _, slices, columns = vol_ref.shape
    tiles = columns // LANES
    angles = off_ref.shape[0]
    taps = taps_ref.shape[0]

    loads = [
        pltpu.make_async_copy(src, dst, load_sem.at[i])
        for i, (src, dst) in enumerate(
            (
                (vol_hbm, vol_ref), (angle_hbm, angle_ref), (taps_hbm, taps_ref),
                (off_hbm, off_ref), (meas_hbm, meas_ref),
            )
        )
    ]
    for load in loads:
        load.start()
    def remote(src, dst, sems, number, depth, height):
        return pltpu.make_async_remote_copy(
            src_ref=src, dst_ref=dst,
            send_sem=sems.at[2 * number], recv_sem=sems.at[2 * number + 1],
            device_id=(depth, height), device_id_type=MESH,
        )

    barrier = pltpu.get_barrier_semaphore()

    def greet(depth, height):
        pl.semaphore_signal(barrier, inc=1, device_id=(depth, height), device_id_type=MESH)

    def fars():
        order = sorted(range(1, far_count), key=lambda i: -min(i, far_count - i))
        return [lax.rem(far_of + i, far_count) for i in order]

    def nears():
        return [lax.rem(near_of + i, NEAR) for i in range(1, NEAR)]

    def everyone():
        order = [(i, j) for i in range(far_count) for j in range(NEAR) if i or j]
        order.sort(key=lambda ij: -min(ij[0], far_count - ij[0]) - min(ij[1], NEAR - ij[1]))
        return [
            lax.rem(far_of + i, far_count) * NEAR + lax.rem(near_of + j, NEAR) for i, j in order
        ]

    @pl.when(has_below)
    def _():
        greet(depth_of, below)

    @pl.when(has_above)
    def _():
        greet(depth_of, above)

    for depth in everyone():
        greet(depth, height_of)

    for load in loads[1:4]:
        load.wait()
    row = lax.broadcasted_iota(jnp.int32, (angles, LANES), 0)
    lane = lax.broadcasted_iota(jnp.int32, (angles, LANES), 1)
    view = jnp.zeros((angles, LANES), jnp.float32)
    for i in range(angles):
        view = jnp.where(row == i, angle_ref[i].astype(jnp.float32), view)
    swing = 0.45 * jnp.sin(2.0 * math.pi / N_VIEWS * view)
    first = taps * slices

    def weights(ref, depth):
        weight = jnp.concatenate([ref[tap] for tap in range(taps)], axis=0)
        weight = jnp.concatenate([weight, jnp.zeros((first, LANES - angles), jnp.float32)], axis=1)
        weight = jnp.concatenate([weight, jnp.zeros((LANES - first, LANES), jnp.float32)], axis=0)
        weight = weight.T[:angles]
        depth_place = (depth * slices + lane % slices).astype(jnp.float32) + 0.5
        rise = 0.5 + swing * jnp.cos(math.pi / (slices * depths) * depth_place)
        return weight * (1.0 - rise), weight * rise

    def offset_of(depth):
        off_lane = lax.broadcasted_iota(jnp.int32, off_ref.shape, 1)
        offset = jnp.where(off_lane == depth, off_ref[...].astype(jnp.float32), 0.0)
        return jnp.sum(offset, axis=1, keepdims=True).astype(jnp.int32)

    def factor(lower, upper):
        return jnp.concatenate(
            [
                upper + pltpu.roll(lower, first, 1),
                pltpu.roll(upper, first, 1) + pltpu.roll(lower, 2 * first, 1),
            ],
            axis=0,
        )

    def transposed(parts):
        whole = jnp.concatenate(parts * 4, axis=0)
        turned = whole.T
        high = turned.astype(jnp.bfloat16).astype(jnp.float32)
        place = lax.broadcasted_iota(jnp.int32, turned.shape, 1)
        return jnp.where(place < turned.shape[1] // 2, high, turned - high).astype(jnp.bfloat16)[: 3 * first]

    lower, upper = weights(taps_ref, depth_of)
    offset = offset_of(depth_of)
    own = jnp.concatenate(
        [upper + pltpu.roll(lower, first, 1), pltpu.roll(upper, first, 1), lower], axis=0
    )
    own = jnp.concatenate(split_bf16(own + pltpu.roll(own, 2 * first, 1)), axis=0)
    from_halo = (lower + pltpu.roll(lower, first, 1))[:, : 2 * first]
    from_halo = jnp.concatenate(split_bf16(from_halo), axis=0)
    zeros = jnp.zeros((slices, LANES), jnp.float32)

    def spread(layers):
        wide = [jnp.concatenate([layer, zeros], axis=1) for layer in layers]
        rows = []
        for layer in wide:
            for tap in range(taps):
                rows.append(layer if tap == 0 else pltpu.roll(layer, tap, 1))
        high, low = split_bf16(jnp.concatenate(rows, axis=0))
        return jnp.concatenate([high, low], axis=0)

    def dot(a, b):
        return jnp.dot(a, b, preferred_element_type=jnp.float32)

    halves = angles // SUBLANES

    def publish(image, ref):
        image = shift_rows(image, -offset)
        for tile in range(tiles):
            for half in range(halves):
                ref[tile * halves + half] = -image[
                    half * SUBLANES : (half + 1) * SUBLANES, tile * LANES : (tile + 1) * LANES
                ]

    def measure(band, ref):
        for half in range(halves):
            place = depth_of // 2 * halves + half
            ref[place] = ref[place] + band[half * SUBLANES : (half + 1) * SUBLANES]

    def to_far(src, dst, number):
        for far in fars():
            remote(src(far), dst, ring_sem, number, far * NEAR + near_of, height_of).start()

    def to_near(src, dst, number):
        for near in nears():
            remote(src(near), dst, ring_sem, number, far_of * NEAR + near, height_of).start()

    def wait_for(ref, count, number, received):
        some = ref.at[pl.ds(0, count)]
        pltpu.make_async_copy(some, some, ring_sem.at[2 * number + int(received)]).wait()

    def total(parts):
        while len(parts) > 1:
            parts = [a + b for a, b in zip(parts[::2], parts[1::2])]
        return parts[0]

    class Direct:
        def __init__(self, number, part, got, res):
            self.number, self.part, self.got, self.res = number, part, got, res

        def one(self):
            for peer in everyone():
                remote(
                    self.part.at[peer], self.got.at[depth_of], ring_sem, self.number, peer, height_of
                ).start()
            self.got[depth_of] = self.part[depth_of]

        def two(self):
            wait_for(self.got, depths - 1, self.number, True)
            self.res[depth_of] = total([self.got[i] for i in range(depths)])
            mine = self.res.at[depth_of]
            for peer in everyone():
                remote(mine, mine, ring_sem, self.number + 1, peer, height_of).start()

        def five(self):
            wait_for(self.res, depths - 1, self.number + 1, True)

        def settle(self):
            wait_for(self.part, depths - 1, self.number, False)
            wait_for(self.res, depths - 1, self.number + 1, False)

    class FarFirst:
        def __init__(self, number, part, got_a, summed, got_b, res):
            self.number, self.part, self.got_a = number, part, got_a
            self.summed, self.got_b, self.res = summed, got_b, res

        def one(self):
            to_far(lambda far: self.part.at[pl.ds(far * NEAR, NEAR)], self.got_a.at[far_of], self.number)
            self.got_a[far_of] = self.part[pl.ds(far_of * NEAR, NEAR)]

        def two(self):
            wait_for(self.got_a, far_count - 1, self.number, True)
            self.summed[...] = total([self.got_a[i] for i in range(far_count)])
            to_near(lambda near: self.summed, self.got_b.at[near_of], self.number + 1)
            self.got_b[near_of] = self.summed[...]

        def three(self):
            wait_for(self.got_b, NEAR - 1, self.number + 1, True)
            place = pl.ds(far_of * NEAR, NEAR)
            self.res[place] = total([self.got_b[i] for i in range(NEAR)])
            block = self.res.at[place]
            to_far(lambda far: block, block, self.number + 2)

        def five(self):
            wait_for(self.res, depths - NEAR, self.number + 2, True)

        def settle(self):
            wait_for(self.part, depths - NEAR, self.number, False)
            wait_for(self.got_b, NEAR - 1, self.number + 1, False)
            wait_for(self.res, depths - NEAR, self.number + 2, False)

    row_1 = Direct(0, part_1, got_1, res_1)
    row_2 = FarFirst(4, part_2, got_2a, sum_2, got_2b, res_2)
    row_0 = FarFirst(7, part_0, got_0a, sum_0, got_0b, res_0)
    late = has_below & (height_of == heights // 2 - 1)
    soon = jnp.logical_not(late)
    lowest = jnp.logical_not(has_below)

    count = 3 * angles
    loads[0].wait()
    both = dot(own, spread([vol_ref[0], vol_ref[1]]))
    both = both[:count] + both[count:]
    publish(both[:angles], part_1)
    loads[4].wait()
    band_pad = jnp.zeros((angles, LANES - meas_ref.shape[2]), jnp.float32)

    def band_of(r):
        band = jnp.concatenate([meas_ref[:, r, :], band_pad], axis=1)
        return jnp.where(depth_of % 2 == 1, pltpu.roll(band, LANES // 2, 1), band)

    band_ref[...] = band_of(0)
    measure(band_of(1), part_1)

    partners = depths - 1 + has_above.astype(jnp.int32) + has_below.astype(jnp.int32)
    pl.semaphore_wait(barrier, partners)

    halos = [
        remote(vol_hbm.at[0], halo_ref, halo_sem, 0, depth_of, below),
        remote(band_ref, band_up, halo_sem, 1, depth_of, below),
    ]

    @pl.when(has_below)
    def _():
        for copy in halos:
            copy.start()

    row_1.one()

    @pl.when(lowest)
    def _():
        publish(both[2 * angles :], part_0)
        measure(band_ref[...], part_0)
        row_0.one()

    pl.when(late)(row_1.two)

    @pl.when(has_above)
    def _():
        halos[0].wait_recv()
        spilled = dot(from_halo, spread([halo_ref[...]]))
        image = both[angles : 2 * angles] + (spilled[:angles] + spilled[angles:])
        publish(image, part_2)
        halos[1].wait_recv()
        measure(band_up[...], part_2)

    @pl.when(jnp.logical_not(has_above))
    def _():
        part_2[...] = jnp.zeros_like(part_2)

    row_2.one()

    last = slices - 2
    sides = [
        remote(taps_hbm, taps_behind, side_sem, 0, ahead, height_of),
        remote(taps_hbm, taps_ahead, side_sem, 1, behind, height_of),
        remote(
            vol_ref.at[:, pl.ds(last, 2)], side_ref.at[:, pl.ds(last, 2)], side_sem, 2, ahead, height_of
        ),
        remote(vol_ref.at[:, pl.ds(0, 2)], side_ref.at[:, pl.ds(0, 2)], side_sem, 3, behind, height_of),
    ]
    for copy in sides:
        copy.start()

    pl.when(soon)(row_1.two)
    pl.when(lowest)(row_0.two)
    row_2.two()
    for copy in sides:
        copy.wait_recv()
    back = transposed([factor(lower, upper)])
    beyond = []
    for ref, depth, kept in (
        (taps_ahead, ahead, lane % slices < 2),
        (taps_behind, behind, lane % slices >= last),
    ):
        pair = weights(ref, depth)
        beyond.append(factor(*[jnp.where(kept, part, 0.0) for part in pair]))
    beyond = transposed(beyond)
    offset_ahead, offset_behind = offset_of(ahead), offset_of(behind)
    pl.when(lowest)(row_0.three)
    row_2.three()
    row_1.five()

    zero_tile = jnp.zeros((angles, LANES), jnp.float32)

    def image_of(ref):
        columns_of = [
            jnp.concatenate([ref[2 * tile], ref[2 * tile + 1]], axis=0) for tile in range(tiles)
        ]
        return jnp.concatenate(columns_of + [zero_tile], axis=1)

    def gathered(update, layer):
        whole = None
        for tap in range(taps):
            start = layer * first + tap * slices
            term = update[start : start + slices]
            if tap:
                term = roll_left(term, tap)
            whole = term if whole is None else whole + term
        return relax_step * whole[:, :columns]

    def prepared(image, moves):
        return [split_bf16(shift_rows(image, move)) for move in moves]

    def stacked(pairs):
        return jnp.concatenate([part for side in zip(*pairs) for part in side] * 2, axis=0)

    around = (offset_ahead, offset_behind)

    side_row = lax.broadcasted_iota(jnp.int32, (slices, columns), 0)
    outside = (side_row < 2) | (side_row >= last)

    def mixed(one, two):
        return stacked([one[0], two[0], one[1], two[1]])

    def pieces(src, dst, places, number, height):
        return [
            remote(src.at[place], dst.at[place], edge_sem, number + i, depth_of, height)
            for i, place in enumerate(places)
        ]

    whole_1 = image_of(res_1)
    own_1, around_1 = prepared(whole_1, (offset,)), prepared(whole_1, around)
    zero = jnp.zeros_like(whole_1).astype(jnp.bfloat16)
    nothing = [(zero, zero)] * 2
    volume_side = jnp.where(outside, side_ref[...], 0.0)
    update = dot(back[:first], stacked([own_1[0], nothing[0]]))
    layer_0 = vol_ref[0] + gathered(update, 0)
    update = dot(beyond[:first], mixed(around_1, nothing))
    side_0 = volume_side[0] + gathered(update, 0)
    down_ref[0] = layer_0
    down_ref[1] = side_0
    edges = (pl.ds(0, 2), pl.ds(last, 2))
    down_copies = pieces(
        down_ref, high_ref, (0, (1, edges[0]), (1, edges[1]), 2, (3, edges[1])), 2, below
    )
    up_copies = pieces(
        up_ref, low_ref, (0, (1, edges[0]), (1, edges[1]), 2, (3, edges[0]), (3, edges[1])), 7, above
    )
    next_copies = pieces(up2_ref, low2_ref, (0, (1, edges[0])), 13, above)

    @pl.when(has_below)
    def _():
        for copy in down_copies[:3]:
            copy.start()

    def completed():
        @pl.when(has_below)
        def _():
            for copy in up_copies[:3]:
                copy.wait_recv()

        up2_ref[0] = layer_0 + low_ref[0]
        up2_ref[1] = side_0 + jnp.where(outside, low_ref[1], 0.0)

        @pl.when(has_above)
        def _():
            for copy in next_copies:
                copy.start()

    pl.when(late)(completed)
    row_2.five()
    whole_2 = image_of(res_2)
    update = dot(back[first:], stacked(own_1 + prepared(whole_2, (offset,))))
    layer_1, part_2h2 = vol_ref[1] + gathered(update, 0), gathered(update, 1)
    up_ref[0] = part_2h2
    up_ref[2] = layer_1
    down_ref[2] = layer_1
    pl.when(has_above)(up_copies[0].start)
    pl.when(has_below)(down_copies[3].start)
    update = dot(beyond[first:], mixed(around_1, prepared(whole_2, around)))
    side_1, side_2h2 = volume_side[1] + gathered(update, 0), gathered(update, 1)
    up_ref[1] = side_2h2
    up_ref[3] = side_1
    down_ref[3] = side_1

    @pl.when(has_above)
    def _():
        for copy in up_copies[1:]:
            copy.start()

    pl.when(has_below)(down_copies[4].start)

    @pl.when(lowest)
    def _():
        row_0.five()
        image = prepared(image_of(res_0), (offset, *around))
        update = dot(back, stacked([nothing[0], image[0]]))
        low_ref[0] = gathered(update, 2)
        update = dot(beyond, mixed(nothing, image[1:]))
        low_ref[1] = gathered(update, 2)
        low_ref[2] = jnp.zeros((slices, columns), jnp.float32)
        low_ref[3] = jnp.zeros((slices, columns), jnp.float32)
        low2_ref[...] = jnp.zeros_like(low2_ref)

    @pl.when(jnp.logical_not(has_above))
    def _():
        high_ref[...] = jnp.zeros_like(high_ref)

    def arrive(condition, copies):
        @pl.when(condition)
        def _():
            for copy in copies:
                copy.wait_recv()

    def layer_of(inner, outer, kept=outside):
        return jnp.concatenate([inner, jnp.where(kept, outer, 0.0)], axis=0)

    place = lax.broadcasted_iota(jnp.int32, (2 * slices, columns), 0)
    place = depth_of * slices + jnp.where(place < slices + 4, place, place - 2 * slices)

    def normal(here, over, layer):
        layer = 2 * height_of + layer
        return directions(here, over, layer, 2 * heights, place, slices * depths)

    arrive(has_above, down_copies[:3])
    at_1 = layer_of(layer_1, side_1)
    at_2 = layer_of(high_ref[0] + part_2h2, high_ref[1] + side_2h2)
    n_1 = normal(at_1, at_2, 1)
    pl.when(soon)(completed)
    at_0 = layer_of(up2_ref[0], up2_ref[1])
    n_0 = normal(at_0, at_1, 0)
    next_1 = denoised(at_1, n_1, n_0[0])
    arrive(has_below, up_copies[3:])
    below_1 = layer_of(low_ref[2], low_ref[3])
    m_1 = normal(below_1, at_0, -1)
    next_0 = denoised(at_0, n_0, m_1[0])
    then_0 = normal(next_0, next_1, 0)
    row_1.settle()
    row_2.settle()
    pl.when(lowest)(row_0.settle)
    for copy in sides:
        copy.wait_send()

    @pl.when(has_below)
    def _():
        for copy in (*halos, *down_copies[:3]):
            copy.wait_send()

    arrive(has_below, next_copies)
    below_2 = layer_of(low2_ref[0], low2_ref[1], side_row < 2)
    under_1 = denoised(below_1, m_1, normal(below_2, below_1, -2)[0])
    stores = [pltpu.make_async_copy(result.at[i], out_ref.at[i], load_sem.at[i]) for i in range(2)]
    result[0] = denoised(next_0, then_0, normal(under_1, next_0, -1)[0])[:slices]
    stores[0].start()
    arrive(has_above, down_copies[3:])
    at_3 = layer_of(high_ref[2], high_ref[3], side_row >= last)
    next_2 = denoised(at_2, normal(at_2, at_3, 2), n_1[0])
    result[1] = denoised(next_1, normal(next_1, next_2, 1), then_0[0])[:slices]
    stores[1].start()

    for store in stores:
        store.wait()

    @pl.when(has_below)
    def _():
        down_copies[3].wait_send()
        down_copies[4].wait_send()

    @pl.when(has_above)
    def _():
        for copy in (*up_copies, *next_copies):
            copy.wait_send()


def per_device(volume, measured, taps, band_offset, angle_index):
    heights = lax.axis_size("height")
    depths = lax.axis_size("depth")
    f32 = jnp.float32
    layers, slices, columns = volume.shape
    far = depths // NEAR
    taps = jnp.swapaxes(taps, 1, 2)
    tile = (SUBLANES, LANES)
    main = (slices, columns)
    vmem = pltpu.VMEM
    far_first = [
        vmem((depths, *tile), f32), vmem((far, NEAR, *tile), f32), vmem((NEAR, *tile), f32),
        vmem((NEAR, NEAR, *tile), f32), vmem((depths, *tile), f32),
    ]
    scratch = [
        vmem(volume.shape, f32), vmem(measured.shape, f32), vmem(taps.shape, f32),
        vmem(band_offset.shape, jnp.int32), pltpu.SMEM(angle_index.shape, jnp.int32),
        vmem(main, f32), *[vmem((measured.shape[0], LANES), f32)] * 2, vmem(volume.shape, f32),
        vmem(taps.shape, f32), vmem(taps.shape, f32),
        *[vmem((depths, *tile), f32)] * 3, *far_first, *far_first,
        *[vmem((4, *main), f32)] * 4,
        vmem((2, *main), f32), vmem((2, *main), f32), vmem(volume.shape, f32),
        pltpu.SemaphoreType.DMA((5,)),
        pltpu.SemaphoreType.DMA((4,)),
        pltpu.SemaphoreType.DMA((8,)),
        pltpu.SemaphoreType.DMA((20,)),
        pltpu.SemaphoreType.DMA((30,)),
    ]
    return pl.pallas_call(
        functools.partial(kernel, heights, depths),
        out_shape=jax.ShapeDtypeStruct(volume.shape, f32),
        in_specs=[pl.BlockSpec(memory_space=pl.ANY)] * 5,
        out_specs=pl.BlockSpec(memory_space=pl.ANY),
        scratch_shapes=scratch,
        compiler_params=pltpu.CompilerParams(
            collective_id=0, has_side_effects=True, vmem_limit_bytes=60 * 1024 * 1024
        ),
    )(volume, measured, taps, band_offset, angle_index)


def solution(mesh):
    in_specs = (
        P("height", "depth", None),
        P(None, "height", "depth"),
        P(None, None, "depth"),
        P(),
        P(),
    )
    out_specs = P("height", "depth", None)
    return jax.shard_map(
        per_device, mesh=mesh, in_specs=in_specs, out_specs=out_specs, check_vma=False
    )
```
